128 devices in a mesh: dp: 32 (over z_hi, x, y), fsdp: 4 (over z_lo, core).
Axes of the slice: x: 4, y: 4, z: 4 (z_hi: 2, z_lo: 2; z = z_hi * 2 + z_lo), core: 2. Of those that a mesh axis runs over, the one named last changes fastest.
Arguments:
- tokens: bfloat16 [32768, 1024], P(('dp', 'fsdp')), may hold values from -6 to 6
- attn_norm_gain: bfloat16 [1024], P('fsdp'), may hold values from 0.5 to 1.5
- attn_norm_shift: bfloat16 [1024], P('fsdp'), may hold values from -4 to 4
- qkv_weight: bfloat16 [1024, 3072], P('fsdp'), may hold values from -0.1875 to 0.1875
- qkv_bias: bfloat16 [3072], P('fsdp'), may hold values from -6 to 6
- out_weight: bfloat16 [1024, 1024], P('fsdp'), may hold values from -0.5 to 0.5
- mlp_norm_gain: bfloat16 [1024], P('fsdp'), may hold values from 0.5 to 1.5
- mlp_norm_shift: bfloat16 [1024], P('fsdp'), may hold values from -4 to 4
- gate_up_weight: bfloat16 [1024, 5632], P('fsdp'), may hold values from -0.1875 to 0.1875
- down_weight: bfloat16 [2816, 1024], P('fsdp'), may hold values from -0.109375 to 0.109375
- cotangent: bfloat16 [32768, 1024], P(('dp', 'fsdp')), may hold values from -6 to 6
Outputs:
- layer_out: bfloat16 [32768, 1024], P(('dp', 'fsdp'))
- tokens_grad: float32 [32768, 1024], P(('dp', 'fsdp'))
- grad_attn_norm_gain: float32 [1024], P('fsdp')
- grad_attn_norm_shift: float32 [1024], P('fsdp')
- grad_qkv_weight: float32 [1024, 3072], P('fsdp')
- grad_qkv_bias: float32 [3072], P('fsdp')
- grad_out_weight: float32 [1024, 1024], P('fsdp')
- grad_mlp_norm_gain: float32 [1024], P('fsdp')
- grad_mlp_norm_shift: float32 [1024], P('fsdp')
- grad_gate_up_weight: float32 [1024, 5632], P('fsdp')
- grad_down_weight: float32 [2816, 1024], P('fsdp')
The draws below stay inside these ranges and needn't reach their ends.
All inputs are finite; a program needn't handle non-finite values.
Results may differ from the reference program's by a relative error of at most 0.028.
Values may be sent and summed in bfloat16 or wider, within the bound.
No kernel may reach another device: no remote copies, remote signals or barrier semaphores. Data moves between devices by JAX's collectives and lax.ppermute only.
A program may use at most 192 MiB of HBM per device.

```python
import math
import jax
import jax.numpy as jnp
from jax import lax

D = 1024
HEADS = 16
HEAD = 64
ROTARY = 16
FF = 2816
SEQ_LEN = 1024
TOKENS = 32768
N_DP = 32


def block_levels(stream_key, extent, split, smallest, high):
    def one(position, shards_of):
        draws = jax.random.uniform(jax.random.fold_in(jax.random.fold_in(stream_key, 6), position), (shards_of,), jnp.float32, smallest / len(split), high / len(split))
        return jnp.repeat(jnp.exp(draws), extent[position] // shards_of).reshape((-1,) + (1,) * (len(extent) - position - 1))

    factor_of = one(*split[0])
    for cut in split[1:]:
        factor_of = factor_of * one(*cut)
    return factor_of


def scatter_about(own_key, shape, width, limit, split=(), kind=jnp.bfloat16):
    gain = block_levels(own_key, shape, split, -0.22, 0.18) if split else 1.0
    values = jax.random.normal(own_key, shape, jnp.float32) * width * gain
    return jnp.minimum(jnp.maximum(values, -limit), limit).astype(kind)


def setup_inputs(seed: int = 0) -> dict:
    seeds = jax.random.split(jax.random.key(seed), 12)
    return {
        "tokens": scatter_about(seeds[0], (TOKENS, D), 1.0, 6.0, ((0, 128),)),
        "attn_norm_gain": jnp.clip(1.0 + 0.1 * jax.random.normal(seeds[1], (D,), jnp.float32), 0.5, 1.5).astype(jnp.bfloat16),
        "attn_norm_shift": scatter_about(seeds[2], (D,), 0.3, 4.0, ((0, 4),)),
        "qkv_weight": scatter_about(seeds[3], (D, 3 * D), D ** -0.5, 0.1875, ((0, 4),)),
        "qkv_bias": scatter_about(seeds[4], (3 * D,), 0.5, 6.0, ((0, 4),)),
        "out_weight": scatter_about(seeds[5], (D, D), (D // 8) ** -0.5, 0.5, ((0, 4),)),
        "mlp_norm_gain": jnp.clip(1.0 + 0.1 * jax.random.normal(seeds[6], (D,), jnp.float32), 0.5, 1.5).astype(jnp.bfloat16),
        "mlp_norm_shift": scatter_about(seeds[7], (D,), 0.3, 4.0, ((0, 4),)),
        "gate_up_weight": scatter_about(seeds[8], (D, 2 * FF), D ** -0.5, 0.1875, ((0, 4),)),
        "down_weight": scatter_about(seeds[9], (FF, D), FF ** -0.5, 0.109375, ((0, 4),)),
        "cotangent": scatter_about(seeds[10], (TOKENS, D), 1.0, 6.0, ((0, 128),)),
    }


@jax.custom_vjp
def low(v):
    return lax.optimization_barrier(v.astype(jnp.bfloat16)).astype(jnp.float32)

@jax.custom_vjp
def low_back(v):
    return v

def low_keep(v):
    return (low(v), None)

def low_pass(kept, grad):
    return (grad,)

def back_keep(v):
    return (v, None)

def back_low(kept, grad):
    return (low(grad),)
low.defvjp(low_keep, low_pass)
low_back.defvjp(back_keep, back_low)
epsilon = 1e-05
masked = -1e+30
highest = lax.Precision.HIGHEST

def matmul(former, latter):
    return jnp.dot(former, latter, precision=highest, preferred_element_type=jnp.float32)

def apply_layer_normalization(operand, norm_gain, norm_shift):
    centred = operand - lax.optimization_barrier(jnp.mean(operand, axis=1, keepdims=True))
    inverse = lax.rsqrt(lax.optimization_barrier(jnp.mean(centred * centred, axis=1, keepdims=True)) + epsilon)
    normed = centred * inverse
    return normed * norm_gain + norm_shift

def rotary_tables(places):
    indices = jnp.arange(ROTARY // 2, dtype=jnp.float32)
    frequency = jnp.exp(indices * (-math.log(10000.0) / (ROTARY // 2)))
    angles = places[:, None] * frequency[None, :]
    return (jnp.cos(angles)[:, None, :], jnp.sin(angles)[:, None, :])

def rotate(operand, cosine, sine_table):
    half_dims = ROTARY // 2
    leading = operand[:, :, :half_dims]
    trailing = operand[:, :, half_dims:ROTARY]
    return jnp.concatenate([leading * cosine - trailing * sine_table, trailing * cosine + leading * sine_table, operand[:, :, ROTARY:]], axis=2)

def forward(inputs, attn_gain, attn_shift, qkv_w, qkv_b, out_w, mlp_gain, mlp_shift, gate_up_w, down_w):
    length = inputs.shape[0]
    places = jnp.arange(length)
    cosine, sine_table = rotary_tables(places.astype(jnp.float32))
    hidden = low(apply_layer_normalization(inputs, attn_gain, attn_shift))
    projected = low_back(matmul(hidden, qkv_w) + qkv_b)
    queries = low(rotate(projected[:, :D].reshape(length, HEADS, HEAD), cosine, sine_table))
    keyset = low(rotate(projected[:, D:2 * D].reshape(length, HEADS, HEAD), cosine, sine_table))
    valueset = low(projected[:, 2 * D:].reshape(length, HEADS, HEAD))
    scores = low_back(jnp.einsum('qhd,khd->hqk', queries, keyset, precision=highest) * HEAD ** (-0.5))
    allowed = places[None, :] <= places[:, None]
    scores = jnp.where(allowed[None], scores, masked)
    largest = lax.optimization_barrier(jnp.max(scores, axis=2, keepdims=True))
    exp_scores = jnp.exp(scores - largest)
    attn_probs = exp_scores / lax.optimization_barrier(jnp.sum(exp_scores, axis=2, keepdims=True))
    attn_mixed = jnp.einsum('hqk,khd->qhd', low(attn_probs), valueset, precision=highest).reshape(length, D)
    attn_mixed = low_back(low(attn_mixed))
    residual_between = inputs + low_back(matmul(attn_mixed, out_w))
    hidden_mlp = low(apply_layer_normalization(residual_between, mlp_gain, mlp_shift))
    gate_up = low_back(matmul(hidden_mlp, gate_up_w))
    gate_part = gate_up[:, :FF]
    activation = low(gate_part * jax.nn.sigmoid(gate_part) * gate_up[:, FF:])
    return residual_between + low_back(matmul(activation, down_w))

def reference(tokens, attn_norm_gain, attn_norm_shift, qkv_weight, qkv_bias, out_weight, mlp_norm_gain, mlp_norm_shift, gate_up_weight, down_weight, cotangent):
    params = tuple((weight.astype(jnp.float32) for weight in (attn_norm_gain, attn_norm_shift, qkv_weight, qkv_bias, out_weight, mlp_norm_gain, mlp_norm_shift, gate_up_weight, down_weight)))
    sequences = tokens.reshape(N_DP, SEQ_LEN, D)
    cotangents = cotangent.reshape(N_DP, SEQ_LEN, D)

    def one_sequence(totals, paired):
        inputs = paired[0].astype(jnp.float32)
        result, pullback = jax.vjp(forward, inputs, *params)
        grads = pullback(paired[1].astype(jnp.float32))
        totals = tuple((total + grad_part for total, grad_part in zip(totals, grads[1:])))
        return (totals, (result.astype(jnp.bfloat16), grads[0]))
    zeros = tuple((jnp.zeros(weight.shape, jnp.float32) for weight in params))
    totals, (outputs, input_grads) = lax.scan(one_sequence, zeros, (sequences, cotangents))
    return (outputs.reshape(TOKENS, D), input_grads.reshape(TOKENS, D), totals[0], totals[1], totals[2], totals[3], totals[4], totals[5], totals[6], totals[7], totals[8])
```

```python
import functools
import math

import jax
import jax.numpy as jnp
from jax import lax
from jax.experimental import pallas as pl
from jax.experimental.pallas import tpu as pltpu
from jax.sharding import PartitionSpec as P

D = 1024
HEADS = 16
HEAD = 64
ROTARY = 16
FF = 2816
GROUP = 4
ROWS = 256
FFS = FF // GROUP
FFP = 768
EPS = 1e-05
F32 = jnp.float32
BF16 = jnp.bfloat16
AXES = ("dp", "fsdp")
LOG2E = 1.0 / math.log(2.0)
SCALE2 = HEAD ** (-0.5) * LOG2E


def where_is(lin):
    return [(lin // 16) % 4, (lin // 4) % 4, (lin // 64) * 2 + (lin // 2) % 2, lin % 2]


def linear(x, y, z, core):
    return (((z // 2) * 4 + x) * 4 + y) * 4 + (z % 2) * 2 + core


def perm_of(move):
    return tuple((lin, linear(*move(*where_is(lin)))) for lin in range(128))


def flip(v, which):
    return v ^ 1 if which == 0 else 3 - v


SIBLING = perm_of(lambda x, y, z, c: (x, y, z, 1 - c))
ZNEAR = perm_of(lambda x, y, z, c: (x, y, z ^ 1, c))
ZFAR = perm_of(lambda x, y, z, c: (x, y, 3 - z, c))
ZFAR_SIBLING = perm_of(lambda x, y, z, c: (x, y, 3 - z, 1 - c))
ZNEAR_SIBLING = perm_of(lambda x, y, z, c: (x, y, z ^ 1, 1 - c))
ZREPLICA = perm_of(lambda x, y, z, c: (x, y, (z + 2) % 4, c))
SIBLING_T = perm_of(lambda x, y, z, c: (y, x, z, 1 - c))
ZNEAR_SIBLING_T = perm_of(lambda x, y, z, c: (y, x, z ^ 1, 1 - c))


def cube_move(bit):
    def move(x, y, z, c):
        on_x = (bit < 2) == (c == 0)
        return (flip(x, bit % 2), y, z, c) if on_x else (x, flip(y, bit % 2), z, c)

    return perm_of(move)


CUBE = tuple(cube_move(bit) for bit in range(4))


def gray(v):
    return (((v + 1) // 2) % 2, v // 2)


def piece_of(x, y, c):
    first, second = (x, y) if c == 0 else (y, x)
    a, b = gray(first)
    d, e = gray(second)
    return 8 * a + 4 * b + 2 * d + e


def plane_groups():
    groups = {}
    for lin in range(128):
        x, y, z, c = where_is(lin)
        groups.setdefault((z, c), []).append((4 * x + y, lin))
    return [[lin for _, lin in sorted(g)] for g in groups.values()]


PLANES = plane_groups()
PIECES = tuple(piece_of(n // 4, n % 4, 0) for n in range(16))
SPLITS = (
    ((0, 2, 128), (1, 2, 64), (2, 2, 32), (3, 2, 16)),
    ((1, 4, 64), (0, 2, 64), (3, 4, 16), (2, 2, 16)),
)
ME, SLOT, BIT = 0, 1, 5


def send(value, perm):
    return lax.ppermute(value, AXES, perm)


def dot(a, b):
    return lax.dot_general(a, b, (((1,), (0,)), ((), ())), preferred_element_type=F32)


def dot_nt(a, b):
    return lax.dot_general(a, b, (((1,), (1,)), ((), ())), preferred_element_type=F32)


def dot_tn(a, b):
    return lax.dot_general(a, b, (((0,), (0,)), ((), ())), preferred_element_type=F32)


def shaped(*shape, dtype=BF16):
    return jax.ShapeDtypeStruct(shape, dtype)


SMEM = pl.BlockSpec(memory_space=pltpu.SMEM)
ANY = pl.BlockSpec(memory_space=pl.ANY)
VMEM = pl.BlockSpec(memory_space=pltpu.VMEM)


def call(kernel, name, in_specs, out_shape, operands, *, us=1, limit=48, **kw):
    return pl.pallas_call(
        kernel,
        in_specs=in_specs,
        out_shape=out_shape,
        compiler_params=pltpu.CompilerParams(vmem_limit_bytes=limit << 20),
        cost_estimate=pl.CostEstimate(flops=us * 10**9, bytes_accessed=us << 20, transcendentals=0),
        name=name,
        **kw,
    )(*operands)


def row_of(slot, rows=ROWS):
    return pl.ds(pl.multiple_of(slot * rows, rows), rows)


def lanes_of(start, width=128):
    return pl.ds(pl.multiple_of(start, 128), width)


def stats_of(x):
    cen = x - jnp.mean(x, axis=1, keepdims=True)
    inv = lax.rsqrt(jnp.mean(cen * cen, axis=1, keepdims=True) + EPS)
    return cen * inv, inv


def partner_of(t, lane):
    return jnp.where(lane % HEAD < ROTARY // 2, pltpu.roll(t, 120, 1), pltpu.roll(t, 8, 1))


def pack_kernel(a_ref, b_ref, c_ref, d_ref, bias_ref, out_ref):
    out_ref[...] = jnp.zeros((16, D), BF16)
    for v, ref in enumerate((a_ref, b_ref, c_ref, d_ref)):
        out_ref[0:1, 256 * v : 256 * v + 256] = ref[...]
    out_ref[1:2, :768] = bias_ref[...]


def pack(*vectors):
    rows = [v.reshape(1, -1) for v in vectors]
    return call(pack_kernel, "pack", [VMEM] * 5, shaped(16, D), rows, limit=16, us=0)


def tables_kernel(info, cos_ref, sin_ref):
    at = lax.broadcasted_iota(jnp.int32, (ROWS, 128), 1) % HEAD
    rate = jnp.exp((at % (ROTARY // 2)).astype(F32) * (-math.log(10000.0) / (ROTARY // 2)))
    row = lax.broadcasted_iota(jnp.int32, (ROWS, 128), 0)
    for j in range(GROUP):
        place = row + (info[ME] ^ (0, 2, 1, 3)[j]) * ROWS
        angle = place.astype(F32) * rate
        sin = jnp.where(at < ROTARY // 2, -jnp.sin(angle), jnp.sin(angle))
        rows = slice(ROWS * j, ROWS * j + ROWS)
        cos_ref[rows, :] = jnp.where(at < ROTARY, jnp.cos(angle), 1.0)
        sin_ref[rows, :] = jnp.where(at < ROTARY, sin, 0.0)


def tables(info):
    return call(tables_kernel, "tables", [SMEM], [shaped(D, 128, dtype=F32)] * 2, (info,), limit=16, us=0)


def pick_qkv_kernel(info, w_ref, *outs):
    for j, out in enumerate(outs):
        d = info[ME] ^ j
        for c in range(3):
            out[:, 256 * c : 256 * c + 256] = w_ref[:, lanes_of(c * D + d * 256, 256)]


def pick_qkv(info, w):
    return call(
        pick_qkv_kernel, "pick_qkv", [SMEM, VMEM], [shaped(ROWS, 768)] * 4, (info, w), limit=32, us=0
    )


def pick_gate_up_kernel(info, w_ref, *refs):
    outs, all_ref = refs[:4], refs[4]
    all_ref[...] = jnp.zeros_like(all_ref)
    for d in range(GROUP):
        all_ref[d, :, :FFS] = w_ref[:, FFS * d : FFS * d + FFS]
        all_ref[d, :, FFP : FFP + FFS] = w_ref[:, FF + FFS * d : FF + FFS * d + FFS]
    for j, out in enumerate(outs):
        out[...] = all_ref[info[ME] ^ j]


def pick_gate_up(info, w):
    return call(
        pick_gate_up_kernel,
        "pick_gate_up",
        [SMEM, VMEM],
        [shaped(ROWS, 2 * FFP)] * 4,
        (info, w),
        limit=32,
        us=0,
        scratch_shapes=[pltpu.VMEM((GROUP, ROWS, 2 * FFP), BF16)],
    )


def project_kernel(
    info, x0, x1, x2, x3, v0, v1, v2, v3, w0, w1, w2, w3, cos_ref, sin_ref,
    hid_ref, qkv_ref, w_ref, norms_ref, bias_ref, sems,
):
    me = info[ME]
    copies = []
    for j, w in enumerate((w0, w1, w2, w3)):
        copy = pltpu.make_async_copy(w, w_ref.at[row_of(me ^ j)], sems.at[j])
        copy.start()
        copies.append(copy)
    for j, v in enumerate((v0, v1, v2, v3)):
        owner = me ^ (0, 2, 1, 3)[j]
        extra = v[0:2, :].astype(F32)
        for n in range(4):
            norms_ref[n : n + 1, lanes_of(owner * 256, 256)] = extra[0:1, 256 * n : 256 * n + 256]
        bias_ref[0:1, lanes_of(owner * 768, 768)] = extra[1:2, :768]
    gain, shift = norms_ref[0:1, :], norms_ref[1:2, :]
    bias = jnp.concatenate(
        [bias_ref[0:1, lanes_of(c * D + me * 256, 256)] for c in range(3)], axis=1
    )
    lane = lax.broadcasted_iota(jnp.int32, (ROWS, 128), 1)
    for j, x in enumerate((x0, x1, x2, x3)):
        rows = slice(ROWS * j, ROWS * j + ROWS)
        xhat, _ = stats_of(x[...].astype(F32))
        hid = (xhat * gain + shift).astype(BF16)
        hid_ref[rows, :] = hid
        if j == 0:
            for copy in copies:
                copy.wait()
        proj = dot(hid, w_ref[...]) + bias
        cos, sin = cos_ref[rows, :], sin_ref[rows, :]
        for c in range(4):
            t = proj[:, 128 * c : 128 * c + 128]
            qkv_ref[rows, 128 * c : 128 * c + 128] = (t * cos + partner_of(t, lane) * sin).astype(BF16)
        qkv_ref[rows, 512:] = proj[:, 512:].astype(BF16)


def project(info, xs, vs, ws, cos, sin):
    return call(
        project_kernel,
        "project",
        [SMEM] + [VMEM] * 8 + [ANY] * 4 + [VMEM] * 2,
        [shaped(D, D), shaped(D, 768), shaped(D, 768), shaped(8, D, dtype=F32)],
        (info, *xs, *vs, *ws, cos, sin),
        us=0,
        scratch_shapes=[pltpu.VMEM((8, 3 * D), F32), pltpu.SemaphoreType.DMA((4,))],
    )


def later_keys():
    return lax.broadcasted_iota(jnp.int32, (ROWS, ROWS), 0) > lax.broadcasted_iota(
        jnp.int32, (ROWS, ROWS), 1
    )


def attend_kernel(info, qkv_ref, w_ref, mixed_ref, lse_ref, low_ref, up_ref):
    pair = pl.program_id(0)
    side = lax.broadcasted_iota(jnp.int32, (ROWS, 128), 1) // HEAD
    lane0 = pair * 128
    later = later_keys()
    zero = jnp.zeros((), BF16)
    for i in range(GROUP):
        rows = row_of(info[SLOT + i])
        both = qkv_ref[rows, lanes_of(lane0)]
        outs = []
        for h in range(2):
            q = jnp.where(side == h, both, zero)
            tiles = []
            for n in range(i + 1):
                st = dot_nt(qkv_ref[row_of(info[SLOT + n]), lanes_of(lane0 + 256)], q)
                tiles.append(jnp.where(later, -1e30, st) if n == i else st)
            top = functools.reduce(jnp.maximum, [jnp.max(t, axis=0, keepdims=True) for t in tiles])
            top = top * SCALE2
            total = jnp.zeros((1, ROWS), F32)
            out = jnp.zeros((128, ROWS), F32)
            for n in range(i + 1):
                p = jnp.exp2(tiles[n] * SCALE2 - top)
                total = total + jnp.sum(p, axis=0, keepdims=True)
                v = qkv_ref[row_of(info[SLOT + n]), lanes_of(lane0 + 512)]
                out = out + dot_tn(v, p.astype(BF16))
            outs.append((out / total).T)
            lse_ref[0, h : h + 1, rows] = top + jnp.log2(total)
        mixed_ref[rows, lanes_of(lane0)] = jnp.where(side == 0, outs[0], outs[1]).astype(BF16)

    @pl.when(pair == 1)
    def _():
        up_ref[...] = dot(mixed_ref[512:, :], w_ref[...]).astype(BF16)
        low_ref[...] = dot(mixed_ref[:512, :], w_ref[...]).astype(BF16)


def attend(info, qkv, w):
    fixed = lambda h: (0, 0)
    return call(
        attend_kernel,
        "attend",
        [SMEM, pl.BlockSpec((D, 768), fixed), pl.BlockSpec((256, D), fixed)],
        [shaped(D, 256), shaped(2, 2, D, dtype=F32), shaped(512, D), shaped(512, D)],
        (info, qkv, w),
        us=0,
        grid=(2,),
        out_specs=[
            pl.BlockSpec((D, 256), fixed),
            pl.BlockSpec((1, 2, D), lambda h: (h, 0, 0)),
            pl.BlockSpec((512, D), fixed),
            pl.BlockSpec((512, D), fixed),
        ],
    )


def attend_back_kernel(
    pair, info, qkv_ref, b0, b1, b2, b3, w_ref, lse_ref, cos_ref, sin_ref,
    out_ref, do_ref, dq_ref, dk_ref, dv_ref,
):
    side = lax.broadcasted_iota(jnp.int32, (ROWS, 128), 1) // HEAD
    cols = [slice(256 * c + 128 * pair, 256 * c + 128 * pair + 128) for c in range(3)]
    later = later_keys()
    zero = jnp.zeros((), BF16)
    for j, b in enumerate((b0, b1, b2, b3)):
        do_ref[ROWS * j : ROWS * j + ROWS, :] = dot_nt(b[...], w_ref[...]).astype(BF16)
    dk_ref[...] = jnp.zeros_like(dk_ref)
    dv_ref[...] = jnp.zeros_like(dv_ref)
    for i in range(GROUP):
        rows = row_of(info[SLOT + i])
        q_both = qkv_ref[rows, cols[0]]
        do_both = do_ref[rows, :]
        dqt = jnp.zeros((128, ROWS), F32)
        for h in range(2):
            q = jnp.where(side == h, q_both, zero)
            do = jnp.where(side == h, do_both, zero)
            lse = lse_ref[pair, h : h + 1, rows]
            probs, grads = [], []
            delta = jnp.zeros((1, ROWS), F32)
            for n in range(i + 1):
                there = row_of(info[SLOT + n])
                p = jnp.exp2(dot_nt(qkv_ref[there, cols[1]], q) * SCALE2 - lse)
                if n == i:
                    p = jnp.where(later, 0.0, p)
                dp = dot_nt(qkv_ref[there, cols[2]], do)
                delta = delta + jnp.sum(p * dp, axis=0, keepdims=True)
                dv_ref[there, :] += dot(p.astype(BF16), do)
                probs.append(p)
                grads.append(dp)
            for n in range(i + 1):
                there = row_of(info[SLOT + n])
                k = jnp.where(side == h, qkv_ref[there, cols[1]], zero)
                ds = (probs[n] * (grads[n] - delta)).astype(BF16)
                dk_ref[there, :] += dot(ds, q)
                dqt = dqt + dot_tn(k, ds)
        dq_ref[rows, :] = dqt.T
    lane = lax.broadcasted_iota(jnp.int32, (D, 128), 1)
    scale = HEAD ** (-0.5)
    cos, sin = cos_ref[...], sin_ref[...]
    dq = dq_ref[...] * scale
    out_ref[:, :128] = (dq * cos - partner_of(dq, lane) * sin).astype(BF16)
    dk = dk_ref[...] * scale
    out_ref[:, 128:256] = (dk * cos - partner_of(dk, lane) * sin).astype(BF16)
    out_ref[:, 256:] = dv_ref[...].astype(BF16)


def attend_back(pair, info, qkv, branch, w, lse, cos, sin):
    fixed = lambda i: (0, 0)
    block = pl.BlockSpec((ROWS, D), fixed)
    return call(
        functools.partial(attend_back_kernel, pair),
        "attend_back",
        [
            SMEM,
            pl.BlockSpec((D, 768), fixed),
            block, block, block, block,
            pl.BlockSpec((128, D), lambda i: (pair, 0)),
            pl.BlockSpec((2, 2, D), lambda i: (0, 0, 0)),
            pl.BlockSpec((D, 128), fixed),
            pl.BlockSpec((D, 128), fixed),
        ],
        shaped(D, 384),
        (info, qkv, *branch, w, lse, cos, sin),
        us=7,
        grid=(1,),
        out_specs=pl.BlockSpec((D, 384), fixed),
        scratch_shapes=[pltpu.VMEM((D, 128), BF16)] + [pltpu.VMEM((D, 128), F32)] * 3,
    )


def whole(first, second):
    return jnp.concatenate(
        [v[:, 128 * c : 128 * c + 128] for c in range(3) for v in (first, second)], axis=1
    )


def hidden_back_kernel(d0, d1, w_ref, x0, x1, x2, x3, low_ref, up_ref, sums_ref):
    gains = jnp.zeros((1, D), F32)
    shifts = jnp.zeros((1, D), F32)
    for j in (2, 3, 0, 1):
        x = (x0, x1, x2, x3)[j]
        rows = slice(ROWS * j, ROWS * j + ROWS)
        e = dot_nt(whole(d0[rows, :], d1[rows, :]), w_ref[...])
        xhat, _ = stats_of(x[...].astype(F32))
        gains = gains + jnp.sum(e * xhat, axis=0, keepdims=True)
        shifts = shifts + jnp.sum(e, axis=0, keepdims=True)
        out = low_ref if j < 2 else up_ref
        out[ROWS * (j % 2) : ROWS * (j % 2) + ROWS, :] = e.astype(BF16)
    sums_ref[0:1, :] = gains
    sums_ref[1:2, :] = shifts


def hidden_back(dqkvs, w, xs):
    return call(
        hidden_back_kernel,
        "hidden_back",
        [VMEM] * 7,
        [shaped(512, D), shaped(512, D), shaped(2, D, dtype=F32)],
        (*dqkvs, w, *xs),
        us=5,
    )


def add_halves_kernel(low_ref, got_ref, own_ref, near_ref):
    total = low_ref[...].astype(F32) + got_ref[...].astype(F32)
    own_ref[...] = total[:ROWS, :]
    near_ref[...] = total[ROWS:, :].astype(BF16)


def scatter_group(low, up):
    own, near = call(
        add_halves_kernel,
        "add_halves",
        [VMEM] * 2,
        [shaped(ROWS, D, dtype=F32), shaped(ROWS, D)],
        (low, send(up, SIBLING)),
        limit=16,
    )
    return own, near


def gather_group(own, keep=None):
    near = send(own, ZNEAR)
    return (own, near, send(own, SIBLING), send(near, SIBLING))


def middle_kernel(x_ref, part_ref, other_ref, norms_ref, mid_ref, hid_ref):
    mid = x_ref[...].astype(F32) + part_ref[...] + other_ref[...].astype(F32)
    mid_ref[...] = mid
    xhat, _ = stats_of(mid)
    hid_ref[...] = (xhat * norms_ref[2:3, :] + norms_ref[3:4, :]).astype(BF16)


def middle_of(x, part, other, norms):
    return call(
        middle_kernel,
        "middle",
        [VMEM] * 4,
        [shaped(ROWS, D, dtype=F32), shaped(ROWS, D)],
        (x, part, other, norms),
        limit=16,
    )


def norm_back_kernel(which, part_ref, other_ref, base_ref, res_ref, norms_ref, out_ref, *rest):
    e = part_ref[...] + other_ref[...].astype(F32)
    xhat, inv = stats_of(base_ref[...].astype(F32))
    u = e * norms_ref[which : which + 1, :]
    back = u - jnp.mean(u, axis=1, keepdims=True) - xhat * jnp.mean(u * xhat, axis=1, keepdims=True)
    out = res_ref[...].astype(F32) + inv * back
    out_ref[...] = out
    if rest:
        low_ref, sums_ref = rest
        low_ref[...] = out.astype(BF16)
        sums_ref[0:1, :] = jnp.sum(e * xhat, axis=0, keepdims=True)
        sums_ref[1:2, :] = jnp.sum(e, axis=0, keepdims=True)


def norm_back(part, other, base, res, norms, which):
    outs = [shaped(ROWS, D, dtype=F32)]
    if which == 2:
        outs += [shaped(ROWS, D), shaped(2, D, dtype=F32)]
    return call(
        functools.partial(norm_back_kernel, which),
        "norm_back",
        [VMEM] * 5,
        outs,
        (part, other, base, res, norms),
        limit=16,
    )


def layer_out_kernel(mid_ref, part_ref, other_ref, out_ref):
    out_ref[...] = (mid_ref[...] + part_ref[...] + other_ref[...].astype(F32)).astype(BF16)


def layer_out_of(mid, part, other):
    return call(
        layer_out_kernel, "layer_out", [VMEM] * 3, shaped(ROWS, D), (mid, part, other), limit=16
    )


def feed_kernel(
    info, h0, h1, h2, h3, g0, g1, g2, g3, w0, w1, w2, w3, d_ref,
    act_ref, dgu_ref, gh_low, gh_up, out_low, out_up, h_ref, g_ref, w_ref, down_ref, sems,
):
    step = pl.program_id(0)

    def tokens_in(j):
        rows = slice(ROWS * j, ROWS * j + ROWS)
        return (
            pltpu.make_async_copy((h0, h1, h2, h3)[j], h_ref.at[rows], sems.at[j]),
            pltpu.make_async_copy((g0, g1, g2, g3)[j], g_ref.at[rows], sems.at[4 + j]),
        )

    def weights_in():
        for j, w in enumerate((w0, w1, w2, w3)):
            yield pltpu.make_async_copy(w, w_ref.at[row_of(info[ME] ^ j)], sems.at[8 + j])
        yield pltpu.make_async_copy(d_ref, down_ref.at[:FFS], sems.at[12])

    @pl.when(step == 0)
    def _():
        first = [*tokens_in(0), *tokens_in(1)]
        weights = list(weights_in())
        for copy in (*first, *weights, *tokens_in(2), *tokens_in(3)):
            copy.start()
        down_ref[FFS:, :] = jnp.zeros((FFP - FFS, D), BF16)
        for copy in (*first, *weights):
            copy.wait()

    @pl.when(step == 1)
    def _():
        for copy in (*tokens_in(2), *tokens_in(3)):
            copy.wait()

    rows = pl.ds(pl.multiple_of(step * 512, 512), 512)
    h, g = h_ref[rows, :], g_ref[rows, :]
    gate = dot(h, w_ref[:, :FFP])
    up = dot(h, w_ref[:, FFP:])
    sig = jax.nn.sigmoid(gate)
    silu = gate * sig
    act = (silu * up).astype(BF16)
    act_ref[...] = act
    grad_act = dot_nt(g, down_ref[...])
    dgate = (grad_act * up * (sig * (1.0 + gate * (1.0 - sig)))).astype(BF16)
    dup = (grad_act * silu).astype(BF16)
    dgu_ref[:, :FFP] = dgate
    dgu_ref[:, FFP:] = dup
    gh = (dot_nt(dgate, w_ref[:, :FFP]) + dot_nt(dup, w_ref[:, FFP:])).astype(BF16)
    out = dot(act, down_ref[...]).astype(BF16)

    @pl.when(step == 0)
    def _():
        gh_low[...] = gh
        out_low[...] = out

    @pl.when(step == 1)
    def _():
        gh_up[...] = gh
        out_up[...] = out


def feed(info, hs, gs, ws, down):
    row = lambda i: (i, 0)
    fixed = lambda i: (0, 0)
    half = pl.BlockSpec((512, D), fixed)
    return call(
        feed_kernel,
        "feed",
        [SMEM] + [ANY] * 13,
        [shaped(D, FFP), shaped(D, 2 * FFP)] + [shaped(512, D)] * 4,
        (info, *hs, *gs, *ws, down),
        us=18,
        limit=56,
        grid=(2,),
        out_specs=[pl.BlockSpec((512, FFP), row), pl.BlockSpec((512, 2 * FFP), row)] + [half] * 4,
        scratch_shapes=[
            pltpu.VMEM((D, D), BF16),
            pltpu.VMEM((D, D), BF16),
            pltpu.VMEM((D, 2 * FFP), BF16),
            pltpu.VMEM((FFP, D), BF16),
            pltpu.SemaphoreType.DMA((13,)),
        ],
    )


def halve(info, step, rows_of, outs):
    for part in range(2):
        bit, outer, run = SPLITS[part][step]
        mine = info[BIT + bit]
        keep, away = outs[2 * part], outs[2 * part + 1]
        for o in range(outer):
            at = slice(o * run, o * run + run)
            keep[at, :] = rows_of(part, pl.ds(pl.multiple_of((2 * o + mine) * run, run), run))
            away[at, :] = rows_of(part, pl.ds(pl.multiple_of((2 * o + 1 - mine) * run, run), run))


def split_result(info, res_ref, outs):
    halve(info, 0, lambda part, at: res_ref[part, at, :], outs)


def mlp_weights_kernel(
    info, h0, h1, h2, h3, g0, g1, g2, g3, dgu_ref, act_ref, k1, s1, k2, s2, h_ref, g_ref, res_ref, sems
):
    step = pl.program_id(0)

    def copies(refs, into, first):
        return [
            pltpu.make_async_copy(r, into.at[ROWS * j : ROWS * j + ROWS], sems.at[first + j])
            for j, r in enumerate(refs)
        ]

    @pl.when(step == 0)
    def _():
        hs = copies((h0, h1, h2, h3), h_ref, 0)
        for copy in hs + copies((g0, g1, g2, g3), g_ref, 4):
            copy.start()
        for copy in hs:
            copy.wait()

    @pl.when(step == 2)
    def _():
        for copy in copies((g0, g1, g2, g3), g_ref, 4):
            copy.wait()

    for half in range(2):
        cols = slice(512 * half, 512 * half + 512)

        @pl.when(step < 2)
        def _():
            res_ref[half] = dot_tn(h_ref[:, cols], dgu_ref[...]).astype(BF16)

        @pl.when(step == 2)
        def _():
            res_ref[half] = dot_tn(g_ref[:, cols], act_ref[...]).astype(BF16)

    split_result(info, res_ref, (k1, s1, k2, s2))


def mlp_weights(info, hs, gs, dgu, act):
    col = lambda i: (0, i)
    return call(
        mlp_weights_kernel,
        "mlp_weights",
        [SMEM]
        + [ANY] * 8
        + [pl.BlockSpec((D, FFP), lambda i: (0, jnp.minimum(i, 1))), pl.BlockSpec((D, FFP), lambda i: (0, 0))],
        [shaped(256, 3 * FFP)] * 4,
        (info, *hs, *gs, dgu, act),
        us=10,
        grid=(3,),
        out_specs=[pl.BlockSpec((256, FFP), col)] * 4,
        scratch_shapes=[
            pltpu.VMEM((D, D), BF16),
            pltpu.VMEM((D, D), BF16),
            pltpu.VMEM((2, 512, FFP), BF16),
            pltpu.SemaphoreType.DMA((8,)),
        ],
    )


EX = 128
ATT = 768 + EX + 256


def attn_weights_kernel(
    info, h_ref, d0, d1, m_ref, b0, b1, b2, b3, sa_ref, sm_ref,
    k1, s1, k2, s2, b_ref, d_ref, ex_ref, res_ref, sems,
):
    me = info[ME]
    copies = [
        pltpu.make_async_copy(r, b_ref.at[ROWS * j : ROWS * j + ROWS], sems.at[j])
        for j, r in enumerate((b0, b1, b2, b3))
    ]
    for copy in copies:
        copy.start()
    d_ref[...] = whole(d0[...], d1[...])
    ex_ref[...] = jnp.zeros_like(ex_ref)
    ex_ref[0:2, :] = sa_ref[...]
    ex_ref[2:4, :] = sm_ref[...]
    db = dot(jnp.ones((8, D), BF16), d_ref[...])[0:1, :]
    for c in range(3):
        one = db[:, 256 * c : 256 * c + 256]
        ex_ref[pl.ds(8 + 4 * c + me, 1), :] = jnp.concatenate([one] * GROUP, axis=1)
    ex = ex_ref[...].T.astype(BF16)
    for half in range(2):
        rows = slice(512 * half, 512 * half + 512)
        res_ref[half, :, :768] = dot_tn(h_ref[:, rows], d_ref[...]).astype(BF16)
        res_ref[half, :, 768 : 768 + EX] = ex[rows, :]
    for copy in copies:
        copy.wait()
    for half in range(2):
        res_ref[half, :, 768 + EX :] = dot_tn(b_ref[:, 512 * half : 512 * half + 512], m_ref[...]).astype(BF16)
    split_result(info, res_ref, (k1, s1, k2, s2))


def attn_weights(info, hidden, dqkvs, mixed, branch, sums_a, sums_m):
    return call(
        attn_weights_kernel,
        "attn_weights",
        [SMEM] + [VMEM] * 4 + [ANY] * 4 + [VMEM] * 2,
        [shaped(256, ATT)] * 4,
        (info, hidden, *dqkvs, mixed, *branch, sums_a, sums_m),
        us=5,
        scratch_shapes=[
            pltpu.VMEM((D, D), BF16),
            pltpu.VMEM((D, 768), BF16),
            pltpu.VMEM((EX, D), F32),
            pltpu.VMEM((2, 512, ATT), BF16),
            pltpu.SemaphoreType.DMA((4,)),
        ],
    )


def add(a, b):
    return (a.astype(F32) + b.astype(F32)).astype(BF16)


def halve_kernel(step, info, a1, g1, a2, g2, *outs):
    ins = ((a1, g1), (a2, g2))
    halve(info, step, lambda part, at: add(ins[part][0][at, :], ins[part][1][at, :]), outs)


def piece_kernel(a1, g1, a2, g2, out):
    out[:32, :] = add(a1[...], g1[...])
    out[32:, :] = add(a2[...], g2[...])


def share_kernel(cols, info, a_ref, g_ref, o0, o1, o2, o3, kept):
    width = a_ref.shape[1] - cols
    for j, out in enumerate((o0, o1, o2, o3)):
        rows = row_of(info[ME] ^ j, 16)
        out[...] = add(a_ref[rows, :cols], g_ref[rows, :cols])
    for t in range(GROUP):
        rows = slice(16 * t, 16 * t + 16)
        kept[:, width * t : width * t + width] = add(a_ref[rows, cols:], g_ref[rows, cols:])


def scatter_plane(info, first, name, gates):
    k1, s1, k2, s2 = first
    width = k1.shape[1]
    s1 = after(s1, *gates[0])
    s2 = after(s2, *gates[0])
    for step in range(4):
        got1 = send(s1, CUBE[SPLITS[0][step][0]])
        got2 = send(s2, CUBE[SPLITS[1][step][0]])
        operands = (after(k1, *gates[step + 1]), got1, k2, got2)
        if step == 3:
            return call(piece_kernel, "piece_" + name, [VMEM] * 4, shaped(64, width), operands, limit=24)
        rows = k1.shape[0] // 2
        k1, s1, k2, s2 = call(
            functools.partial(halve_kernel, step + 1),
            "halve_" + name,
            [SMEM] + [VMEM] * 4,
            [shaped(rows, width)] * 4,
            (info, *operands),
            limit=24,
        )


def share(info, piece, cols, name, gate=()):
    width = piece.shape[1]
    *blocks, kept = call(
        functools.partial(share_kernel, cols),
        "share_" + name,
        [SMEM] + [VMEM] * 2,
        [shaped(16, cols)] * 4 + [shaped(16, GROUP * (width - cols))],
        (info, after(piece, *gate), send(piece, ZREPLICA)),
        limit=16,
    )
    perms = (None, SIBLING_T, ZNEAR, ZNEAR_SIBLING_T)
    return [b if p is None else send(b, p) for b, p in zip(blocks, perms)], kept


def join_mlp_kernel(info, r0, r1, r2, r3, kept, out):
    for j, r in enumerate((r0, r1, r2, r3)):
        s = info[ME] ^ j
        out[:, lanes_of(s * FFP, FFP)] = r[:, :FFP]
        out[:, lanes_of((GROUP + s) * FFP, FFP)] = r[:, FFP:]
    out[:, 2 * GROUP * FFP :] = kept[...]


def join_attn_kernel(info, r0, r1, r2, r3, kept, one, two):
    refs = (r0, r1, r2, r3)
    for j, r in enumerate(refs):
        s = info[ME] ^ j
        one[:, lanes_of(s * 256, 256)] = r[:, :256]
        one[:, lanes_of(D + s * 256, 256)] = r[:, 256:512]
        two[:, lanes_of(s * 256, 256)] = r[:, 512:768]
    two[:, D : D + EX] = sum(r[:, 768:].astype(F32) for r in refs).astype(BF16)
    two[:, D + EX :] = kept[...]


def finish_mlp_kernel(info, all_ref, gu_ref, down_ref, turn_ref):
    for n, piece in enumerate(PIECES):
        turned = 4 * (n % 4) + n // 4
        at = row_of(jnp.where(info[ME] % 2 == 0, n, turned), 16)
        to = slice(16 * piece, 16 * piece + 16)
        for s in range(GROUP):
            for c in range(2):
                lo = (GROUP * c + s) * FFP
                gu_ref[to, FF * c + FFS * s : FF * c + FFS * s + FFS] = all_ref[at, lo : lo + FFS].astype(F32)
        turn_ref[to, :] = all_ref[at, 2 * GROUP * FFP :].astype(F32)
    for t in range(GROUP):
        down_ref[:, 256 * t : 256 * t + 256] = turn_ref[:, FFP * t : FFP * t + FFP].T[:FFS, :]


def finish_attn_kernel(info, a1, g1, a2, g2, qkv_ref, out_ref, vec_ref, turn_ref, ex_ref):
    q = info[BIT] * 8 + info[BIT + 1] * 4 + info[BIT + 2] * 2 + info[BIT + 3]
    for piece in range(16):
        d = q ^ piece
        e = ((d >> 2) & 1) * 8 + ((d >> 3) & 1) * 4 + (d & 1) * 2 + ((d >> 1) & 1)
        to = slice(16 * piece, 16 * piece + 16)
        for own, got, slot, one in ((a1, g1, d, True), (a2, g2, e, False)):
            at = row_of(slot & 7, 16)
            v = jnp.where(slot >= 8, got[at, :].astype(F32), own[at, :].astype(F32))
            if one:
                qkv_ref[to, : 2 * D] = v
            else:
                qkv_ref[to, 2 * D :] = v[:, :D]
                ex_ref[to, :] = v[:, D : D + EX]
                turn_ref[to, :] = v[:, D + EX :]
    for t in range(GROUP):
        out_ref[:, 256 * t : 256 * t + 256] = turn_ref[:, 256 * t : 256 * t + 256].T
    vec_ref[...] = ex_ref[...].T


def gather_plane(parts):
    for step in (3, 2, 1, 0):
        got = [send(p, CUBE[SPLITS[i][step][0]]) for i, p in enumerate(parts)]
        if step == 0:
            return parts[0], got[0], parts[1], got[1]
        parts = [jnp.concatenate([p, g], axis=0) for p, g in zip(parts, got)]


def after(value, *earlier):
    return lax.optimization_barrier((value, *earlier))[0]


def body(
    tokens,
    attn_norm_gain,
    attn_norm_shift,
    qkv_weight,
    qkv_bias,
    out_weight,
    mlp_norm_gain,
    mlp_norm_shift,
    gate_up_weight,
    down_weight,
    cotangent,
):
    me = lax.axis_index("fsdp")
    rank = lax.axis_index("dp")
    x, y = (rank // 4) % 4, rank % 4
    first = jnp.where(me % 2 == 0, x, y)
    second = jnp.where(me % 2 == 0, y, x)
    info = jnp.stack(
        [me]
        + [2 * ((n ^ me) % 2) + (n ^ me) // 2 for n in range(GROUP)]
        + [((first + 1) // 2) % 2, first // 2, ((second + 1) // 2) % 2, second // 2]
    ).astype(jnp.int32)
    near = send(tokens, ZNEAR)
    sibling = send(tokens, SIBLING)
    qkv_parts = pick_qkv(info, qkv_weight)
    far = (None, SIBLING, ZFAR, ZFAR_SIBLING)
    qkv_ws = [b if p is None else send(b, p) for b, p in zip(qkv_parts, far)]
    vs = gather_group(
        pack(attn_norm_gain, attn_norm_shift, mlp_norm_gain, mlp_norm_shift, after(qkv_bias, qkv_parts[0]))
    )
    cos, sin = tables(info)
    gate_up_parts = pick_gate_up(info, after(gate_up_weight, vs[0]))
    near = after(near, cos, gate_up_parts[0])
    xs = (tokens, near, sibling, send(near, SIBLING))
    gate_up_ws = [
        gate_up_parts[0],
        send(after(gate_up_parts[1], near), SIBLING),
        send(after(gate_up_parts[2], *qkv_ws[2:]), ZFAR),
        send(after(gate_up_parts[3], near), ZNEAR_SIBLING),
    ]

    hidden, qkv, qkv_w, norms = project(info, xs, vs, qkv_ws, cos, sin)
    mixed, lse, low, up = attend(info, qkv, out_weight)
    gs = gather_group(after(cotangent, gate_up_ws[3]))
    own, near = scatter_group(low, up)
    near = after(near, gate_up_ws[2], gs[1])
    mid, hid_own = middle_of(tokens, own, send(near, ZNEAR), norms)
    hs = gather_group(hid_own)
    act, dgu, gh_low, gh_up, out_low, out_up = feed(info, hs, gs, gate_up_ws, down_weight)

    gh_own, gh_near = scatter_group(gh_low, gh_up)
    mlp_halves = mlp_weights(info, hs, gs, after(dgu, gh_near), act)
    grad_mid, branch_own, sums_m = norm_back(gh_own, send(gh_near, ZNEAR), mid, cotangent, norms, 2)
    branch = gather_group(branch_own)

    dqkv0 = attend_back(0, info, qkv, branch, out_weight, lse, cos, sin)
    dqkv1 = attend_back(1, after(info, dqkv0), qkv, branch, out_weight, lse, cos, sin)
    dqkvs = (dqkv0, dqkv1)
    ga_low, ga_up, sums_a = hidden_back(dqkvs, qkv_w, xs)
    attn_halves = attn_weights(info, hidden, dqkvs, mixed, branch, after(sums_a, ga_low), sums_m)

    mlp_gates = ((branch_own,), (branch[1],), (dqkv0,), (dqkv1,), (ga_low,))
    mlp_piece = scatter_plane(info, mlp_halves, "mlp", mlp_gates)
    mlp_blocks, mlp_kept = share(info, mlp_piece, 2 * FFP, "mlp", (attn_halves[0],))
    mlp_piece = call(
        join_mlp_kernel,
        "join_mlp",
        [SMEM] + [VMEM] * 5,
        shaped(16, 3 * GROUP * FFP),
        (info, *mlp_blocks, mlp_kept),
        limit=16,
    )
    mlp_all = lax.all_gather(mlp_piece, AXES, axis=0, axis_index_groups=PLANES, tiled=True)

    o_own, o_near = scatter_group(out_low, after(out_up, gh_near))
    ga_own, ga_near = scatter_group(ga_low, ga_up)
    ga_other = send(after(ga_near, attn_halves[0]), ZNEAR)
    o_other = send(after(o_near, attn_halves[0]), ZNEAR)
    attn_gates = ((), (mlp_piece,), (), (ga_other,), (o_other,))
    attn_piece = scatter_plane(info, attn_halves, "attn", attn_gates)
    attn_blocks, attn_kept = share(info, attn_piece, 768 + EX, "attn")
    pieces = call(
        join_attn_kernel,
        "join_attn",
        [SMEM] + [VMEM] * 5,
        [shaped(16, 2 * D), shaped(16, 2 * D + EX)],
        (info, *attn_blocks, attn_kept),
        limit=16,
    )
    (tokens_grad,) = norm_back(ga_own, ga_other, tokens, grad_mid, norms, 0)
    layer_out = layer_out_of(mid, o_own, o_other)

    grad_gate_up, grad_down = call(
        finish_mlp_kernel,
        "finish_mlp",
        [SMEM, VMEM],
        [shaped(ROWS, 2 * FF, dtype=F32), shaped(FFS, D, dtype=F32)],
        (info, mlp_all),
        us=5,
        scratch_shapes=[pltpu.VMEM((ROWS, GROUP * FFP), F32)],
    )
    grad_qkv, grad_out, vec = call(
        finish_attn_kernel,
        "finish_attn",
        [SMEM] + [VMEM] * 4,
        [shaped(ROWS, 3 * D, dtype=F32), shaped(256, D, dtype=F32), shaped(EX, ROWS, dtype=F32)],
        (after(info, grad_down), *gather_plane(pieces)),
        us=4,
        scratch_shapes=[pltpu.VMEM((ROWS, D), F32), pltpu.VMEM((ROWS, EX), F32)],
    )
    grad_bias = lax.dynamic_slice_in_dim(vec[8:20].reshape(3 * D), 768 * me, 768, 0)
    return (
        layer_out,
        tokens_grad,
        vec[0],
        vec[1],
        grad_qkv,
        grad_bias,
        grad_out,
        vec[2],
        vec[3],
        grad_gate_up,
        grad_down,
    )


def solution(mesh):
    rows = P(("dp", "fsdp"), None)
    vector = P("fsdp")
    matrix = P("fsdp", None)
    in_specs = (rows, vector, vector, matrix, vector, matrix, vector, vector, matrix, matrix, rows)
    out_specs = (rows, rows, vector, vector, matrix, vector, matrix, vector, vector, matrix, matrix)
    return jax.shard_map(body, mesh=mesh, in_specs=in_specs, out_specs=out_specs, check_vma=False)
```

```python
import functools
import math

import jax
import jax.numpy as jnp
from jax import lax
from jax.experimental import pallas as pl
from jax.experimental.pallas import tpu as pltpu
from jax.sharding import PartitionSpec as P

D = 1024
HEADS = 16
HEAD = 64
ROTARY = 16
FF = 2816
GROUP = 4
ROWS = 256
FFS = FF // GROUP
FFP = 768
EPS = 1e-05
F32 = jnp.float32
BF16 = jnp.bfloat16
AXES = ("dp", "fsdp")
LOG2E = 1.0 / math.log(2.0)
SCALE2 = HEAD ** (-0.5) * LOG2E


def where_is(lin):
    return [(lin // 16) % 4, (lin // 4) % 4, (lin // 64) * 2 + (lin // 2) % 2, lin % 2]


def linear(x, y, z, core):
    return (((z // 2) * 4 + x) * 4 + y) * 4 + (z % 2) * 2 + core


def perm_of(move):
    return tuple((lin, linear(*move(*where_is(lin)))) for lin in range(128))


def flip(v, which):
    return v ^ 1 if which == 0 else 3 - v


SIBLING = perm_of(lambda x, y, z, c: (x, y, z, 1 - c))
ZNEAR = perm_of(lambda x, y, z, c: (x, y, z ^ 1, c))
ZFAR = perm_of(lambda x, y, z, c: (x, y, 3 - z, c))
ZFAR_SIBLING = perm_of(lambda x, y, z, c: (x, y, 3 - z, 1 - c))
ZNEAR_SIBLING = perm_of(lambda x, y, z, c: (x, y, z ^ 1, 1 - c))
ZREPLICA = perm_of(lambda x, y, z, c: (x, y, (z + 2) % 4, c))
def cube_move(bit):
    def move(x, y, z, c):
        on_x = (bit < 2) == (c == 0)
        return (flip(x, bit % 2), y, z, c) if on_x else (x, flip(y, bit % 2), z, c)

    return perm_of(move)


CUBE = tuple(cube_move(bit) for bit in range(4))


SPLITS = (
    ((0, 2, 128), (1, 2, 64), (2, 2, 32), (3, 2, 16)),
    ((1, 4, 64), (0, 2, 64), (3, 4, 16), (2, 2, 16)),
)
ME, SLOT, BIT = 0, 1, 5


def send(value, perm):
    return lax.ppermute(value, AXES, perm)


def dot(a, b):
    return lax.dot_general(a, b, (((1,), (0,)), ((), ())), preferred_element_type=F32)


def dot_nt(a, b):
    return lax.dot_general(a, b, (((1,), (1,)), ((), ())), preferred_element_type=F32)


def dot_tn(a, b):
    return lax.dot_general(a, b, (((0,), (0,)), ((), ())), preferred_element_type=F32)


def shaped(*shape, dtype=BF16):
    return jax.ShapeDtypeStruct(shape, dtype)


SMEM = pl.BlockSpec(memory_space=pltpu.SMEM)
ANY = pl.BlockSpec(memory_space=pl.ANY)
VMEM = pl.BlockSpec(memory_space=pltpu.VMEM)


def call(kernel, name, in_specs, out_shape, operands, *, limit=48, **kw):
    return pl.pallas_call(
        kernel,
        in_specs=in_specs,
        out_shape=out_shape,
        compiler_params=pltpu.CompilerParams(vmem_limit_bytes=limit << 20),
        cost_estimate=pl.CostEstimate(flops=0, bytes_accessed=0, transcendentals=0),
        name=name,
        **kw,
    )(*operands)


def row_of(slot, rows=ROWS):
    return pl.ds(pl.multiple_of(slot * rows, rows), rows)


def lanes_of(start, width=128):
    return pl.ds(pl.multiple_of(start, 128), width)


def stats_of(x):
    cen = x - jnp.mean(x, axis=1, keepdims=True)
    inv = lax.rsqrt(jnp.mean(cen * cen, axis=1, keepdims=True) + EPS)
    return cen * inv, inv


def partner_of(t, lane):
    return jnp.where(lane % HEAD < ROTARY // 2, pltpu.roll(t, 120, 1), pltpu.roll(t, 8, 1))


def pack_kernel(a_ref, b_ref, c_ref, d_ref, bias_ref, out_ref):
    out_ref[...] = jnp.zeros((16, D), BF16)
    for v, ref in enumerate((a_ref, b_ref, c_ref, d_ref)):
        out_ref[0:1, 256 * v : 256 * v + 256] = ref[...].reshape(1, 256)
    out_ref[1:2, :768] = bias_ref[...].reshape(1, 768)


def pack(*vectors):
    return call(pack_kernel, "pack", [VMEM] * 5, shaped(16, D), vectors, limit=16)


def tables_kernel(info, cos_ref, sin_ref):
    at = lax.broadcasted_iota(jnp.int32, (ROWS, 128), 1) % HEAD
    rate = jnp.exp((at % (ROTARY // 2)).astype(F32) * (-math.log(10000.0) / (ROTARY // 2)))
    row = lax.broadcasted_iota(jnp.int32, (ROWS, 128), 0)
    for j in range(GROUP):
        place = row + (info[ME] ^ (0, 2, 1, 3)[j]) * ROWS
        angle = place.astype(F32) * rate
        sin = jnp.where(at < ROTARY // 2, -jnp.sin(angle), jnp.sin(angle))
        rows = slice(ROWS * j, ROWS * j + ROWS)
        cos_ref[rows, :] = jnp.where(at < ROTARY, jnp.cos(angle), 1.0)
        sin_ref[rows, :] = jnp.where(at < ROTARY, sin, 0.0)


def tables(info):
    return call(tables_kernel, "tables", [SMEM], [shaped(D, 128, dtype=F32)] * 2, (info,), limit=16)


def pick_qkv_kernel(info, w_ref, own, sibling, far):
    for j in range(GROUP):
        d = info[ME] ^ j
        for c in range(3):
            cols = w_ref[:, lanes_of(c * D + d * 256, 256)]
            if j < 2:
                (own, sibling)[j][:, 256 * c : 256 * c + 256] = cols
            else:
                far[ROWS * (j - 2) : ROWS * (j - 1), 256 * c : 256 * c + 256] = cols


def pick_qkv(info, w):
    return call(
        pick_qkv_kernel,
        "pick_qkv",
        [SMEM, VMEM],
        [shaped(ROWS, 768), shaped(ROWS, 768), shaped(2 * ROWS, 768)],
        (info, w),
        limit=32,
    )


def pick_gate_up_kernel(info, w_ref, *refs):
    outs, all_ref = refs[:4], refs[4]
    all_ref[...] = jnp.zeros_like(all_ref)
    for d in range(GROUP):
        all_ref[d, :, :FFS] = w_ref[:, FFS * d : FFS * d + FFS]
        all_ref[d, :, FFP : FFP + FFS] = w_ref[:, FF + FFS * d : FF + FFS * d + FFS]
    for j, out in enumerate(outs):
        out[...] = all_ref[info[ME] ^ j]


def pick_gate_up(info, w):
    return call(
        pick_gate_up_kernel,
        "pick_gate_up",
        [SMEM, VMEM],
        [shaped(ROWS, 2 * FFP)] * 4,
        (info, w),
        limit=32,
        scratch_shapes=[pltpu.VMEM((GROUP, ROWS, 2 * FFP), BF16)],
    )


def project_kernel(
    info, x0, x1, x2, x3, v0, v1, v2, v3, w0, w1, w2, w3, cos_ref, sin_ref,
    hid_ref, qkv_ref, w_ref, norms_ref, bias_ref, sems,
):
    me = info[ME]
    copies = []
    for j, w in enumerate((w0, w1, w2, w3)):
        copy = pltpu.make_async_copy(w.at[:ROWS], w_ref.at[row_of(me ^ j)], sems.at[j])
        copy.start()
        copies.append(copy)
    for j, v in enumerate((v0, v1, v2, v3)):
        owner = me ^ (0, 2, 1, 3)[j]
        extra = v[0:2, :].astype(F32)
        for n in range(4):
            norms_ref[n : n + 1, lanes_of(owner * 256, 256)] = extra[0:1, 256 * n : 256 * n + 256]
        bias_ref[0:1, lanes_of(owner * 768, 768)] = extra[1:2, :768]
    gain, shift = norms_ref[0:1, :], norms_ref[1:2, :]
    bias = jnp.concatenate(
        [bias_ref[0:1, lanes_of(c * D + me * 256, 256)] for c in range(3)], axis=1
    )
    lane = lax.broadcasted_iota(jnp.int32, (ROWS, 128), 1)
    for j, x in enumerate((x0, x1, x2, x3)):
        rows = slice(ROWS * j, ROWS * j + ROWS)
        xhat, _ = stats_of(x[...].astype(F32))
        hid = (xhat * gain + shift).astype(BF16)
        hid_ref[rows, :] = hid
        if j == 0:
            for copy in copies:
                copy.wait()
        proj = dot(hid, w_ref[...]) + bias
        cos, sin = cos_ref[rows, :], sin_ref[rows, :]
        for c in range(4):
            t = proj[:, 128 * c : 128 * c + 128]
            qkv_ref[rows, 128 * c : 128 * c + 128] = (t * cos + partner_of(t, lane) * sin).astype(BF16)
        qkv_ref[rows, 512:] = proj[:, 512:].astype(BF16)


def project(info, xs, vs, ws, cos, sin):
    return call(
        project_kernel,
        "project",
        [SMEM] + [VMEM] * 8 + [ANY] * 4 + [VMEM] * 2,
        [shaped(D, D), shaped(D, 768), shaped(D, 768), shaped(8, D, dtype=F32)],
        (info, *xs, *vs, *ws, cos, sin),
        limit=20,
        scratch_shapes=[pltpu.VMEM((8, 3 * D), F32), pltpu.SemaphoreType.DMA((4,))],
    )


def later_keys():
    return lax.broadcasted_iota(jnp.int32, (ROWS, 2 * ROWS), 0) > (
        lax.broadcasted_iota(jnp.int32, (ROWS, 2 * ROWS), 1) % ROWS
    )


def two_heads(v):
    side = lax.broadcasted_iota(jnp.int32, v.shape, 1) // HEAD
    zero = jnp.zeros((), v.dtype)
    return jnp.concatenate([jnp.where(side == h, v, zero) for h in range(2)], axis=0)


def one_pair(vt):
    return jnp.concatenate([vt[:HEAD, :ROWS], vt[HEAD:, ROWS:]], axis=0).T


def attend_pair(pair, info, qkv_ref, mixed_ref, lse_ref):
    cols = [slice(256 * c + 128 * pair, 256 * c + 128 * pair + 128) for c in range(3)]
    later = later_keys()
    for i in range(GROUP):
        rows = row_of(info[SLOT + i])
        q = two_heads(qkv_ref[rows, cols[0]])
        tiles = []
        for n in range(i + 1):
            st = dot_nt(qkv_ref[row_of(info[SLOT + n]), cols[1]], q)
            tiles.append(jnp.where(later, -1e30, st) if n == i else st)
        top = functools.reduce(jnp.maximum, [jnp.max(t, axis=0, keepdims=True) for t in tiles])
        top = top * SCALE2
        total = jnp.zeros((1, 2 * ROWS), F32)
        out = jnp.zeros((128, 2 * ROWS), F32)
        for n in range(i + 1):
            p = jnp.exp2(tiles[n] * SCALE2 - top)
            total = total + jnp.sum(p, axis=0, keepdims=True)
            out = out + dot_tn(qkv_ref[row_of(info[SLOT + n]), cols[2]], p.astype(BF16))
        mixed_ref[rows, :] = one_pair(out / total).astype(BF16)
        lse = top + jnp.log2(total)
        lse_ref[0:1, rows] = lse[:, :ROWS]
        lse_ref[1:2, rows] = lse[:, ROWS:]


def attend_first_kernel(info, qkv_ref, mixed_ref, lse_ref):
    attend_pair(0, info, qkv_ref, mixed_ref, lse_ref)


def attend_second_kernel(info, qkv_ref, m0, w_ref, mixed_ref, lse_ref, low_ref, up_ref):
    attend_pair(1, info, qkv_ref, mixed_ref, lse_ref)
    for rows, out in ((slice(512, D), up_ref), (slice(0, 512), low_ref)):
        m = jnp.concatenate([m0[rows, :], mixed_ref[rows, :]], axis=1)
        out[...] = dot(m, w_ref[...]).astype(BF16)


def attend_first(info, qkv):
    return call(
        attend_first_kernel,
        "attend_first",
        [SMEM, VMEM],
        [shaped(D, 128), shaped(2, D, dtype=F32)],
        (info, qkv),
        limit=24,
    )


def attend_second(info, qkv, m0, w):
    return call(
        attend_second_kernel,
        "attend_second",
        [SMEM] + [VMEM] * 3,
        [shaped(D, 128), shaped(2, D, dtype=F32), shaped(512, D), shaped(512, D)],
        (info, qkv, m0, w),
        limit=24,
    )


def attend_back_kernel(
    pair, info, qkv_ref, b0, b1, b2, b3, w_ref, lse_ref, cos_ref, sin_ref,
    out_ref, do_ref, dq_ref, dk_ref, dv_ref,
):
    cols = [slice(256 * c + 128 * pair, 256 * c + 128 * pair + 128) for c in range(3)]
    later = later_keys()
    w = w_ref[128 * pair : 128 * pair + 128, :]
    for j, b in enumerate((b0, b1, b2, b3)):
        do_ref[ROWS * j : ROWS * j + ROWS, :] = dot_nt(b[...], w).astype(BF16)
    dk_ref[...] = jnp.zeros_like(dk_ref)
    dv_ref[...] = jnp.zeros_like(dv_ref)
    for i in range(GROUP):
        rows = row_of(info[SLOT + i])
        q = two_heads(qkv_ref[rows, cols[0]])
        do = two_heads(do_ref[rows, :])
        lse = jnp.concatenate([lse_ref[0:1, rows], lse_ref[1:2, rows]], axis=1)
        probs, grads = [], []
        delta = jnp.zeros((1, 2 * ROWS), F32)
        for n in range(i + 1):
            there = row_of(info[SLOT + n])
            p = jnp.exp2(dot_nt(qkv_ref[there, cols[1]], q) * SCALE2 - lse)
            if n == i:
                p = jnp.where(later, 0.0, p)
            dp = dot_nt(qkv_ref[there, cols[2]], do)
            delta = delta + jnp.sum(p * dp, axis=0, keepdims=True)
            dv_ref[there, :] += dot(p.astype(BF16), do)
            probs.append(p)
            grads.append(dp)
        dqt = jnp.zeros((128, 2 * ROWS), F32)
        for n in range(i + 1):
            there = row_of(info[SLOT + n])
            ds = (probs[n] * (grads[n] - delta)).astype(BF16)
            dk_ref[there, :] += dot(ds, q)
            dqt = dqt + dot_tn(qkv_ref[there, cols[1]], ds)
        dq_ref[rows, :] = one_pair(dqt)
    lane = lax.broadcasted_iota(jnp.int32, (D, 128), 1)
    scale = HEAD ** (-0.5)
    cos, sin = cos_ref[...], sin_ref[...]
    dq = dq_ref[...] * scale
    out_ref[:, :128] = (dq * cos - partner_of(dq, lane) * sin).astype(BF16)
    dk = dk_ref[...] * scale
    out_ref[:, 128:256] = (dk * cos - partner_of(dk, lane) * sin).astype(BF16)
    out_ref[:, 256:] = dv_ref[...].astype(BF16)


def attend_back(pair, info, qkv, branch, w, lse, cos, sin):
    return call(
        functools.partial(attend_back_kernel, pair),
        "attend_back",
        [SMEM] + [VMEM] * 9,
        shaped(D, 384),
        (info, qkv, *branch, w, lse, cos, sin),
        limit=32,
        scratch_shapes=[pltpu.VMEM((D, 128), BF16)] + [pltpu.VMEM((D, 128), F32)] * 3,
    )


def whole(first, second):
    return jnp.concatenate(
        [v[:, 128 * c : 128 * c + 128] for c in range(3) for v in (first, second)], axis=1
    )


def hidden_back_kernel(d0, d1, w_ref, low_ref, up_ref):
    for j in range(2):
        rows = slice(512 * j, 512 * j + 512)
        (low_ref, up_ref)[j][...] = dot_nt(whole(d0[rows, :], d1[rows, :]), w_ref[...]).astype(BF16)


def hidden_back(dqkvs, w):
    return call(
        hidden_back_kernel,
        "hidden_back",
        [VMEM] * 3,
        [shaped(512, D), shaped(512, D)],
        (*dqkvs, w),
        limit=24,
    )


def add_halves_kernel(low_ref, got_ref, own_ref, near_ref):
    total = low_ref[...].astype(F32) + got_ref[...].astype(F32)
    own_ref[...] = total[:ROWS, :]
    near_ref[...] = total[ROWS:, :].astype(BF16)


def add_base_kernel(base_ref, low_ref, got_ref, own_ref, near_ref):
    add_halves_kernel(low_ref, got_ref, own_ref, near_ref)
    own_ref[...] += base_ref[...]


def scatter_group_onto(base, low, got):
    return call(
        add_base_kernel,
        "add_base",
        [VMEM] * 3,
        [shaped(ROWS, D, dtype=F32), shaped(ROWS, D)],
        (base, low, got),
        limit=16,
    )


def scatter_group(low, up):
    own, near = call(
        add_halves_kernel,
        "add_halves",
        [VMEM] * 2,
        [shaped(ROWS, D, dtype=F32), shaped(ROWS, D)],
        (low, send(up, SIBLING)),
        limit=16,
    )
    return own, near


def gather_group(own, keep=None):
    near = send(own, ZNEAR)
    return (own, near, send(own, SIBLING), send(near, SIBLING))


def middle_kernel(x_ref, part_ref, other_ref, norms_ref, mid_ref, hid_ref):
    mid = x_ref[...].astype(F32) + part_ref[...] + other_ref[...].astype(F32)
    mid_ref[...] = mid
    xhat, _ = stats_of(mid)
    hid_ref[...] = (xhat * norms_ref[2:3, :] + norms_ref[3:4, :]).astype(BF16)


def middle_of(x, part, other, norms):
    return call(
        middle_kernel,
        "middle",
        [VMEM] * 4,
        [shaped(ROWS, D, dtype=F32), shaped(ROWS, D)],
        (x, part, other, norms),
        limit=16,
    )


def norm_back_kernel(which, part_ref, other_ref, base_ref, res_ref, norms_ref, out_ref, *rest):
    e = part_ref[...] + other_ref[...].astype(F32)
    xhat, inv = stats_of(base_ref[...].astype(F32))
    u = e * norms_ref[which : which + 1, :]
    back = u - jnp.mean(u, axis=1, keepdims=True) - xhat * jnp.mean(u * xhat, axis=1, keepdims=True)
    out = res_ref[...].astype(F32) + inv * back
    out_ref[...] = out
    if rest:
        low_ref, sums_ref = rest
        low_ref[...] = out.astype(BF16)
        sums_ref[0:1, :] = jnp.sum(e * xhat, axis=0, keepdims=True)
        sums_ref[1:2, :] = jnp.sum(e, axis=0, keepdims=True)


def norm_back(part, other, base, res, norms, which):
    outs = [shaped(ROWS, D, dtype=F32)]
    if which == 2:
        outs += [shaped(ROWS, D), shaped(2, D, dtype=F32)]
    return call(
        functools.partial(norm_back_kernel, which),
        "norm_back",
        [VMEM] * 5,
        outs,
        (part, other, base, res, norms),
        limit=16,
    )


def layer_out_kernel(part_ref, other_ref, out_ref):
    out_ref[...] = (part_ref[...] + other_ref[...].astype(F32)).astype(BF16)


def layer_out_of(part, other):
    return call(layer_out_kernel, "layer_out", [VMEM] * 2, shaped(ROWS, D), (part, other), limit=16)


def feed_kernel(
    info, h0, h1, h2, h3, g0, g1, g2, g3, w0, w1, w2, w3, d_ref,
    act_ref, dgu_ref, gh_low, gh_up, out_low, out_up, h_ref, g_ref, w_ref, down_ref, sems,
):
    step = pl.program_id(0)

    def tokens_in(j):
        rows = slice(ROWS * j, ROWS * j + ROWS)
        return (
            pltpu.make_async_copy((h0, h1, h2, h3)[j], h_ref.at[rows], sems.at[j]),
            pltpu.make_async_copy((g0, g1, g2, g3)[j], g_ref.at[rows], sems.at[4 + j]),
        )

    def weights_in():
        for j, w in enumerate((w0, w1, w2, w3)):
            yield pltpu.make_async_copy(w, w_ref.at[row_of(info[ME] ^ j)], sems.at[8 + j])
        yield pltpu.make_async_copy(d_ref, down_ref.at[:FFS], sems.at[12])

    @pl.when(step == 0)
    def _():
        first = [*tokens_in(0), *tokens_in(1)]
        weights = list(weights_in())
        for copy in (*first, *weights, *tokens_in(2), *tokens_in(3)):
            copy.start()
        down_ref[FFS:, :] = jnp.zeros((FFP - FFS, D), BF16)
        for copy in (*first, *weights):
            copy.wait()

    @pl.when(step == 1)
    def _():
        for copy in (*tokens_in(2), *tokens_in(3)):
            copy.wait()

    rows = pl.ds(pl.multiple_of(step * 512, 512), 512)
    h, g = h_ref[rows, :], g_ref[rows, :]
    gate = dot(h, w_ref[:, :FFP])
    up = dot(h, w_ref[:, FFP:])
    sig = jax.nn.sigmoid(gate)
    silu = gate * sig
    act = (silu * up).astype(BF16)
    act_ref[...] = act
    grad_act = dot_nt(g, down_ref[...])
    dgate = (grad_act * up * (sig * (1.0 + gate * (1.0 - sig)))).astype(BF16)
    dup = (grad_act * silu).astype(BF16)
    dgu_ref[:, :FFP] = dgate
    dgu_ref[:, FFP:] = dup
    gh = (dot_nt(dgate, w_ref[:, :FFP]) + dot_nt(dup, w_ref[:, FFP:])).astype(BF16)
    out = dot(act, down_ref[...]).astype(BF16)

    @pl.when(step == 0)
    def _():
        gh_low[...] = gh
        out_low[...] = out

    @pl.when(step == 1)
    def _():
        gh_up[...] = gh
        out_up[...] = out


def feed(info, hs, gs, ws, down):
    row = lambda i: (i, 0)
    fixed = lambda i: (0, 0)
    half = pl.BlockSpec((512, D), fixed)
    return call(
        feed_kernel,
        "feed",
        [SMEM] + [ANY] * 13,
        [shaped(D, FFP), shaped(D, 2 * FFP)] + [shaped(512, D)] * 4,
        (info, *hs, *gs, *ws, down),
        limit=38,
        grid=(2,),
        out_specs=[pl.BlockSpec((512, FFP), row), pl.BlockSpec((512, 2 * FFP), row)] + [half] * 4,
        scratch_shapes=[
            pltpu.VMEM((D, D), BF16),
            pltpu.VMEM((D, D), BF16),
            pltpu.VMEM((D, 2 * FFP), BF16),
            pltpu.VMEM((FFP, D), BF16),
            pltpu.SemaphoreType.DMA((13,)),
        ],
    )


def halve(info, step, rows_of, outs):
    for part in range(2):
        bit, outer, run = SPLITS[part][step]
        mine = info[BIT + bit]
        keep, away = outs[2 * part], outs[2 * part + 1]
        for o in range(outer):
            at = slice(o * run, o * run + run)
            keep[at, :] = rows_of(part, pl.ds(pl.multiple_of((2 * o + mine) * run, run), run))
            away[at, :] = rows_of(part, pl.ds(pl.multiple_of((2 * o + 1 - mine) * run, run), run))


def own_order(info, piece):
    return jnp.where(info[ME] % 2 == 0, piece, ((piece & 3) << 2) | (piece >> 2))


def split_result(info, res_ref, outs):
    for part in range(2):
        mine = info[BIT + part]
        weight = 8 >> part
        for t in range(2):
            for n in range(8):
                low = n if part == 0 else (n & 3) | ((n & 4) << 1)
                to = slice(128 * t + 16 * n, 128 * t + 16 * n + 16)
                for out, bit in ((outs[2 * part], mine), (outs[2 * part + 1], 1 - mine)):
                    out[to, :] = res_ref[part, row_of(16 * t + own_order(info, low + weight * bit), 16), :]


def mlp_weights_kernel(
    info, h0, h1, h2, h3, g0, g1, g2, g3, dgu_ref, act_ref, k1, s1, k2, s2, h_ref, g_ref, res_ref, sems
):
    step = pl.program_id(0)

    def copies(refs, into, first):
        return [
            pltpu.make_async_copy(r, into.at[ROWS * j : ROWS * j + ROWS], sems.at[first + j])
            for j, r in enumerate(refs)
        ]

    @pl.when(step == 0)
    def _():
        hs = copies((h0, h1, h2, h3), h_ref, 0)
        for copy in hs + copies((g0, g1, g2, g3), g_ref, 4):
            copy.start()
        for copy in hs:
            copy.wait()

    @pl.when(step == 2)
    def _():
        for copy in copies((g0, g1, g2, g3), g_ref, 4):
            copy.wait()

    for half in range(2):
        cols = slice(512 * half, 512 * half + 512)

        @pl.when(step < 2)
        def _():
            res_ref[half] = dot_tn(h_ref[:, cols], dgu_ref[...]).astype(BF16)

        @pl.when(step == 2)
        def _():
            res_ref[half] = dot_tn(g_ref[:, cols], act_ref[...]).astype(BF16)

    split_result(info, res_ref, (k1, s1, k2, s2))


def mlp_weights(info, hs, gs, dgu, act):
    col = lambda i: (0, i)
    return call(
        mlp_weights_kernel,
        "mlp_weights",
        [SMEM]
        + [ANY] * 8
        + [pl.BlockSpec((D, FFP), lambda i: (0, jnp.minimum(i, 1))), pl.BlockSpec((D, FFP), lambda i: (0, 0))],
        [shaped(256, 3 * FFP)] * 4,
        (info, *hs, *gs, dgu, act),
        limit=26,
        grid=(3,),
        out_specs=[pl.BlockSpec((256, FFP), col)] * 4,
        scratch_shapes=[
            pltpu.VMEM((D, D), BF16),
            pltpu.VMEM((D, D), BF16),
            pltpu.VMEM((2, 512, FFP), BF16),
            pltpu.SemaphoreType.DMA((8,)),
        ],
    )


EX = 128
ATT = 768 + EX + 256


def attn_weights_kernel(
    info, h_ref, d0, d1, w_ref, m0, m1, b0, b1, b2, b3, norms_ref, sm_ref,
    k1, s1, k2, s2, d_ref, b_ref, ex_ref, res_ref, sems,
):
    me = info[ME]
    copies = [
        pltpu.make_async_copy(r, b_ref.at[ROWS * j : ROWS * j + ROWS], sems.at[j])
        for j, r in enumerate((b0, b1, b2, b3))
    ]
    for copy in copies:
        copy.start()
    d_ref[...] = whole(d0[...], d1[...])
    ex_ref[...] = jnp.zeros_like(ex_ref)
    ex_ref[0:2, :] = norms_ref[0:2, :]
    ex_ref[2:4, :] = sm_ref[...]
    db = dot(jnp.ones((8, D), BF16), d_ref[...])[0:1, :]
    for c in range(3):
        one = db[:, 256 * c : 256 * c + 256]
        ex_ref[pl.ds(8 + 4 * c + me, 1), :] = jnp.concatenate([one] * GROUP, axis=1)
    ex = ex_ref[...].T
    lane = lax.broadcasted_iota(jnp.int32, (512, EX), 1)
    for half in range(2):
        rows = slice(512 * half, 512 * half + 512)
        dw = dot_tn(h_ref[:, rows], d_ref[...])
        res_ref[half, :, :768] = dw.astype(BF16)
        w = w_ref[rows, :].astype(F32)
        gain, shift = ex[rows, 0:1], ex[rows, 1:2]
        sum_e = jnp.sum(w * db, axis=1, keepdims=True)
        sum_xe = (jnp.sum(w * dw, axis=1, keepdims=True) - shift * sum_e) / gain
        cols = jnp.where(lane == 0, sum_xe, jnp.where(lane == 1, sum_e, ex[rows, :]))
        res_ref[half, :, 768 : 768 + EX] = cols.astype(BF16)
    for copy in copies:
        copy.wait()
    m = jnp.concatenate([m0[...], m1[...]], axis=1)
    for half in range(2):
        res_ref[half, :, 768 + EX :] = dot_tn(b_ref[:, 512 * half : 512 * half + 512], m).astype(BF16)
    split_result(info, res_ref, (k1, s1, k2, s2))


def attn_weights(info, hidden, dqkvs, w, mixed, branch, norms, sums_m):
    return call(
        attn_weights_kernel,
        "attn_weights",
        [SMEM] + [VMEM] * 6 + [ANY] * 4 + [VMEM] * 2,
        [shaped(256, ATT)] * 4,
        (info, hidden, *dqkvs, w, *mixed, *branch, norms, sums_m),
        limit=30,
        scratch_shapes=[
            pltpu.VMEM((D, 768), BF16),
            pltpu.VMEM((D, D), BF16),
            pltpu.VMEM((EX, D), F32),
            pltpu.VMEM((2, 512, ATT), BF16),
            pltpu.SemaphoreType.DMA((4,)),
        ],
    )


def add(a, b):
    return (a.astype(F32) + b.astype(F32)).astype(BF16)


def halve_kernel(step, info, a1, g1, a2, g2, *outs):
    ins = ((a1, g1), (a2, g2))
    halve(info, step, lambda part, at: add(ins[part][0][at, :], ins[part][1][at, :]), outs)


def piece_kernel(a1, g1, a2, g2, out):
    out[:32, :] = add(a1[...], g1[...])
    out[32:, :] = add(a2[...], g2[...])


def share_kernel(cols, info, a_ref, g_ref, o0, o1, o2, o3, kept):
    width = a_ref.shape[1] - cols
    for j, out in enumerate((o0, o1, o2, o3)):
        rows = row_of(info[ME] ^ j, 16)
        out[...] = add(a_ref[rows, :cols], g_ref[rows, :cols])
    for t in range(GROUP):
        rows = slice(16 * t, 16 * t + 16)
        kept[:, width * t : width * t + width] = add(a_ref[rows, cols:], g_ref[rows, cols:])


def scatter_plane(info, first, name, gates):
    k1, s1, k2, s2 = first
    width = k1.shape[1]
    s1 = after(s1, *gates[0]())
    s2 = after(s2, *gates[0]())
    for step in range(4):
        got1 = send(s1, CUBE[SPLITS[0][step][0]])
        got2 = send(s2, CUBE[SPLITS[1][step][0]])
        operands = (after(k1, *gates[step + 1]()), got1, k2, got2)
        if step == 3:
            yield call(piece_kernel, "piece_" + name, [VMEM] * 4, shaped(64, width), operands, limit=24)
            return
        rows = k1.shape[0] // 2
        k1, s1, k2, s2 = call(
            functools.partial(halve_kernel, step + 1),
            "halve_" + name,
            [SMEM] + [VMEM] * 4,
            [shaped(rows, width)] * 4,
            (info, *operands),
            limit=24,
        )
        yield k1


def share(info, piece, cols, name, gate=()):
    width = piece.shape[1]
    *blocks, kept = call(
        functools.partial(share_kernel, cols),
        "share_" + name,
        [SMEM] + [VMEM] * 2,
        [shaped(16, cols)] * 4 + [shaped(16, GROUP * (width - cols))],
        (info, after(piece, *gate), send(piece, ZREPLICA)),
        limit=16,
    )
    perms = (None, SIBLING, ZNEAR, ZNEAR_SIBLING)
    return [b if p is None else send(b, p) for b, p in zip(blocks, perms)], kept


def join_mlp_kernel(info, r0, r1, r2, r3, kept, one, two):
    for j, r in enumerate((r0, r1, r2, r3)):
        s = info[ME] ^ j
        one[:, lanes_of(s * FFP, FFP)] = r[:, :FFP]

        @pl.when(s < 2)
        def _():
            one[:, lanes_of((GROUP + s) * FFP, FFP)] = r[:, FFP:]

        @pl.when(s >= 2)
        def _():
            two[:, lanes_of((s - 2) * FFP, FFP)] = r[:, FFP:]

    two[:, 2 * FFP :] = kept[...]


def join_attn_kernel(info, r0, r1, r2, r3, kept, one, two):
    refs = (r0, r1, r2, r3)
    for j, r in enumerate(refs):
        s = info[ME] ^ j
        one[:, lanes_of(s * 256, 256)] = r[:, :256]
        one[:, lanes_of(D + s * 256, 256)] = r[:, 256:512]
        two[:, lanes_of(s * 256, 256)] = r[:, 512:768]
    two[:, D : D + EX] = sum(r[:, 768:].astype(F32) for r in refs).astype(BF16)
    two[:, D + EX :] = kept[...]


def slots_of(info, piece):
    d = own_order(info, piece) ^ (info[BIT] * 8 + info[BIT + 1] * 4 + info[BIT + 2] * 2 + info[BIT + 3])
    return d, ((d >> 2) & 1) * 8 + ((d >> 3) & 1) * 4 + (d & 1) * 2 + ((d >> 1) & 1)


def at_slot(own, got, slot):
    rows = row_of(slot & 7, 16)
    return jnp.where(slot >= 8, got[rows, :].astype(F32), own[rows, :].astype(F32))


def finish_mlp_kernel(info, a1, g1, a2, g2, gu_ref, down_ref, turn_ref):
    for piece in range(16):
        to = slice(16 * piece, 16 * piece + 16)
        one, two = slots_of(info, piece)
        v, u = at_slot(a1, g1, one), at_slot(a2, g2, two)
        for s in range(2 * GROUP):
            src, lo = (v, s * FFP) if s < 6 else (u, (s - 6) * FFP)
            gu_ref[to, FFS * s : FFS * s + FFS] = src[:, lo : lo + FFS]
        turn_ref[to, :] = u[:, 2 * FFP :]
    for t in range(GROUP):
        down_ref[:, 256 * t : 256 * t + 256] = turn_ref[:, FFP * t : FFP * t + FFP].T[:FFS, :]


def finish_attn_kernel(info, a1, g1, a2, g2, qkv_ref, out_ref, vec_ref, turn_ref, ex_ref):
    for piece in range(16):
        to = slice(16 * piece, 16 * piece + 16)
        one, two = slots_of(info, piece)
        qkv_ref[to, : 2 * D] = at_slot(a1, g1, one)
        v = at_slot(a2, g2, two)
        qkv_ref[to, 2 * D :] = v[:, :D]
        ex_ref[to, :] = v[:, D : D + EX]
        turn_ref[to, :] = v[:, D + EX :]
    for t in range(GROUP):
        out_ref[:, 256 * t : 256 * t + 256] = turn_ref[:, 256 * t : 256 * t + 256].T
    vec_ref[...] = ex_ref[...].T


def stack_kernel(a1, g1, a2, g2, one, two):
    rows = a1.shape[0]
    for own, got, out in ((a1, g1, one), (a2, g2, two)):
        out[:rows, :] = own[...]
        out[rows:, :] = got[...]


def gather_plane(parts, name, gates=((), (), ())):
    for step in (3, 2, 1, 0):
        got = [send(p, CUBE[SPLITS[i][step][0]]) for i, p in enumerate(parts)]
        four = (parts[0], got[0], parts[1], got[1])
        yield four
        if step == 0:
            return
        parts = call(
            stack_kernel,
            "stack_" + name,
            [VMEM] * 4,
            [shaped(2 * p.shape[0], p.shape[1]) for p in parts],
            (after(four[0], *gates[3 - step]()), *four[1:]),
            limit=16,
        )


def after(value, *earlier):
    return lax.optimization_barrier((value, *earlier))[0]


def body(
    tokens,
    attn_norm_gain,
    attn_norm_shift,
    qkv_weight,
    qkv_bias,
    out_weight,
    mlp_norm_gain,
    mlp_norm_shift,
    gate_up_weight,
    down_weight,
    cotangent,
):
    me = lax.axis_index("fsdp")
    rank = lax.axis_index("dp")
    x, y = (rank // 4) % 4, rank % 4
    first = jnp.where(me % 2 == 0, x, y)
    second = jnp.where(me % 2 == 0, y, x)
    info = jnp.stack(
        [me]
        + [2 * ((n ^ me) % 2) + (n ^ me) // 2 for n in range(GROUP)]
        + [((first + 1) // 2) % 2, first // 2, ((second + 1) // 2) % 2, second // 2]
    ).astype(jnp.int32)
    near = send(tokens, ZNEAR)
    own_w, sibling_w, far_w = pick_qkv(info, qkv_weight)
    far_w = send(far_w, ZFAR)
    cos, sin = tables(info)
    gate_up_parts = pick_gate_up(info, after(gate_up_weight, own_w))
    vec = pack(
        attn_norm_gain, attn_norm_shift, mlp_norm_gain, mlp_norm_shift, after(qkv_bias, cos, gate_up_parts[0])
    )
    near_vec = send(vec, ZNEAR)
    near = after(near, near_vec)
    xs = (tokens, near, send(tokens, SIBLING), send(near, SIBLING))
    vs = (vec, near_vec, send(vec, SIBLING), send(near_vec, SIBLING))
    qkv_ws = (own_w, send(sibling_w, SIBLING), far_w, send(far_w[ROWS:], SIBLING))
    gs = gather_group(after(cotangent, near))
    gate_up_ws = [
        gate_up_parts[0],
        send(after(gate_up_parts[1], near), SIBLING),
        send(after(gate_up_parts[2], far_w), ZFAR),
    ]
    gate_up_ws.append(send(after(gate_up_parts[3], gate_up_ws[2]), ZFAR_SIBLING))

    hidden, qkv, qkv_w, norms = project(info, xs, vs, qkv_ws, cos, sin)
    m0, lse0 = attend_first(info, qkv)
    m1, lse1, low, up = attend_second(info, qkv, m0, out_weight)
    up = after(up, gate_up_ws[1], gate_up_ws[2], gs[1])
    own, near = scatter_group(low, up)
    mid, hid_own = middle_of(tokens, own, send(near, ZNEAR), norms)
    hs = gather_group(after(hid_own, gate_up_ws[3]))
    act, dgu, gh_low, gh_up, out_low, out_up = feed(info, hs, gs, gate_up_ws, down_weight)

    gh_own, gh_near = scatter_group(gh_low, gh_up)
    mlp_halves = mlp_weights(info, hs, gs, after(dgu, gh_near), act)
    out_got = send(after(out_up, gh_near), SIBLING)
    o_own, o_near = scatter_group_onto(mid, out_low, out_got)
    gh_own = after(gh_own, o_near)
    grad_mid, branch_own, sums_m = norm_back(gh_own, send(gh_near, ZNEAR), mid, cotangent, norms, 2)
    branch = gather_group(after(branch_own, mlp_halves[0]))

    ready = {}
    mlp_sums = scatter_plane(
        info,
        mlp_halves,
        "mlp",
        (
            lambda: (),
            lambda: (branch[2], branch[3]),
            lambda: (ready["dqkv0"],),
            lambda: (ready["dqkv1"],),
            lambda: (),
        ),
    )
    dqkv0 = attend_back(0, after(info, next(mlp_sums)), qkv, branch, out_weight, lse0, cos, sin)
    ready["dqkv0"] = dqkv0
    dqkv1 = attend_back(1, after(info, next(mlp_sums)), qkv, branch, out_weight, lse1, cos, sin)
    ready["dqkv1"] = dqkv1
    dqkvs = (dqkv0, dqkv1)
    ga_low, ga_up = hidden_back((dqkv0, after(dqkv1, next(mlp_sums))), qkv_w)
    attn_halves = attn_weights(
        after(info, ga_low), hidden, dqkvs, qkv_w, (m0, m1), branch, norms, sums_m
    )
    mlp_piece = next(mlp_sums)
    ga_own, ga_near = scatter_group(after(ga_low, mlp_piece), ga_up)
    mlp_blocks, mlp_kept = share(info, mlp_piece, 2 * FFP, "mlp", (ga_near,))
    attn_sums = scatter_plane(
        info,
        attn_halves,
        "attn",
        (
            lambda: (ga_near,),
            lambda: mlp_blocks[1:],
            lambda: ready["got0"],
            lambda: (*ready["got1"], tokens_grad),
            lambda: ready["got2"],
        ),
    )
    sum0 = next(attn_sums)
    ga_other = send(after(ga_near, sum0), ZNEAR)
    (tokens_grad,) = norm_back(ga_own, ga_other, tokens, grad_mid, norms, 0)
    mlp_all = gather_plane(
        call(
            join_mlp_kernel,
            "join_mlp",
            [SMEM] + [VMEM] * 5,
            [shaped(16, 6 * FFP), shaped(16, 6 * FFP)],
            (after(info, sum0), *mlp_blocks, mlp_kept),
            limit=16,
        ),
        "mlp",
        (lambda: (sum1,), lambda: (sum2,), lambda: (attn_piece,)),
    )
    ready["got0"] = next(mlp_all)[1::2]
    sum1 = next(attn_sums)
    ready["got1"] = next(mlp_all)[1::2]
    sum2 = next(attn_sums)
    ready["got2"] = next(mlp_all)[1::2]
    attn_piece = next(attn_sums)
    mlp_four = next(mlp_all)
    attn_blocks, attn_kept = share(info, attn_piece, 768 + EX, "attn", (mlp_four[0],))
    pieces = call(
        join_attn_kernel,
        "join_attn",
        [SMEM] + [VMEM] * 5,
        [shaped(16, 2 * D), shaped(16, 2 * D + EX)],
        (after(info, mlp_four[1], mlp_four[3]), *attn_blocks, attn_kept),
        limit=16,
    )
    *_, attn_four = gather_plane(
        pieces, "attn", (lambda: (), lambda: (), lambda: ())
    )

    grad_gate_up, grad_down = call(
        finish_mlp_kernel,
        "finish_mlp",
        [SMEM] + [VMEM] * 4,
        [shaped(ROWS, 2 * FF, dtype=F32), shaped(FFS, D, dtype=F32)],
        (info, *mlp_four),
        limit=30,
        scratch_shapes=[pltpu.VMEM((ROWS, GROUP * FFP), F32)],
    )
    grad_qkv, grad_out, vec = call(
        finish_attn_kernel,
        "finish_attn",
        [SMEM] + [VMEM] * 4,
        [shaped(ROWS, 3 * D, dtype=F32), shaped(256, D, dtype=F32), shaped(EX, ROWS, dtype=F32)],
        (after(info, grad_down), *attn_four),
        limit=24,
        scratch_shapes=[pltpu.VMEM((ROWS, D), F32), pltpu.VMEM((ROWS, EX), F32)],
    )
    layer_out = layer_out_of(after(o_own, grad_qkv), send(after(o_near, pieces[0]), ZNEAR))
    grad_bias = lax.dynamic_slice_in_dim(vec[8:20].reshape(3 * D), 768 * me, 768, 0)
    return (
        layer_out,
        tokens_grad,
        vec[0],
        vec[1],
        grad_qkv,
        grad_bias,
        grad_out,
        vec[2],
        vec[3],
        grad_gate_up,
        grad_down,
    )


def solution(mesh):
    rows = P(("dp", "fsdp"), None)
    vector = P("fsdp")
    matrix = P("fsdp", None)
    in_specs = (rows, vector, vector, matrix, vector, matrix, vector, vector, matrix, matrix, rows)
    out_specs = (rows, rows, vector, vector, matrix, vector, matrix, vector, vector, matrix, matrix)
    return jax.shard_map(body, mesh=mesh, in_specs=in_specs, out_specs=out_specs, check_vma=False)
```

```python
import functools
import math

import jax
import jax.numpy as jnp
from jax import lax
from jax.experimental import pallas as pl
from jax.experimental.pallas import tpu as pltpu
from jax.sharding import PartitionSpec as P

D = 1024
HEADS = 16
HEAD = 64
ROTARY = 16
FF = 2816
GROUP = 4
ROWS = 256
HALF = 128
FFS = FF // GROUP
FFP = 768
EPS = 1e-05
F32 = jnp.float32
BF16 = jnp.bfloat16
AXES = ("dp", "fsdp")
LOG2E = 1.0 / math.log(2.0)
SCALE2 = HEAD ** (-0.5) * LOG2E


def where_is(lin):
    return [(lin // 16) % 4, (lin // 4) % 4, (lin // 64) * 2 + (lin // 2) % 2, lin % 2]


def linear(x, y, z, core):
    return (((z // 2) * 4 + x) * 4 + y) * 4 + (z % 2) * 2 + core


def perm_of(move):
    return tuple((lin, linear(*move(*where_is(lin)))) for lin in range(128))


def flip(v, which):
    return v ^ 1 if which == 0 else 3 - v


SIBLING = perm_of(lambda x, y, z, c: (x, y, z, 1 - c))
ZNEAR = perm_of(lambda x, y, z, c: (x, y, z ^ 1, c))
ZFAR = perm_of(lambda x, y, z, c: (x, y, 3 - z, c))
ZFAR_SIBLING = perm_of(lambda x, y, z, c: (x, y, 3 - z, 1 - c))
ZNEAR_SIBLING = perm_of(lambda x, y, z, c: (x, y, z ^ 1, 1 - c))
ZREPLICA = perm_of(lambda x, y, z, c: (x, y, (z + 2) % 4, c))
def cube_move(bit):
    def move(x, y, z, c):
        on_x = (bit < 2) == (c == 0)
        return (flip(x, bit % 2), y, z, c) if on_x else (x, flip(y, bit % 2), z, c)

    return perm_of(move)


CUBE = tuple(cube_move(bit) for bit in range(4))
FOUR = (CUBE[3], CUBE[2], tuple((a, CUBE[3][b][1]) for a, b in CUBE[2]))


SPLITS = ((0, 1), (1, 0))
ME, SLOT, BIT = 0, 1, 5


def send(value, perm):
    return lax.ppermute(value, AXES, perm)


def dot(a, b):
    return lax.dot_general(a, b, (((1,), (0,)), ((), ())), preferred_element_type=F32)


def dot_nt(a, b):
    return lax.dot_general(a, b, (((1,), (1,)), ((), ())), preferred_element_type=F32)


def dot_tn(a, b):
    return lax.dot_general(a, b, (((0,), (0,)), ((), ())), preferred_element_type=F32)


def shaped(*shape, dtype=BF16):
    return jax.ShapeDtypeStruct(shape, dtype)


SMEM = pl.BlockSpec(memory_space=pltpu.SMEM)
ANY = pl.BlockSpec(memory_space=pl.ANY)
VMEM = pl.BlockSpec(memory_space=pltpu.VMEM)


def call(kernel, name, in_specs, out_shape, operands, *, us=0, limit=48, **kw):
    return pl.pallas_call(
        kernel,
        in_specs=in_specs,
        out_shape=out_shape,
        compiler_params=pltpu.CompilerParams(vmem_limit_bytes=limit << 20),
        cost_estimate=pl.CostEstimate(flops=us * 10**9, bytes_accessed=us << 20, transcendentals=0),
        name=name,
        **kw,
    )(*operands)


def call_far(kernel, name, out_shape, operands, **kw):
    n = len(operands)
    n_out = len(out_shape) if isinstance(out_shape, list) else 1

    def whole_kernel(*refs):
        ins, outs, held, sems = refs[:n], refs[n : n + n_out], refs[n + n_out : -1], refs[-1]
        copies = [pltpu.make_async_copy(r, h, sems.at[i]) for i, (r, h) in enumerate(zip(ins, held))]
        for copy in copies:
            copy.start()
        for copy in copies:
            copy.wait()
        kernel(*held, *outs)

    return call(
        whole_kernel,
        name,
        [ANY] * n,
        out_shape,
        operands,
        scratch_shapes=[pltpu.VMEM(v.shape, v.dtype) for v in operands] + [pltpu.SemaphoreType.DMA((n,))],
        **kw,
    )


def row_of(slot, rows=ROWS):
    return pl.ds(pl.multiple_of(slot * rows, rows), rows)


def lanes_of(start, width=128):
    return pl.ds(pl.multiple_of(start, 128), width)


def stats_of(x):
    cen = x - jnp.mean(x, axis=1, keepdims=True)
    inv = lax.rsqrt(jnp.mean(cen * cen, axis=1, keepdims=True) + EPS)
    return cen * inv, inv


def partner_of(t, lane):
    return jnp.where(lane % HEAD < ROTARY // 2, pltpu.roll(t, 120, 1), pltpu.roll(t, 8, 1))


def pack_kernel(a_ref, b_ref, c_ref, d_ref, bias_ref, out_ref):
    out_ref[...] = jnp.zeros((16, D), BF16)
    for v, ref in enumerate((a_ref, b_ref, c_ref, d_ref)):
        out_ref[0:1, 256 * v : 256 * v + 256] = ref[...].reshape(1, 256)
    out_ref[1:2, :768] = bias_ref[...].reshape(1, 768)


def pack(*vectors):
    return call(pack_kernel, "pack", [VMEM] * 5, shaped(16, D), vectors, limit=16)


def tables_kernel(info, cos_ref, sin_ref):
    at = lax.broadcasted_iota(jnp.int32, (ROWS, 128), 1) % HEAD
    rate = jnp.exp((at % (ROTARY // 2)).astype(F32) * (-math.log(10000.0) / (ROTARY // 2)))
    row = lax.broadcasted_iota(jnp.int32, (ROWS, 128), 0)
    for j in range(GROUP):
        place = row + (info[ME] ^ (0, 2, 1, 3)[j]) * ROWS
        angle = place.astype(F32) * rate
        sin = jnp.where(at < ROTARY // 2, -jnp.sin(angle), jnp.sin(angle))
        rows = slice(ROWS * j, ROWS * j + ROWS)
        cos_ref[rows, :] = jnp.where(at < ROTARY, jnp.cos(angle), 1.0)
        sin_ref[rows, :] = jnp.where(at < ROTARY, sin, 0.0)


def tables(info):
    return call(tables_kernel, "tables", [SMEM], [shaped(D, 128, dtype=F32)] * 2, (info,), limit=16)


def pick_qkv_kernel(info, w_ref, own, sibling, far):
    for j in range(GROUP):
        d = info[ME] ^ j
        for c in range(3):
            cols = w_ref[:, lanes_of(c * D + d * 256, 256)]
            if j < 2:
                (own, sibling)[j][:, 256 * c : 256 * c + 256] = cols
            else:
                far[ROWS * (j - 2) : ROWS * (j - 1), 256 * c : 256 * c + 256] = cols


def pick_qkv(info, w):
    return call(
        pick_qkv_kernel,
        "pick_qkv",
        [SMEM, VMEM],
        [shaped(ROWS, 768), shaped(ROWS, 768), shaped(2 * ROWS, 768)],
        (info, w),
        limit=32,
    )


CUT = 64


def pick_gate_up_kernel(info, w_ref, *refs):
    outs, all_ref = refs[:5], refs[5]
    all_ref[...] = jnp.zeros_like(all_ref)
    for d in range(GROUP):
        all_ref[d, :, :FFS] = w_ref[:, FFS * d : FFS * d + FFS]
        all_ref[d, :, FFP : FFP + FFS] = w_ref[:, FF + FFS * d : FF + FFS * d + FFS]
    for j, out in enumerate(outs[:3]):
        out[...] = all_ref[info[ME] ^ j]
    outs[3][...] = all_ref[info[ME] ^ 3, :CUT, :]
    outs[4][...] = all_ref[info[ME] ^ 3, CUT:, :]


def pick_gate_up(info, w):
    return call(
        pick_gate_up_kernel,
        "pick_gate_up",
        [SMEM, VMEM],
        [shaped(rows, 2 * FFP) for rows in (ROWS, ROWS, ROWS, CUT, ROWS - CUT)],
        (info, w),
        limit=32,
        scratch_shapes=[pltpu.VMEM((GROUP, ROWS, 2 * FFP), BF16)],
    )


def project_kernel(
    info, x0, x1, x2, x3, v0, v1, v2, v3, w0, w1, w2, w3, cos_ref, sin_ref,
    hid_ref, qkv_ref, w_ref, norms_ref, bias_ref, sems,
):
    me = info[ME]
    copies = []
    for j, w in enumerate((w0, w1, w2, w3)):
        copy = pltpu.make_async_copy(w.at[:ROWS], w_ref.at[row_of(me ^ j)], sems.at[j])
        copy.start()
        copies.append(copy)
    for j, v in enumerate((v0, v1, v2, v3)):
        owner = me ^ (0, 2, 1, 3)[j]
        extra = v[0:2, :].astype(F32)
        for n in range(4):
            norms_ref[n : n + 1, lanes_of(owner * 256, 256)] = extra[0:1, 256 * n : 256 * n + 256]
        bias_ref[0:1, lanes_of(owner * 768, 768)] = extra[1:2, :768]
    gain, shift = norms_ref[0:1, :], norms_ref[1:2, :]
    bias = jnp.concatenate(
        [bias_ref[0:1, lanes_of(c * D + me * 256, 256)] for c in range(3)], axis=1
    )
    lane = lax.broadcasted_iota(jnp.int32, (ROWS, 128), 1)
    for j, x in enumerate((x0, x1, x2, x3)):
        rows = slice(ROWS * j, ROWS * j + ROWS)
        xhat, _ = stats_of(x[...].astype(F32))
        hid = (xhat * gain + shift).astype(BF16)
        hid_ref[rows, :] = hid
        if j == 0:
            for copy in copies:
                copy.wait()
        proj = dot(hid, w_ref[...]) + bias
        cos, sin = cos_ref[rows, :], sin_ref[rows, :]
        for c in range(4):
            t = proj[:, 128 * c : 128 * c + 128]
            qkv_ref[rows, 128 * c : 128 * c + 128] = (t * cos + partner_of(t, lane) * sin).astype(BF16)
        qkv_ref[rows, 512:] = proj[:, 512:].astype(BF16)


def project(info, xs, vs, ws, cos, sin):
    return call(
        project_kernel,
        "project",
        [SMEM] + [VMEM] * 8 + [ANY] * 4 + [VMEM] * 2,
        [shaped(D, D), shaped(D, 768), shaped(D, 768), shaped(8, D, dtype=F32)],
        (info, *xs, *vs, *ws, cos, sin),
        limit=20,
        scratch_shapes=[pltpu.VMEM((8, 3 * D), F32), pltpu.SemaphoreType.DMA((4,))],
    )


def two_heads(v):
    side = lax.broadcasted_iota(jnp.int32, v.shape, 1) // HEAD
    zero = jnp.zeros((), v.dtype)
    return jnp.concatenate([jnp.where(side == h, v, zero) for h in range(2)], axis=0)


def one_pair(vt):
    n = vt.shape[1] // 2
    return jnp.concatenate([vt[:HEAD, :n], vt[HEAD:, n:]], axis=0).T


def later_keys(keys, queries, first):
    return lax.broadcasted_iota(jnp.int32, (keys, 2 * queries), 0) > (
        lax.broadcasted_iota(jnp.int32, (keys, 2 * queries), 1) % queries + first
    )


def half_rows(slot, half):
    return pl.ds(pl.multiple_of(slot * ROWS + half * HALF, HALF), HALF)


def put_blocks(outs, value):
    for j, out in enumerate(outs):
        out[...] = value[HALF * j : HALF * j + HALF, :]


def attend_kernel(half, info, qkv_ref, w_ref, mixed_ref, lse_ref, *outs):
    own_keys = HALF * (half + 1)
    later = later_keys(own_keys, HALF, HALF * half)
    for pair in range(2):
        cols = [slice(256 * c + 128 * pair, 256 * c + 128 * pair + 128) for c in range(3)]
        for i in range(GROUP):
            slot = info[SLOT + i]
            q = two_heads(qkv_ref[half_rows(slot, half), cols[0]])
            there = [row_of(info[SLOT + n]) for n in range(i)]
            there.append(pl.ds(pl.multiple_of(slot * ROWS, ROWS), own_keys))
            tiles = [dot_nt(qkv_ref[at, cols[1]], q) for at in there]
            tiles[i] = jnp.where(later, -1e30, tiles[i])
            top = functools.reduce(jnp.maximum, [jnp.max(t, axis=0, keepdims=True) for t in tiles])
            top = top * SCALE2
            total = jnp.zeros((1, 2 * HALF), F32)
            out = jnp.zeros((128, 2 * HALF), F32)
            for at, tile in zip(there, tiles):
                p = jnp.exp2(tile * SCALE2 - top)
                total = total + jnp.sum(p, axis=0, keepdims=True)
                out = out + dot_tn(qkv_ref[at, cols[2]], p.astype(BF16))
            to = pl.ds(pl.multiple_of(slot * HALF, HALF), HALF)
            mixed_ref[to, 128 * pair : 128 * pair + 128] = one_pair(out / total).astype(BF16)
            lse = top + jnp.log2(total)
            for h in range(2):
                lse_ref[2 * pair + h : 2 * pair + h + 1, to] = lse[:, HALF * h : HALF * h + HALF]
    put_blocks(outs, dot(mixed_ref[...], w_ref[...]).astype(BF16))


def attend(half, info, qkv, w):
    return call(
        functools.partial(attend_kernel, half),
        "attend",
        [SMEM] + [VMEM] * 2,
        [shaped(4 * HALF, 256), shaped(4, 4 * HALF, dtype=F32)] + [shaped(HALF, D)] * 4,
        (info, qkv, w),
        limit=24,
    )


def attend_back_kernel(
    pair, info, qkv_ref, a0, a1, a2, a3, b0, b1, b2, b3, w_ref, lse0, lse1, cos_ref, sin_ref,
    out_ref, do_ref, dq_ref, dk_ref, dv_ref,
):
    cols = [slice(256 * c + 128 * pair, 256 * c + 128 * pair + 128) for c in range(3)]
    later = later_keys(ROWS, ROWS, 0)
    w = w_ref[128 * pair : 128 * pair + 128, :]
    for j, (a, b) in enumerate(((a0, b0), (a1, b1), (a2, b2), (a3, b3))):
        rows = jnp.concatenate([a[...], b[...]], axis=0)
        do_ref[ROWS * j : ROWS * j + ROWS, :] = dot_nt(rows, w).astype(BF16)
    dk_ref[...] = jnp.zeros_like(dk_ref)
    dv_ref[...] = jnp.zeros_like(dv_ref)
    for i in range(GROUP):
        rows = row_of(info[SLOT + i])
        q = two_heads(qkv_ref[rows, cols[0]])
        do = two_heads(do_ref[rows, :])
        to = pl.ds(pl.multiple_of(info[SLOT + i] * HALF, HALF), HALF)
        lse = jnp.concatenate(
            [ref[2 * pair + h : 2 * pair + h + 1, to] for h in range(2) for ref in (lse0, lse1)], axis=1
        )
        probs, grads = [], []
        delta = jnp.zeros((1, 2 * ROWS), F32)
        for n in range(i + 1):
            there = row_of(info[SLOT + n])
            p = jnp.exp2(dot_nt(qkv_ref[there, cols[1]], q) * SCALE2 - lse)
            if n == i:
                p = jnp.where(later, 0.0, p)
            dp = dot_nt(qkv_ref[there, cols[2]], do)
            delta = delta + jnp.sum(p * dp, axis=0, keepdims=True)
            dv_ref[there, :] += dot(p.astype(BF16), do)
            probs.append(p)
            grads.append(dp)
        dqt = jnp.zeros((128, 2 * ROWS), F32)
        for n in range(i + 1):
            there = row_of(info[SLOT + n])
            ds = (probs[n] * (grads[n] - delta)).astype(BF16)
            dk_ref[there, :] += dot(ds, q)
            dqt = dqt + dot_tn(qkv_ref[there, cols[1]], ds)
        dq_ref[rows, :] = one_pair(dqt)
    lane = lax.broadcasted_iota(jnp.int32, (D, 128), 1)
    scale = HEAD ** (-0.5)
    cos, sin = cos_ref[...], sin_ref[...]
    dq = dq_ref[...] * scale
    out_ref[:, :128] = (dq * cos - partner_of(dq, lane) * sin).astype(BF16)
    dk = dk_ref[...] * scale
    out_ref[:, 128:256] = (dk * cos - partner_of(dk, lane) * sin).astype(BF16)
    out_ref[:, 256:] = dv_ref[...].astype(BF16)


def attend_back(pair, info, qkv, branch, w, lse, cos, sin):
    return call(
        functools.partial(attend_back_kernel, pair),
        "attend_back",
        [SMEM] + [VMEM] * 14,
        shaped(D, 384),
        (info, qkv, *branch, w, *lse, cos, sin),
        us=20 * pair,
        limit=32,
        scratch_shapes=[pltpu.VMEM((D, 128), BF16)] + [pltpu.VMEM((D, 128), F32)] * 3,
    )


def whole(first, second):
    return jnp.concatenate(
        [v[:, 128 * c : 128 * c + 128] for c in range(3) for v in (first, second)], axis=1
    )


def hidden_back_kernel(d0, d1, w_ref, *outs):
    for half in range(2):
        rows = slice(512 * half, 512 * half + 512)
        part = dot_nt(whole(d0[rows, :], d1[rows, :]), w_ref[...]).astype(BF16)
        outs[2 * half][...] = part[:ROWS, :]
        outs[2 * half + 1][...] = part[ROWS:, :]


def hidden_back(dqkvs, w):
    return call(
        hidden_back_kernel,
        "hidden_back",
        [VMEM] * 3,
        [shaped(ROWS, D)] * 4,
        (*dqkvs, w),
        limit=24,
    )


def add_near_kernel(low_ref, got_ref, near_ref):
    near_ref[...] = add(low_ref[...], got_ref[...])


def scatter_group(blocks):
    own, near, sibling, both = blocks
    got_near = send(both, SIBLING)
    got_own = send(sibling, SIBLING)
    near = call(add_near_kernel, "add_near", [VMEM] * 2, shaped(ROWS, D), (near, got_near), limit=16)
    return (own, got_own), near


def scatter_half(blocks):
    own, near, sibling, both = blocks
    got_near = send(both, SIBLING)
    got_own = send(sibling, SIBLING)
    near = call(add_near_kernel, "add_half", [VMEM] * 2, shaped(HALF, D), (near, got_near), limit=16)
    return (own, got_own), near


def gather_group(own, keep=None):
    near = send(own, ZNEAR)
    return (own, near, send(own, SIBLING), send(near, SIBLING))


def total_of(*refs):
    return sum(ref[...].astype(F32) for ref in refs)


def half_total(low_ref, got_ref, other_ref):
    return total_of(low_ref.at[:HALF], got_ref.at[:HALF], other_ref)


def middle_kernel(half, x_ref, own_ref, got_ref, other_ref, norms_ref, mid_ref, hid_ref):
    mid = x_ref[HALF * half : HALF * half + HALF, :].astype(F32) + total_of(own_ref, got_ref, other_ref)
    mid_ref[...] = mid
    xhat, _ = stats_of(mid)
    hid_ref[...] = (xhat * norms_ref[2:3, :] + norms_ref[3:4, :]).astype(BF16)


def middle_of(half, x, own, other, norms):
    return call(
        functools.partial(middle_kernel, half),
        "middle",
        [VMEM] * 5,
        [shaped(HALF, D, dtype=F32), shaped(HALF, D)],
        (x, *own, other, norms),
        limit=16,
    )


def norm_back_of(e, x, gain):
    xhat, inv = stats_of(x)
    u = e * gain
    back = u - jnp.mean(u, axis=1, keepdims=True) - xhat * jnp.mean(u * xhat, axis=1, keepdims=True)
    return inv * back, xhat


def middle_back_kernel(
    half, own_ref, got_ref, other_ref, mid_ref, res_ref, norms_ref, out_ref, branch_ref, sums_ref
):
    e = total_of(own_ref, got_ref, other_ref)
    back, xhat = norm_back_of(e, mid_ref[...], norms_ref[2:3, :])
    out = res_ref[HALF * half : HALF * half + HALF, :].astype(F32) + back
    out_ref[...] = out
    branch_ref[...] = out.astype(BF16)
    sums_ref[0:1, :] = jnp.sum(e * xhat, axis=0, keepdims=True)
    sums_ref[1:2, :] = jnp.sum(e, axis=0, keepdims=True)


def middle_back(half, own, other, mid, res, norms, us):
    return call(
        functools.partial(middle_back_kernel, half),
        "middle_back",
        [VMEM] * 6,
        [shaped(HALF, D, dtype=F32), shaped(HALF, D), shaped(2, D, dtype=F32)],
        (*own, other, mid, res, norms),
        us=us,
        limit=16,
    )


def tokens_back_kernel(own_ref, got_ref, other_ref, x_ref, res0, res1, norms_ref, out_ref):
    e = total_of(own_ref, got_ref, other_ref)
    back, _ = norm_back_of(e, x_ref[...].astype(F32), norms_ref[0:1, :])
    out_ref[:HALF, :] = res0[...] + back[:HALF, :]
    out_ref[HALF:, :] = res1[...] + back[HALF:, :]


def tokens_back(own, other, x, res, norms):
    return call_far(
        tokens_back_kernel,
        "tokens_back",
        shaped(ROWS, D, dtype=F32),
        (*own, other, x, *res, norms),
        limit=16,
    )


def out_near_kernel(l0, g0, l1, g1, near_ref):
    near_ref[:HALF, :] = add(l0[HALF:, :], g0[HALF:, :])
    near_ref[HALF:, :] = add(l1[HALF:, :], g1[HALF:, :])


def out_near_of(lows, gots):
    return call_far(
        out_near_kernel,
        "out_near",
        shaped(ROWS, D),
        (lows[0], gots[0], lows[1], gots[1]),
        limit=16,
    )


def layer_out_kernel(m0, m1, l0, g0, l1, g1, other_ref, out_ref):
    for n, (m, low, got) in enumerate(((m0, l0, g0), (m1, l1, g1))):
        rows = slice(HALF * n, HALF * n + HALF)
        out_ref[rows, :] = (m[...] + half_total(low, got, other_ref.at[rows])).astype(BF16)


def layer_out_of(mids, lows, gots, other):
    return call_far(
        layer_out_kernel,
        "layer_out",
        shaped(ROWS, D),
        (*mids, lows[0], gots[0], lows[1], gots[1], other),
        limit=16,
    )


def feed_kernel(h_ref, g_ref, w_ref, down_ref, act_ref, dgu_ref, ghs, out_low, out_up):
    h, g = h_ref[...], g_ref[...]
    gate = dot(h, w_ref[:, :FFP])
    up = dot(h, w_ref[:, FFP:])
    sig = jax.nn.sigmoid(gate)
    silu = gate * sig
    act = (silu * up).astype(BF16)
    act_ref[...] = act
    grad_act = dot_nt(g, down_ref[...])
    dgate = (grad_act * up * (sig * (1.0 + gate * (1.0 - sig)))).astype(BF16)
    dup = (grad_act * silu).astype(BF16)
    dgu_ref[:, :FFP] = dgate
    dgu_ref[:, FFP:] = dup
    put_blocks(ghs, (dot_nt(dgate, w_ref[:, :FFP]) + dot_nt(dup, w_ref[:, FFP:])).astype(BF16))
    out = dot(act, down_ref[...]).astype(BF16)
    out_low[...] = out[:ROWS, :]
    out_up[...] = out[ROWS:, :]


def tokens_in(half, hs, gs, h_ref, g_ref, sems):
    copies = []
    for j in range(GROUP):
        rows = slice(HALF * j, HALF * j + HALF)
        copies.append(pltpu.make_async_copy(hs[j], h_ref.at[rows], sems.at[j]))
        half_g = gs[j].at[HALF * half : HALF * half + HALF]
        copies.append(pltpu.make_async_copy(half_g, g_ref.at[rows], sems.at[GROUP + j]))
    return copies


def feed_first_kernel(
    info, h0, h1, h2, h3, g0, g1, g2, g3, w0, w1, w2, w3, w4, d_ref,
    act_ref, dgu_ref, gh0, gh1, gh2, gh3, out_low, out_up, w_ref, down_ref, h_ref, g_ref, sems,
):
    copies = tokens_in(0, (h0, h1, h2, h3), (g0, g1, g2, g3), h_ref, g_ref, sems)
    for j, w in enumerate((w0, w1, w2)):
        copies.append(pltpu.make_async_copy(w, w_ref.at[row_of(info[ME] ^ j)], sems.at[8 + j]))
    for j, w in enumerate((w3, w4)):
        at = pl.ds(pl.multiple_of((info[ME] ^ 3) * ROWS + j * CUT, CUT), w.shape[0])
        copies.append(pltpu.make_async_copy(w, w_ref.at[at], sems.at[11 + j]))
    copies.append(pltpu.make_async_copy(d_ref, down_ref.at[:FFS], sems.at[13]))
    for copy in copies:
        copy.start()
    down_ref[FFS:, :] = jnp.zeros((FFP - FFS, D), BF16)
    for copy in copies:
        copy.wait()
    feed_kernel(h_ref, g_ref, w_ref, down_ref, act_ref, dgu_ref, (gh0, gh1, gh2, gh3), out_low, out_up)


def feed_second_kernel(
    info, h0, h1, h2, h3, g0, g1, g2, g3, w_ref, down_ref,
    act_ref, dgu_ref, gh0, gh1, gh2, gh3, out_low, out_up, h_ref, g_ref, sems,
):
    copies = tokens_in(1, (h0, h1, h2, h3), (g0, g1, g2, g3), h_ref, g_ref, sems)
    for copy in copies:
        copy.start()
    for copy in copies:
        copy.wait()
    feed_kernel(h_ref, g_ref, w_ref, down_ref, act_ref, dgu_ref, (gh0, gh1, gh2, gh3), out_low, out_up)


FEED_OUT = (
    [shaped(4 * HALF, FFP), shaped(4 * HALF, 2 * FFP)] + [shaped(HALF, D)] * 4 + [shaped(ROWS, D)] * 2
)
FEED_SCRATCH = [pltpu.VMEM((4 * HALF, D), BF16)] * 2


def feed_first(info, hs, gs, ws, down):
    return call(
        feed_first_kernel,
        "feed_first",
        [SMEM] + [ANY] * 14,
        FEED_OUT + [shaped(D, 2 * FFP), shaped(FFP, D)],
        (info, *hs, *gs, *ws, down),
        limit=28,
        scratch_shapes=FEED_SCRATCH + [pltpu.SemaphoreType.DMA((14,))],
    )


def feed_second(info, hs, gs, w, down):
    return call(
        feed_second_kernel,
        "feed_second",
        [SMEM] + [ANY] * 8 + [VMEM] * 2,
        FEED_OUT,
        (info, *hs, *gs, w, down),
        limit=28,
        scratch_shapes=FEED_SCRATCH + [pltpu.SemaphoreType.DMA((8,))],
    )


def own_order(info, piece):
    return jnp.where(info[ME] % 2 == 0, piece, ((piece & 3) << 2) | (piece >> 2))


def split_result(info, res_ref, outs):
    for part in range(2):
        mine = info[BIT + part]
        weight = 8 >> part
        for t in range(2):
            for n in range(8):
                low = n if part == 0 else (n & 3) | ((n & 4) << 1)
                to = slice(128 * t + 16 * n, 128 * t + 16 * n + 16)
                for out, bit in ((outs[2 * part], mine), (outs[2 * part + 1], 1 - mine)):
                    out[to, :] = res_ref[part, row_of(16 * t + own_order(info, low + weight * bit), 16), :]


def mlp_weights_kernel(
    info, h0, h1, h2, h3, h4, h5, h6, h7, g0, g1, g2, g3, dgu0, dgu1, act0, act1,
    k1, s1, k2, s2, h_ref, g_ref, res_ref, sems,
):
    step = pl.program_id(0)

    def copies(which):
        out = []
        for n in range(2 * GROUP):
            rows = slice(HALF * n, HALF * n + HALF)
            half, j = n // GROUP, n % GROUP
            if which == 0:
                out.append(pltpu.make_async_copy((h0, h1, h2, h3, h4, h5, h6, h7)[n], h_ref.at[rows], sems.at[n]))
            else:
                half_g = (g0, g1, g2, g3)[j].at[HALF * half : HALF * half + HALF]
                out.append(pltpu.make_async_copy(half_g, g_ref.at[rows], sems.at[8 + n]))
        return out

    @pl.when(step == 0)
    def _():
        hs = copies(0)
        for copy in hs + copies(1):
            copy.start()
        for copy in hs:
            copy.wait()

    @pl.when(step == 2)
    def _():
        for copy in copies(1):
            copy.wait()

    def product(left, right0, right1, cols):
        both = dot_tn(left[: 4 * HALF, cols], right0[...]) + dot_tn(left[4 * HALF :, cols], right1[...])
        return both.astype(BF16)

    for part in range(2):
        cols = slice(512 * part, 512 * part + 512)

        @pl.when(step < 2)
        def _():
            res_ref[part] = product(h_ref, dgu0, dgu1, cols)

        @pl.when(step == 2)
        def _():
            res_ref[part] = product(g_ref, act0, act1, cols)

    split_result(info, res_ref, (k1, s1, k2, s2))


def mlp_weights(info, hs, gs, dgus, acts):
    col = lambda i: (0, i)
    dgu = pl.BlockSpec((4 * HALF, FFP), lambda i: (0, jnp.minimum(i, 1)))
    act = pl.BlockSpec((4 * HALF, FFP), lambda i: (0, 0))
    return call(
        mlp_weights_kernel,
        "mlp_weights",
        [SMEM] + [ANY] * 12 + [dgu, dgu, act, act],
        [shaped(256, 3 * FFP)] * 4,
        (info, *hs, *gs, *dgus, *acts),
        limit=26,
        grid=(3,),
        out_specs=[pl.BlockSpec((256, FFP), col)] * 4,
        scratch_shapes=[
            pltpu.VMEM((D, D), BF16),
            pltpu.VMEM((D, D), BF16),
            pltpu.VMEM((2, 512, FFP), BF16),
            pltpu.SemaphoreType.DMA((16,)),
        ],
    )


EX = 128
ATT = 768 + EX + 256


def attn_weights_kernel(
    info, h_ref, d0, d1, w_ref, m0, m1, b0, b1, b2, b3, b4, b5, b6, b7, norms_ref, sm0, sm1,
    k1, s1, k2, s2, d_ref, b_ref, ex_ref, res_ref, sems,
):
    me = info[ME]
    copies = [
        pltpu.make_async_copy(r, b_ref.at[HALF * j : HALF * j + HALF], sems.at[j])
        for j, r in enumerate((b0, b1, b2, b3, b4, b5, b6, b7))
    ]
    for copy in copies:
        copy.start()
    d_ref[...] = whole(d0[...], d1[...])
    ex_ref[...] = jnp.zeros_like(ex_ref)
    ex_ref[0:2, :] = norms_ref[0:2, :]
    ex_ref[2:4, :] = sm0[...] + sm1[...]
    db = dot(jnp.ones((8, D), BF16), d_ref[...])[0:1, :]
    for c in range(3):
        one = db[:, 256 * c : 256 * c + 256]
        ex_ref[pl.ds(8 + 4 * c + me, 1), :] = jnp.concatenate([one] * GROUP, axis=1)
    ex = ex_ref[...].T
    lane = lax.broadcasted_iota(jnp.int32, (512, EX), 1)
    for half in range(2):
        rows = slice(512 * half, 512 * half + 512)
        dw = dot_tn(h_ref[:, rows], d_ref[...])
        res_ref[half, :, :768] = dw.astype(BF16)
        w = w_ref[rows, :].astype(F32)
        gain, shift = ex[rows, 0:1], ex[rows, 1:2]
        sum_e = jnp.sum(w * db, axis=1, keepdims=True)
        sum_xe = (jnp.sum(w * dw, axis=1, keepdims=True) - shift * sum_e) / gain
        cols = jnp.where(lane == 0, sum_xe, jnp.where(lane == 1, sum_e, ex[rows, :]))
        res_ref[half, :, 768 : 768 + EX] = cols.astype(BF16)
    for copy in copies:
        copy.wait()
    m = jnp.concatenate([m0[...], m1[...]], axis=0)
    for half in range(2):
        res_ref[half, :, 768 + EX :] = dot_tn(b_ref[:, 512 * half : 512 * half + 512], m).astype(BF16)
    split_result(info, res_ref, (k1, s1, k2, s2))


def attn_weights(info, hidden, dqkvs, w, mixed, branch, norms, sums_m):
    return call(
        attn_weights_kernel,
        "attn_weights",
        [SMEM] + [VMEM] * 6 + [ANY] * 8 + [VMEM] * 3,
        [shaped(256, ATT)] * 4,
        (info, hidden, *dqkvs, w, *mixed, *branch, norms, *sums_m),
        limit=30,
        scratch_shapes=[
            pltpu.VMEM((D, 768), BF16),
            pltpu.VMEM((D, D), BF16),
            pltpu.VMEM((EX, D), F32),
            pltpu.VMEM((2, 512, ATT), BF16),
            pltpu.SemaphoreType.DMA((8,)),
        ],
    )


def add(a, b):
    return (a.astype(F32) + b.astype(F32)).astype(BF16)


def halve_kernel(info, a1, g1, a2, g2, k1, s1, k2, s2):
    for part, (a, g, keep, away) in enumerate(((a1, g1, k1, s1), (a2, g2, k2, s2))):
        mine = info[BIT + SPLITS[part][1]]
        for t in range(2):
            to = slice(64 * t, 64 * t + 64)
            for out, bit in ((keep, mine), (away, 1 - mine)):
                at = row_of(2 * t + bit, 64)
                out[to, :] = add(a[at, :], g[at, :])


def quarter_kernel(info, a1, g1, a2, g2, *outs):
    mine = info[BIT + 2] * 2 + info[BIT + 3]
    for part, (a, g) in enumerate(((a1, g1), (a2, g2))):
        for t in range(2):
            to = slice(32 * part + 16 * t, 32 * part + 16 * t + 16)
            for flips, out in enumerate(outs):
                at = row_of(4 * t + (mine ^ flips), 16)
                out[to, :] = add(a[at, :], g[at, :])


def piece_kernel(a, g1, g2, g3, out):
    out[...] = total_of(a, g1, g2, g3).astype(BF16)


def share_kernel(cols, info, a_ref, g_ref, o0, o1, o2, o3, kept):
    width = a_ref.shape[1] - cols
    for j, out in enumerate((o0, o1, o2, o3)):
        rows = row_of(info[ME] ^ j, 16)
        out[...] = add(a_ref[rows, :cols], g_ref[rows, :cols])
    for t in range(GROUP):
        rows = slice(16 * t, 16 * t + 16)
        kept[:, width * t : width * t + width] = add(a_ref[rows, cols:], g_ref[rows, cols:])


def scatter_plane(info, first, name, gates, start=()):
    k1, s1, k2, s2 = first
    width = k1.shape[1]
    s1, s2 = after(s1, *start), after(s2, *start)
    for step, (kernel, shapes) in enumerate(
        ((halve_kernel, [shaped(128, width)] * 4), (quarter_kernel, [shaped(64, width)] * 4))
    ):
        got1 = send(s1, CUBE[SPLITS[0][step]])
        got2 = send(s2, CUBE[SPLITS[1][step]])
        outs = call(
            kernel,
            ("halve_", "quarter_")[step] + name,
            [SMEM] + [VMEM] * 4,
            shapes,
            (info, after(k1, *gates[step]()), got1, k2, got2),
            limit=24,
        )
        k1, s1, k2, s2 = outs
        yield k1
    keep, *away = outs
    got = [send(a, p) for a, p in zip(away, FOUR)]
    yield call(
        piece_kernel,
        "piece_" + name,
        [VMEM] * 4,
        shaped(64, width),
        (after(keep, *gates[2]()), *got),
        limit=24,
    )


def share(info, piece, cols, name, gate=()):
    width = piece.shape[1]
    *blocks, kept = call(
        functools.partial(share_kernel, cols),
        "share_" + name,
        [SMEM] + [VMEM] * 2,
        [shaped(16, cols)] * 4 + [shaped(16, GROUP * (width - cols))],
        (info, after(piece, *gate), send(piece, ZREPLICA)),
        us=20,
        limit=16,
    )
    perms = (None, SIBLING, ZNEAR, ZNEAR_SIBLING)
    return [b if p is None else send(b, p) for b, p in zip(blocks, perms)], kept


def join_mlp_kernel(info, r0, r1, r2, r3, kept, out):
    for j, r in enumerate((r0, r1, r2, r3)):
        s = info[ME] ^ j
        out[:, lanes_of(s * FFP, FFP)] = r[:, :FFP]
        out[:, lanes_of((GROUP + s) * FFP, FFP)] = r[:, FFP:]
    out[:, 2 * GROUP * FFP :] = kept[...]


def join_attn_kernel(info, r0, r1, r2, r3, kept, out):
    refs = (r0, r1, r2, r3)
    for j, r in enumerate(refs):
        s = info[ME] ^ j
        for c in range(3):
            out[:, lanes_of(c * D + s * 256, 256)] = r[:, 256 * c : 256 * c + 256]
    out[:, 3 * D : 3 * D + EX] = total_of(*(r.at[:, 768:] for r in refs)).astype(BF16)
    out[:, 3 * D + EX :] = kept[...]


def slots_of(info, piece):
    d = own_order(info, piece) ^ (info[BIT] * 8 + info[BIT + 1] * 4 + info[BIT + 2] * 2 + info[BIT + 3])
    return d, ((d >> 2) & 1) * 8 + ((d >> 3) & 1) * 4 + (d & 3)


def at_slot(own, got, slot):
    rows = row_of(slot & 7, 16)
    return jnp.where(slot >= 8, got[rows, :].astype(F32), own[rows, :].astype(F32))


def finish_mlp_kernel(info, a1, g1, a2, g2, gu_ref, down_ref, turn_ref):
    for piece in range(16):
        to = slice(16 * piece, 16 * piece + 16)
        one, two = slots_of(info, piece)
        v, u = at_slot(a1, g1, one), at_slot(a2, g2, two)
        for s in range(2 * GROUP):
            src, lo = (v, s * FFP) if s < 6 else (u, (s - 6) * FFP)
            gu_ref[to, FFS * s : FFS * s + FFS] = src[:, lo : lo + FFS]
        turn_ref[to, :] = u[:, 2 * FFP :]
    for t in range(GROUP):
        down_ref[:, 256 * t : 256 * t + 256] = turn_ref[:, FFP * t : FFP * t + FFP].T[:FFS, :]


def finish_attn_kernel(info, a1, g1, a2, g2, qkv_ref, out_ref, vec_ref, turn_ref, ex_ref):
    for piece in range(16):
        to = slice(16 * piece, 16 * piece + 16)
        one, two = slots_of(info, piece)
        qkv_ref[to, : 2 * D] = at_slot(a1, g1, one)
        v = at_slot(a2, g2, two)
        qkv_ref[to, 2 * D :] = v[:, :D]
        ex_ref[to, :] = v[:, D : D + EX]
        turn_ref[to, :] = v[:, D + EX :]
    for t in range(GROUP):
        out_ref[:, 256 * t : 256 * t + 256] = turn_ref[:, 256 * t : 256 * t + 256].T
    vec_ref[...] = ex_ref[...].T


def stack_four_kernel(own, g1, g2, g3, one, two):
    cut = one.shape[1]
    for n, ref in enumerate((own, g1, g2, g3)):
        rows = slice(16 * n, 16 * n + 16)
        one[rows, :] = ref[:, :cut]
        two[rows, :] = ref[:, cut:]


def stack_kernel(a1, g1, a2, g2, one, two):
    rows = a1.shape[0]
    for own, got, out in ((a1, g1, one), (a2, g2, two)):
        out[:rows, :] = own[...]
        out[rows:, :] = got[...]


def gather_plane(piece, cut, name, gates):
    width = piece.shape[1]
    got = [send(piece, p) for p in FOUR]
    yield got
    parts = call(
        stack_four_kernel,
        "stack_four_" + name,
        [VMEM] * 4,
        [shaped(64, cut), shaped(64, width - cut)],
        (after(piece, *gates[0]()), *got),
        limit=16,
    )
    for step in (1, 0):
        got = [send(p, CUBE[SPLITS[i][step]]) for i, p in enumerate(parts)]
        four = (parts[0], got[0], parts[1], got[1])
        if step == 0:
            yield four
            return
        yield got
        parts = call(
            stack_kernel,
            "stack_" + name,
            [VMEM] * 4,
            [shaped(2 * p.shape[0], p.shape[1]) for p in parts],
            (after(four[0], *gates[1]()), *four[1:]),
            us=20,
            limit=16,
        )


def after(value, *earlier):
    return lax.optimization_barrier((value, *earlier))[0]


def body(
    tokens,
    attn_norm_gain,
    attn_norm_shift,
    qkv_weight,
    qkv_bias,
    out_weight,
    mlp_norm_gain,
    mlp_norm_shift,
    gate_up_weight,
    down_weight,
    cotangent,
):
    me = lax.axis_index("fsdp")
    rank = lax.axis_index("dp")
    x, y = (rank // 4) % 4, rank % 4
    first = jnp.where(me % 2 == 0, x, y)
    second = jnp.where(me % 2 == 0, y, x)
    info = jnp.stack(
        [me]
        + [2 * ((n ^ me) % 2) + (n ^ me) // 2 for n in range(GROUP)]
        + [((first + 1) // 2) % 2, first // 2, ((second + 1) // 2) % 2, second // 2]
    ).astype(jnp.int32)
    near = send(tokens, ZNEAR)
    own_w, sibling_w, far_w = pick_qkv(info, qkv_weight)
    far_w = send(far_w, ZFAR)
    cos, sin = tables(info)
    gate_up_parts = pick_gate_up(info, after(gate_up_weight, own_w))
    vec = pack(
        attn_norm_gain, attn_norm_shift, mlp_norm_gain, mlp_norm_shift, after(qkv_bias, cos, gate_up_parts[0])
    )
    near_vec = send(vec, ZNEAR)
    near = after(near, near_vec)
    xs = (tokens, near, send(tokens, SIBLING), send(near, SIBLING))
    vs = (vec, near_vec, send(vec, SIBLING), send(near_vec, SIBLING))
    qkv_ws = (own_w, send(sibling_w, SIBLING), far_w, send(far_w[ROWS:], SIBLING))
    gs = gather_group(after(cotangent, near))
    gate_up_ws = [
        gate_up_parts[0],
        send(after(gate_up_parts[1], near), SIBLING),
        send(after(gate_up_parts[2], far_w, near_vec), ZFAR),
    ]

    hidden, qkv, qkv_w, norms = project(info, xs, vs, qkv_ws, cos, sin)
    gate_up_ws.append(send(after(gate_up_parts[3], near), ZNEAR_SIBLING))
    mixed, lse, blocks = [], [], []
    for half in range(2):
        m, l, *b = attend(half, after(info, *mixed), qkv, out_weight)
        mixed.append(m)
        lse.append(l)
        blocks.append(b)
    blocks[0][3] = after(blocks[0][3], *gate_up_ws[1:], gs[1])
    gate_up_ws.append(send(after(gate_up_parts[4], gate_up_ws[2], mixed[0]), ZFAR_SIBLING))
    own0, near0 = scatter_half(blocks[0])
    own1, near1 = scatter_half(blocks[1])
    mid0, hid0 = middle_of(0, tokens, own0, after(send(near0, ZNEAR), near1), norms)
    mid1, hid1 = middle_of(1, tokens, own1, send(near1, ZNEAR), norms)
    mids = (mid0, mid1)
    hs = [gather_group(after(hid0, gate_up_ws[4])), gather_group(hid1)]

    act0, dgu0, *blocks0, out_low0, out_up0, feed_w, down_w = feed_first(
        after(info, hid1), hs[0], gs, gate_up_ws, down_weight
    )
    own0, near0 = scatter_half(blocks0)
    act1, dgu1, *blocks1, out_low1, out_up1 = feed_second(after(info, near0), hs[1], gs, feed_w, down_w)
    other0 = send(near0, ZNEAR)
    blocks1[1] = after(blocks1[1], other0)
    own1, near1 = scatter_half(blocks1)
    grad_mid0, branch_own0, sums_m0 = middle_back(0, own0, other0, mids[0], cotangent, norms, 0)
    mlp_halves = mlp_weights(
        info, (*hs[0], *hs[1]), gs, (dgu0, after(dgu1, near1, branch_own0)), (act0, act1)
    )
    other1 = after(send(near1, ZNEAR), mlp_halves[0])
    grad_mid1, branch_own1, sums_m1 = middle_back(1, own1, other1, mids[1], cotangent, norms, 20)
    branch = (*gather_group(branch_own0), *gather_group(branch_own1))
    out_lows = (out_low0, out_low1)
    out_gots = [send(after(v, mlp_halves[0]), SIBLING) for v in (out_up0, out_up1)]
    o_near = out_near_of(out_lows, out_gots)

    ready = {}
    mlp_sums = scatter_plane(
        info,
        mlp_halves,
        "mlp",
        (lambda: (ready["dqkv0"],), lambda: (ready["dqkv1"],), lambda: (ready["halves"][0],)),
        (branch[1],),
    )
    o_other = send(after(o_near, branch[5]), ZNEAR)
    dqkv0 = attend_back(0, after(info, o_near), qkv, branch, out_weight, lse, cos, sin)
    ready["dqkv0"] = dqkv0
    mlp_sum0 = next(mlp_sums)
    dqkv1 = attend_back(1, after(info, mlp_sum0), qkv, branch, out_weight, lse, cos, sin)
    ready["dqkv1"] = dqkv1
    mlp_sum1 = next(mlp_sums)
    dqkvs = (dqkv0, dqkv1)
    layer_out = layer_out_of(mids, out_lows, out_gots, after(o_other, mlp_sum1))
    ga_blocks = hidden_back((after(dqkv0, layer_out), dqkv1), qkv_w)
    attn_halves = attn_weights(
        after(info, ga_blocks[0], mlp_sum1), hidden, dqkvs, qkv_w, mixed, branch, norms, (sums_m0, sums_m1)
    )
    ready["halves"] = attn_halves
    mlp_piece = next(mlp_sums)
    ga_own, ga_near = scatter_group(ga_blocks)
    mlp_blocks, mlp_kept = share(info, mlp_piece, 2 * FFP, "mlp", (attn_halves[0],))
    mlp_joined = call(
        join_mlp_kernel,
        "join_mlp",
        [SMEM] + [VMEM] * 5,
        shaped(16, 3 * GROUP * FFP),
        (info, *mlp_blocks, mlp_kept),
        limit=16,
    )
    attn_sums = scatter_plane(
        info,
        attn_halves,
        "attn",
        (
            lambda: (mlp_blocks[0], ga_near),
            lambda: ready["got0"],
            lambda: ready["got1"],
        ),
    )
    sum0 = next(attn_sums)
    mlp_all = gather_plane(mlp_joined, 6 * FFP, "mlp", (lambda: (sum1,), lambda: (attn_piece,)))
    ready["got0"] = next(mlp_all)
    sum1 = next(attn_sums)
    ready["got1"] = next(mlp_all)
    attn_piece = next(attn_sums)
    attn_blocks, attn_kept = share(info, attn_piece, 768 + EX, "attn")
    mlp_four = next(mlp_all)
    attn_joined = call(
        join_attn_kernel,
        "join_attn",
        [SMEM] + [VMEM] * 5,
        shaped(16, 4 * D + EX),
        (after(info, mlp_four[1], mlp_four[3]), *attn_blocks, attn_kept),
        limit=16,
    )
    attn_all = gather_plane(
        attn_joined, 2 * D, "attn", (lambda: (), lambda: (grad_down, ga_other))
    )
    next(attn_all)
    ga_other = send(after(ga_near, attn_joined), ZNEAR)
    tokens_grad = tokens_back(ga_own, ga_other, tokens, (grad_mid0, grad_mid1), norms)

    grad_gate_up, grad_down = call(
        finish_mlp_kernel,
        "finish_mlp",
        [SMEM] + [VMEM] * 4,
        [shaped(ROWS, 2 * FF, dtype=F32), shaped(FFS, D, dtype=F32)],
        (info, *mlp_four),
        limit=30,
        scratch_shapes=[pltpu.VMEM((ROWS, GROUP * FFP), F32)],
    )
    next(attn_all)
    attn_four = next(attn_all)
    grad_qkv, grad_out, vec = call(
        finish_attn_kernel,
        "finish_attn",
        [SMEM] + [VMEM] * 4,
        [shaped(ROWS, 3 * D, dtype=F32), shaped(256, D, dtype=F32), shaped(EX, ROWS, dtype=F32)],
        (after(info, tokens_grad), *attn_four),
        limit=24,
        scratch_shapes=[pltpu.VMEM((ROWS, D), F32), pltpu.VMEM((ROWS, EX), F32)],
    )
    grad_bias = lax.dynamic_slice_in_dim(vec[8:20].reshape(3 * D), 768 * me, 768, 0)
    return (
        layer_out,
        tokens_grad,
        vec[0],
        vec[1],
        grad_qkv,
        grad_bias,
        grad_out,
        vec[2],
        vec[3],
        grad_gate_up,
        grad_down,
    )


def solution(mesh):
    rows = P(("dp", "fsdp"), None)
    vector = P("fsdp")
    matrix = P("fsdp", None)
    in_specs = (rows, vector, vector, matrix, vector, matrix, vector, vector, matrix, matrix, rows)
    out_specs = (rows, rows, vector, vector, matrix, vector, matrix, vector, vector, matrix, matrix)
    return jax.shard_map(body, mesh=mesh, in_specs=in_specs, out_specs=out_specs, check_vma=False)
```

```python
import functools
import math

import jax
import jax.numpy as jnp
from jax import lax
from jax.experimental import pallas as pl
from jax.experimental.pallas import tpu as pltpu
from jax.sharding import PartitionSpec as P

D = 1024
HEADS = 16
HEAD = 64
ROTARY = 16
FF = 2816
GROUP = 4
ROWS = 256
HALF = 128
FFS = FF // GROUP
FFP = 768
EPS = 1e-05
F32 = jnp.float32
BF16 = jnp.bfloat16
AXES = ("dp", "fsdp")
LOG2E = 1.0 / math.log(2.0)
SCALE2 = HEAD ** (-0.5) * LOG2E


def where_is(lin):
    return [(lin // 16) % 4, (lin // 4) % 4, (lin // 64) * 2 + (lin // 2) % 2, lin % 2]


def linear(x, y, z, core):
    return (((z // 2) * 4 + x) * 4 + y) * 4 + (z % 2) * 2 + core


def perm_of(move):
    return tuple((lin, linear(*move(*where_is(lin)))) for lin in range(128))


def flip(v, which):
    return v ^ 1 if which == 0 else 3 - v


SIBLING = perm_of(lambda x, y, z, c: (x, y, z, 1 - c))
ZNEAR = perm_of(lambda x, y, z, c: (x, y, z ^ 1, c))
ZFAR = perm_of(lambda x, y, z, c: (x, y, 3 - z, c))
ZFAR_SIBLING = perm_of(lambda x, y, z, c: (x, y, 3 - z, 1 - c))
ZNEAR_SIBLING = perm_of(lambda x, y, z, c: (x, y, z ^ 1, 1 - c))
ZREPLICA = perm_of(lambda x, y, z, c: (x, y, (z + 2) % 4, c))
def cube_move(bit):
    def move(x, y, z, c):
        on_x = (bit < 2) == (c == 0)
        return (flip(x, bit % 2), y, z, c) if on_x else (x, flip(y, bit % 2), z, c)

    return perm_of(move)


CUBE = tuple(cube_move(bit) for bit in range(4))
FOUR = (CUBE[3], CUBE[2], tuple((a, CUBE[3][b][1]) for a, b in CUBE[2]))


SPLITS = ((0, 1), (1, 0))
ME, SLOT, BIT = 0, 1, 5


def send(value, perm):
    return lax.ppermute(value, AXES, perm)


def dot(a, b):
    return lax.dot_general(a, b, (((1,), (0,)), ((), ())), preferred_element_type=F32)


def dot_nt(a, b):
    return lax.dot_general(a, b, (((1,), (1,)), ((), ())), preferred_element_type=F32)


def dot_tn(a, b):
    return lax.dot_general(a, b, (((0,), (0,)), ((), ())), preferred_element_type=F32)


def shaped(*shape, dtype=BF16):
    return jax.ShapeDtypeStruct(shape, dtype)


SMEM = pl.BlockSpec(memory_space=pltpu.SMEM)
ANY = pl.BlockSpec(memory_space=pl.ANY)
VMEM = pl.BlockSpec(memory_space=pltpu.VMEM)


def call(kernel, name, in_specs, out_shape, operands, *, us=0, limit=48, **kw):
    return pl.pallas_call(
        kernel,
        in_specs=in_specs,
        out_shape=out_shape,
        compiler_params=pltpu.CompilerParams(vmem_limit_bytes=limit << 20),
        cost_estimate=pl.CostEstimate(flops=us * 10**9, bytes_accessed=us << 20, transcendentals=0),
        name=name,
        **kw,
    )(*operands)


def call_far(kernel, name, out_shape, operands, **kw):
    n = len(operands)
    n_out = len(out_shape) if isinstance(out_shape, list) else 1

    def whole_kernel(*refs):
        ins, outs, held, sems = refs[:n], refs[n : n + n_out], refs[n + n_out : -1], refs[-1]
        copies = [pltpu.make_async_copy(r, h, sems.at[i]) for i, (r, h) in enumerate(zip(ins, held))]
        for copy in copies:
            copy.start()
        for copy in copies:
            copy.wait()
        kernel(*held, *outs)

    return call(
        whole_kernel,
        name,
        [ANY] * n,
        out_shape,
        operands,
        scratch_shapes=[pltpu.VMEM(v.shape, v.dtype) for v in operands] + [pltpu.SemaphoreType.DMA((n,))],
        **kw,
    )


def row_of(slot, rows=ROWS):
    return pl.ds(pl.multiple_of(slot * rows, rows), rows)


def lanes_of(start, width=128):
    return pl.ds(pl.multiple_of(start, 128), width)


def stats_of(x):
    cen = x - jnp.mean(x, axis=1, keepdims=True)
    inv = lax.rsqrt(jnp.mean(cen * cen, axis=1, keepdims=True) + EPS)
    return cen * inv, inv


def partner_of(t, lane):
    return jnp.where(lane % HEAD < ROTARY // 2, pltpu.roll(t, 120, 1), pltpu.roll(t, 8, 1))


def pack_kernel(a_ref, b_ref, c_ref, d_ref, bias_ref, out_ref):
    out_ref[...] = jnp.zeros((16, D), BF16)
    for v, ref in enumerate((a_ref, b_ref, c_ref, d_ref)):
        out_ref[0:1, 256 * v : 256 * v + 256] = ref[...].reshape(1, 256)
    out_ref[1:2, :768] = bias_ref[...].reshape(1, 768)


def pack(*vectors):
    return call(pack_kernel, "pack", [VMEM] * 5, shaped(16, D), vectors, limit=16)


def tables_kernel(info, cos_ref, sin_ref):
    at = lax.broadcasted_iota(jnp.int32, (ROWS, 128), 1) % HEAD
    rate = jnp.exp((at % (ROTARY // 2)).astype(F32) * (-math.log(10000.0) / (ROTARY // 2)))
    row = lax.broadcasted_iota(jnp.int32, (ROWS, 128), 0)
    for j in range(GROUP):
        place = row + (info[ME] ^ (0, 2, 1, 3)[j]) * ROWS
        angle = place.astype(F32) * rate
        sin = jnp.where(at < ROTARY // 2, -jnp.sin(angle), jnp.sin(angle))
        rows = slice(ROWS * j, ROWS * j + ROWS)
        cos_ref[rows, :] = jnp.where(at < ROTARY, jnp.cos(angle), 1.0)
        sin_ref[rows, :] = jnp.where(at < ROTARY, sin, 0.0)


def tables(info):
    return call(tables_kernel, "tables", [SMEM], [shaped(D, 128, dtype=F32)] * 2, (info,), limit=16)


def pick_qkv_kernel(info, w_ref, own, sibling, far):
    for j in range(GROUP):
        d = info[ME] ^ j
        for c in range(3):
            cols = w_ref[:, lanes_of(c * D + d * 256, 256)]
            if j < 2:
                (own, sibling)[j][:, 256 * c : 256 * c + 256] = cols
            else:
                far[ROWS * (j - 2) : ROWS * (j - 1), 256 * c : 256 * c + 256] = cols


def pick_qkv(info, w):
    return call(
        pick_qkv_kernel,
        "pick_qkv",
        [SMEM, VMEM],
        [shaped(ROWS, 768), shaped(ROWS, 768), shaped(2 * ROWS, 768)],
        (info, w),
        limit=32,
    )


CUT = 64


def pick_gate_up_kernel(info, w_ref, *refs):
    outs, all_ref = refs[:5], refs[5]
    all_ref[...] = jnp.zeros_like(all_ref)
    for d in range(GROUP):
        all_ref[d, :, :FFS] = w_ref[:, FFS * d : FFS * d + FFS]
        all_ref[d, :, FFP : FFP + FFS] = w_ref[:, FF + FFS * d : FF + FFS * d + FFS]
    for j, out in enumerate(outs[:3]):
        out[...] = all_ref[info[ME] ^ j]
    outs[3][...] = all_ref[info[ME] ^ 3, :CUT, :]
    outs[4][...] = all_ref[info[ME] ^ 3, CUT:, :]


def pick_gate_up(info, w):
    return call(
        pick_gate_up_kernel,
        "pick_gate_up",
        [SMEM, VMEM],
        [shaped(rows, 2 * FFP) for rows in (ROWS, ROWS, ROWS, CUT, ROWS - CUT)],
        (info, w),
        limit=32,
        scratch_shapes=[pltpu.VMEM((GROUP, ROWS, 2 * FFP), BF16)],
    )


def project_kernel(
    info, x0, x1, x2, x3, v0, v1, v2, v3, w0, w1, w2, w3, cos_ref, sin_ref,
    hid_ref, qkv_ref, w_ref, norms_ref, bias_ref, sems,
):
    me = info[ME]
    copies = []
    for j, w in enumerate((w0, w1, w2, w3)):
        copy = pltpu.make_async_copy(w.at[:ROWS], w_ref.at[row_of(me ^ j)], sems.at[j])
        copy.start()
        copies.append(copy)
    for j, v in enumerate((v0, v1, v2, v3)):
        owner = me ^ (0, 2, 1, 3)[j]
        extra = v[0:2, :].astype(F32)
        for n in range(4):
            norms_ref[n : n + 1, lanes_of(owner * 256, 256)] = extra[0:1, 256 * n : 256 * n + 256]
        bias_ref[0:1, lanes_of(owner * 768, 768)] = extra[1:2, :768]
    gain, shift = norms_ref[0:1, :], norms_ref[1:2, :]
    bias = jnp.concatenate(
        [bias_ref[0:1, lanes_of(c * D + me * 256, 256)] for c in range(3)], axis=1
    )
    lane = lax.broadcasted_iota(jnp.int32, (ROWS, 128), 1)
    for j, x in enumerate((x0, x1, x2, x3)):
        rows = slice(ROWS * j, ROWS * j + ROWS)
        xhat, _ = stats_of(x[...].astype(F32))
        hid = (xhat * gain + shift).astype(BF16)
        hid_ref[rows, :] = hid
        if j == 0:
            for copy in copies:
                copy.wait()
        proj = dot(hid, w_ref[...]) + bias
        cos, sin = cos_ref[rows, :], sin_ref[rows, :]
        for c in range(4):
            t = proj[:, 128 * c : 128 * c + 128]
            qkv_ref[rows, 128 * c : 128 * c + 128] = (t * cos + partner_of(t, lane) * sin).astype(BF16)
        qkv_ref[rows, 512:] = proj[:, 512:].astype(BF16)


def project(info, xs, vs, ws, cos, sin):
    return call(
        project_kernel,
        "project",
        [SMEM] + [VMEM] * 8 + [ANY] * 4 + [VMEM] * 2,
        [shaped(D, D), shaped(D, 768), shaped(D, 768), shaped(8, D, dtype=F32)],
        (info, *xs, *vs, *ws, cos, sin),
        limit=20,
        scratch_shapes=[pltpu.VMEM((8, 3 * D), F32), pltpu.SemaphoreType.DMA((4,))],
    )


def two_heads(v):
    side = lax.broadcasted_iota(jnp.int32, v.shape, 1) // HEAD
    zero = jnp.zeros((), v.dtype)
    return jnp.concatenate([jnp.where(side == h, v, zero) for h in range(2)], axis=0)


def one_pair(vt):
    n = vt.shape[1] // 2
    return jnp.concatenate([vt[:HEAD, :n], vt[HEAD:, n:]], axis=0).T


def later_keys(keys, queries, first):
    return lax.broadcasted_iota(jnp.int32, (keys, 2 * queries), 0) > (
        lax.broadcasted_iota(jnp.int32, (keys, 2 * queries), 1) % queries + first
    )


def half_rows(slot, half):
    return pl.ds(pl.multiple_of(slot * ROWS + half * HALF, HALF), HALF)


def put_blocks(outs, value):
    for j, out in enumerate(outs):
        out[...] = value[HALF * j : HALF * j + HALF, :]


def attend_kernel(half, info, qkv_ref, w_ref, mixed_ref, lse_ref, *outs):
    own_keys = HALF * (half + 1)
    later = later_keys(own_keys, HALF, HALF * half)
    for pair in range(2):
        cols = [slice(256 * c + 128 * pair, 256 * c + 128 * pair + 128) for c in range(3)]
        for i in range(GROUP):
            slot = info[SLOT + i]
            q = two_heads(qkv_ref[half_rows(slot, half), cols[0]])
            there = [row_of(info[SLOT + n]) for n in range(i)]
            there.append(pl.ds(pl.multiple_of(slot * ROWS, ROWS), own_keys))
            tiles = [dot_nt(qkv_ref[at, cols[1]], q) for at in there]
            tiles[i] = jnp.where(later, -1e30, tiles[i])
            top = functools.reduce(jnp.maximum, [jnp.max(t, axis=0, keepdims=True) for t in tiles])
            top = top * SCALE2
            total = jnp.zeros((1, 2 * HALF), F32)
            out = jnp.zeros((128, 2 * HALF), F32)
            for at, tile in zip(there, tiles):
                p = jnp.exp2(tile * SCALE2 - top)
                total = total + jnp.sum(p, axis=0, keepdims=True)
                out = out + dot_tn(qkv_ref[at, cols[2]], p.astype(BF16))
            to = pl.ds(pl.multiple_of(slot * HALF, HALF), HALF)
            mixed_ref[to, 128 * pair : 128 * pair + 128] = one_pair(out / total).astype(BF16)
            lse = top + jnp.log2(total)
            for h in range(2):
                lse_ref[2 * pair + h : 2 * pair + h + 1, to] = lse[:, HALF * h : HALF * h + HALF]
    put_blocks(outs, dot(mixed_ref[...], w_ref[...]).astype(BF16))


def attend(half, info, qkv, w):
    return call(
        functools.partial(attend_kernel, half),
        "attend",
        [SMEM] + [VMEM] * 2,
        [shaped(4 * HALF, 256), shaped(4, 4 * HALF, dtype=F32)] + [shaped(HALF, D)] * 4,
        (info, qkv, w),
        limit=24,
    )


def attend_back_kernel(
    pair, info, qkv_ref, a0, a1, a2, a3, b0, b1, b2, b3, w_ref, lse0, lse1, cos_ref, sin_ref,
    out_ref, do_ref, dq_ref, dk_ref, dv_ref,
):
    cols = [slice(256 * c + 128 * pair, 256 * c + 128 * pair + 128) for c in range(3)]
    later = later_keys(ROWS, ROWS, 0)
    w = w_ref[128 * pair : 128 * pair + 128, :]
    for j, (a, b) in enumerate(((a0, b0), (a1, b1), (a2, b2), (a3, b3))):
        rows = jnp.concatenate([a[...], b[...]], axis=0)
        do_ref[ROWS * j : ROWS * j + ROWS, :] = dot_nt(rows, w).astype(BF16)
    dk_ref[...] = jnp.zeros_like(dk_ref)
    dv_ref[...] = jnp.zeros_like(dv_ref)
    for i in range(GROUP):
        rows = row_of(info[SLOT + i])
        q = two_heads(qkv_ref[rows, cols[0]])
        do = two_heads(do_ref[rows, :])
        to = pl.ds(pl.multiple_of(info[SLOT + i] * HALF, HALF), HALF)
        lse = jnp.concatenate(
            [ref[2 * pair + h : 2 * pair + h + 1, to] for h in range(2) for ref in (lse0, lse1)], axis=1
        )
        probs, grads = [], []
        delta = jnp.zeros((1, 2 * ROWS), F32)
        for n in range(i + 1):
            there = row_of(info[SLOT + n])
            p = jnp.exp2(dot_nt(qkv_ref[there, cols[1]], q) * SCALE2 - lse)
            if n == i:
                p = jnp.where(later, 0.0, p)
            dp = dot_nt(qkv_ref[there, cols[2]], do)
            delta = delta + jnp.sum(p * dp, axis=0, keepdims=True)
            dv_ref[there, :] += dot(p.astype(BF16), do)
            probs.append(p)
            grads.append(dp)
        dqt = jnp.zeros((128, 2 * ROWS), F32)
        for n in range(i + 1):
            there = row_of(info[SLOT + n])
            ds = (probs[n] * (grads[n] - delta)).astype(BF16)
            dk_ref[there, :] += dot(ds, q)
            dqt = dqt + dot_tn(qkv_ref[there, cols[1]], ds)
        dq_ref[rows, :] = one_pair(dqt)
    lane = lax.broadcasted_iota(jnp.int32, (D, 128), 1)
    scale = HEAD ** (-0.5)
    cos, sin = cos_ref[...], sin_ref[...]
    dq = dq_ref[...] * scale
    out_ref[:, :128] = (dq * cos - partner_of(dq, lane) * sin).astype(BF16)
    dk = dk_ref[...] * scale
    out_ref[:, 128:256] = (dk * cos - partner_of(dk, lane) * sin).astype(BF16)
    out_ref[:, 256:] = dv_ref[...].astype(BF16)


def attend_back(pair, info, qkv, branch, w, lse, cos, sin):
    return call(
        functools.partial(attend_back_kernel, pair),
        "attend_back",
        [SMEM] + [VMEM] * 14,
        shaped(D, 384),
        (info, qkv, *branch, w, *lse, cos, sin),
        us=20 * pair,
        limit=32,
        scratch_shapes=[pltpu.VMEM((D, 128), BF16)] + [pltpu.VMEM((D, 128), F32)] * 3,
    )


def whole(first, second):
    return jnp.concatenate(
        [v[:, 128 * c : 128 * c + 128] for c in range(3) for v in (first, second)], axis=1
    )


def hidden_back_kernel(d0, d1, w_ref, *outs):
    for half in range(2):
        rows = slice(512 * half, 512 * half + 512)
        part = dot_nt(whole(d0[rows, :], d1[rows, :]), w_ref[...]).astype(BF16)
        outs[2 * half][...] = part[:ROWS, :]
        outs[2 * half + 1][...] = part[ROWS:, :]


def hidden_back(dqkvs, w):
    return call(
        hidden_back_kernel,
        "hidden_back",
        [VMEM] * 3,
        [shaped(ROWS, D)] * 4,
        (*dqkvs, w),
        limit=24,
    )


def add_near_kernel(low_ref, got_ref, near_ref):
    near_ref[...] = add(low_ref[...], got_ref[...])


def scatter_group(blocks):
    own, near, sibling, both = blocks
    got_near = send(both, SIBLING)
    got_own = send(sibling, SIBLING)
    near = call(add_near_kernel, "add_near", [VMEM] * 2, shaped(ROWS, D), (near, got_near), limit=16)
    return (own, got_own), near


def scatter_half(blocks):
    own, near, sibling, both = blocks
    got_near = send(both, SIBLING)
    got_own = send(sibling, SIBLING)
    near = call(add_near_kernel, "add_half", [VMEM] * 2, shaped(HALF, D), (near, got_near), limit=16)
    return (own, got_own), near


def gather_group(own, keep=None):
    near = send(own, ZNEAR)
    return (own, near, send(own, SIBLING), send(near, SIBLING))


def total_of(*refs):
    return sum(ref[...].astype(F32) for ref in refs)


def half_total(low_ref, got_ref, other_ref):
    return total_of(low_ref.at[:HALF], got_ref.at[:HALF], other_ref)


def middle_kernel(half, x_ref, own_ref, got_ref, other_ref, norms_ref, mid_ref, hid_ref):
    mid = x_ref[HALF * half : HALF * half + HALF, :].astype(F32) + total_of(own_ref, got_ref, other_ref)
    mid_ref[...] = mid
    xhat, _ = stats_of(mid)
    hid_ref[...] = (xhat * norms_ref[2:3, :] + norms_ref[3:4, :]).astype(BF16)


def middle_of(half, x, own, other, norms):
    return call(
        functools.partial(middle_kernel, half),
        "middle",
        [VMEM] * 5,
        [shaped(HALF, D, dtype=F32), shaped(HALF, D)],
        (x, *own, other, norms),
        limit=16,
    )


def norm_back_of(e, x, gain):
    xhat, inv = stats_of(x)
    u = e * gain
    back = u - jnp.mean(u, axis=1, keepdims=True) - xhat * jnp.mean(u * xhat, axis=1, keepdims=True)
    return inv * back, xhat


def middle_back_kernel(
    half, own_ref, got_ref, other_ref, mid_ref, res_ref, norms_ref, out_ref, branch_ref, sums_ref
):
    e = total_of(own_ref, got_ref, other_ref)
    back, xhat = norm_back_of(e, mid_ref[...], norms_ref[2:3, :])
    out = res_ref[HALF * half : HALF * half + HALF, :].astype(F32) + back
    out_ref[...] = out
    branch_ref[...] = out.astype(BF16)
    sums_ref[0:1, :] = jnp.sum(e * xhat, axis=0, keepdims=True)
    sums_ref[1:2, :] = jnp.sum(e, axis=0, keepdims=True)


def middle_back(half, own, other, mid, res, norms, us):
    return call(
        functools.partial(middle_back_kernel, half),
        "middle_back",
        [VMEM] * 6,
        [shaped(HALF, D, dtype=F32), shaped(HALF, D), shaped(2, D, dtype=F32)],
        (*own, other, mid, res, norms),
        us=us,
        limit=16,
    )


def tokens_back_kernel(own_ref, got_ref, other_ref, x_ref, res0, res1, norms_ref, out_ref):
    e = total_of(own_ref, got_ref, other_ref)
    back, _ = norm_back_of(e, x_ref[...].astype(F32), norms_ref[0:1, :])
    out_ref[:HALF, :] = res0[...] + back[:HALF, :]
    out_ref[HALF:, :] = res1[...] + back[HALF:, :]


def tokens_back(own, other, x, res, norms):
    return call_far(
        tokens_back_kernel,
        "tokens_back",
        shaped(ROWS, D, dtype=F32),
        (*own, other, x, *res, norms),
        limit=16,
    )


def out_near_kernel(l0, g0, l1, g1, near_ref):
    near_ref[:HALF, :] = add(l0[HALF:, :], g0[HALF:, :])
    near_ref[HALF:, :] = add(l1[HALF:, :], g1[HALF:, :])


def out_near_of(lows, gots):
    return call_far(
        out_near_kernel,
        "out_near",
        shaped(ROWS, D),
        (lows[0], gots[0], lows[1], gots[1]),
        limit=16,
    )


def layer_out_kernel(m0, m1, l0, g0, l1, g1, other_ref, out_ref):
    for n, (m, low, got) in enumerate(((m0, l0, g0), (m1, l1, g1))):
        rows = slice(HALF * n, HALF * n + HALF)
        out_ref[rows, :] = (m[...] + half_total(low, got, other_ref.at[rows])).astype(BF16)


def layer_out_of(mids, lows, gots, other):
    return call_far(
        layer_out_kernel,
        "layer_out",
        shaped(ROWS, D),
        (*mids, lows[0], gots[0], lows[1], gots[1], other),
        limit=16,
    )


def feed_kernel(h_ref, g_ref, w_ref, down_ref, act_ref, dgu_ref, ghs, out_low, out_up):
    h, g = h_ref[...], g_ref[...]
    gate = dot(h, w_ref[:, :FFP])
    up = dot(h, w_ref[:, FFP:])
    sig = jax.nn.sigmoid(gate)
    silu = gate * sig
    act = (silu * up).astype(BF16)
    act_ref[...] = act
    grad_act = dot_nt(g, down_ref[...])
    dgate = (grad_act * up * (sig * (1.0 + gate * (1.0 - sig)))).astype(BF16)
    dup = (grad_act * silu).astype(BF16)
    dgu_ref[:, :FFP] = dgate
    dgu_ref[:, FFP:] = dup
    put_blocks(ghs, (dot_nt(dgate, w_ref[:, :FFP]) + dot_nt(dup, w_ref[:, FFP:])).astype(BF16))
    out = dot(act, down_ref[...]).astype(BF16)
    out_low[...] = out[:ROWS, :]
    out_up[...] = out[ROWS:, :]


def tokens_in(half, hs, gs, h_ref, g_ref, sems):
    copies = []
    for j in range(GROUP):
        rows = slice(HALF * j, HALF * j + HALF)
        copies.append(pltpu.make_async_copy(hs[j], h_ref.at[rows], sems.at[j]))
        half_g = gs[j].at[HALF * half : HALF * half + HALF]
        copies.append(pltpu.make_async_copy(half_g, g_ref.at[rows], sems.at[GROUP + j]))
    return copies


def feed_first_kernel(
    info, h0, h1, h2, h3, g0, g1, g2, g3, w0, w1, w2, w3, w4, d_ref,
    act_ref, dgu_ref, gh0, gh1, gh2, gh3, out_low, out_up, w_ref, down_ref, h_ref, g_ref, sems,
):
    copies = tokens_in(0, (h0, h1, h2, h3), (g0, g1, g2, g3), h_ref, g_ref, sems)
    for j, w in enumerate((w0, w1, w2)):
        copies.append(pltpu.make_async_copy(w, w_ref.at[row_of(info[ME] ^ j)], sems.at[8 + j]))
    for j, w in enumerate((w3, w4)):
        at = pl.ds(pl.multiple_of((info[ME] ^ 3) * ROWS + j * CUT, CUT), w.shape[0])
        copies.append(pltpu.make_async_copy(w, w_ref.at[at], sems.at[11 + j]))
    copies.append(pltpu.make_async_copy(d_ref, down_ref.at[:FFS], sems.at[13]))
    for copy in copies:
        copy.start()
    down_ref[FFS:, :] = jnp.zeros((FFP - FFS, D), BF16)
    for copy in copies:
        copy.wait()
    feed_kernel(h_ref, g_ref, w_ref, down_ref, act_ref, dgu_ref, (gh0, gh1, gh2, gh3), out_low, out_up)


def feed_second_kernel(
    info, h0, h1, h2, h3, g0, g1, g2, g3, w_ref, down_ref,
    act_ref, dgu_ref, gh0, gh1, gh2, gh3, out_low, out_up, h_ref, g_ref, sems,
):
    copies = tokens_in(1, (h0, h1, h2, h3), (g0, g1, g2, g3), h_ref, g_ref, sems)
    for copy in copies:
        copy.start()
    for copy in copies:
        copy.wait()
    feed_kernel(h_ref, g_ref, w_ref, down_ref, act_ref, dgu_ref, (gh0, gh1, gh2, gh3), out_low, out_up)


FEED_OUT = (
    [shaped(4 * HALF, FFP), shaped(4 * HALF, 2 * FFP)] + [shaped(HALF, D)] * 4 + [shaped(ROWS, D)] * 2
)
FEED_SCRATCH = [pltpu.VMEM((4 * HALF, D), BF16)] * 2


def feed_first(info, hs, gs, ws, down):
    return call(
        feed_first_kernel,
        "feed_first",
        [SMEM] + [ANY] * 14,
        FEED_OUT + [shaped(D, 2 * FFP), shaped(FFP, D)],
        (info, *hs, *gs, *ws, down),
        limit=28,
        scratch_shapes=FEED_SCRATCH + [pltpu.SemaphoreType.DMA((14,))],
    )


def feed_second(info, hs, gs, w, down):
    return call(
        feed_second_kernel,
        "feed_second",
        [SMEM] + [ANY] * 8 + [VMEM] * 2,
        FEED_OUT,
        (info, *hs, *gs, w, down),
        limit=28,
        scratch_shapes=FEED_SCRATCH + [pltpu.SemaphoreType.DMA((8,))],
    )


def own_order(info, piece):
    return jnp.where(info[ME] % 2 == 0, piece, ((piece & 3) << 2) | (piece >> 2))


def split_result(info, res_ref, outs):
    for part in range(2):
        mine = info[BIT + part]
        weight = 8 >> part
        for t in range(2):
            for n in range(8):
                low = n if part == 0 else (n & 3) | ((n & 4) << 1)
                to = slice(128 * t + 16 * n, 128 * t + 16 * n + 16)
                for out, bit in ((outs[2 * part], mine), (outs[2 * part + 1], 1 - mine)):
                    out[to, :] = res_ref[part, row_of(16 * t + own_order(info, low + weight * bit), 16), :]


def mlp_weights_kernel(
    info, h0, h1, h2, h3, h4, h5, h6, h7, g0, g1, g2, g3, dgu0, dgu1, act0, act1,
    k1, s1, k2, s2, h_ref, g_ref, res_ref, sems,
):
    step = pl.program_id(0)

    def copies(which):
        out = []
        for n in range(2 * GROUP):
            rows = slice(HALF * n, HALF * n + HALF)
            half, j = n // GROUP, n % GROUP
            if which == 0:
                out.append(pltpu.make_async_copy((h0, h1, h2, h3, h4, h5, h6, h7)[n], h_ref.at[rows], sems.at[n]))
            else:
                half_g = (g0, g1, g2, g3)[j].at[HALF * half : HALF * half + HALF]
                out.append(pltpu.make_async_copy(half_g, g_ref.at[rows], sems.at[8 + n]))
        return out

    @pl.when(step == 0)
    def _():
        hs = copies(0)
        for copy in hs + copies(1):
            copy.start()
        for copy in hs:
            copy.wait()

    @pl.when(step == 2)
    def _():
        for copy in copies(1):
            copy.wait()

    def product(left, right0, right1, cols):
        both = dot_tn(left[: 4 * HALF, cols], right0[...]) + dot_tn(left[4 * HALF :, cols], right1[...])
        return both.astype(BF16)

    for part in range(2):
        cols = slice(512 * part, 512 * part + 512)

        @pl.when(step < 2)
        def _():
            res_ref[part] = product(h_ref, dgu0, dgu1, cols)

        @pl.when(step == 2)
        def _():
            res_ref[part] = product(g_ref, act0, act1, cols)

    split_result(info, res_ref, (k1, s1, k2, s2))


def mlp_weights(info, hs, gs, dgus, acts):
    col = lambda i: (0, i)
    dgu = pl.BlockSpec((4 * HALF, FFP), lambda i: (0, jnp.minimum(i, 1)))
    act = pl.BlockSpec((4 * HALF, FFP), lambda i: (0, 0))
    return call(
        mlp_weights_kernel,
        "mlp_weights",
        [SMEM] + [ANY] * 12 + [dgu, dgu, act, act],
        [shaped(256, 3 * FFP)] * 4,
        (info, *hs, *gs, *dgus, *acts),
        limit=26,
        grid=(3,),
        out_specs=[pl.BlockSpec((256, FFP), col)] * 4,
        scratch_shapes=[
            pltpu.VMEM((D, D), BF16),
            pltpu.VMEM((D, D), BF16),
            pltpu.VMEM((2, 512, FFP), BF16),
            pltpu.SemaphoreType.DMA((16,)),
        ],
    )


EX = 128
ATT = 768 + EX + 256


def attn_weights_kernel(
    info, h_ref, d0, d1, w_ref, m0, m1, b0, b1, b2, b3, b4, b5, b6, b7, norms_ref, sm0, sm1,
    k1, s1, k2, s2, d_ref, b_ref, ex_ref, res_ref, sems,
):
    me = info[ME]
    copies = [
        pltpu.make_async_copy(r, b_ref.at[HALF * j : HALF * j + HALF], sems.at[j])
        for j, r in enumerate((b0, b1, b2, b3, b4, b5, b6, b7))
    ]
    for copy in copies:
        copy.start()
    d_ref[...] = whole(d0[...], d1[...])
    ex_ref[...] = jnp.zeros_like(ex_ref)
    ex_ref[0:2, :] = norms_ref[0:2, :]
    ex_ref[2:4, :] = sm0[...] + sm1[...]
    db = dot(jnp.ones((8, D), BF16), d_ref[...])[0:1, :]
    for c in range(3):
        one = db[:, 256 * c : 256 * c + 256]
        ex_ref[pl.ds(8 + 4 * c + me, 1), :] = jnp.concatenate([one] * GROUP, axis=1)
    ex = ex_ref[...].T
    lane = lax.broadcasted_iota(jnp.int32, (512, EX), 1)
    for half in range(2):
        rows = slice(512 * half, 512 * half + 512)
        dw = dot_tn(h_ref[:, rows], d_ref[...])
        res_ref[half, :, :768] = dw.astype(BF16)
        w = w_ref[rows, :].astype(F32)
        gain, shift = ex[rows, 0:1], ex[rows, 1:2]
        sum_e = jnp.sum(w * db, axis=1, keepdims=True)
        sum_xe = (jnp.sum(w * dw, axis=1, keepdims=True) - shift * sum_e) / gain
        cols = jnp.where(lane == 0, sum_xe, jnp.where(lane == 1, sum_e, ex[rows, :]))
        res_ref[half, :, 768 : 768 + EX] = cols.astype(BF16)
    for copy in copies:
        copy.wait()
    m = jnp.concatenate([m0[...], m1[...]], axis=0)
    for half in range(2):
        res_ref[half, :, 768 + EX :] = dot_tn(b_ref[:, 512 * half : 512 * half + 512], m).astype(BF16)
    split_result(info, res_ref, (k1, s1, k2, s2))


def attn_weights(info, hidden, dqkvs, w, mixed, branch, norms, sums_m):
    return call(
        attn_weights_kernel,
        "attn_weights",
        [SMEM] + [VMEM] * 6 + [ANY] * 8 + [VMEM] * 3,
        [shaped(256, ATT)] * 4,
        (info, hidden, *dqkvs, w, *mixed, *branch, norms, *sums_m),
        limit=30,
        scratch_shapes=[
            pltpu.VMEM((D, 768), BF16),
            pltpu.VMEM((D, D), BF16),
            pltpu.VMEM((EX, D), F32),
            pltpu.VMEM((2, 512, ATT), BF16),
            pltpu.SemaphoreType.DMA((8,)),
        ],
    )


def add(a, b):
    return (a.astype(F32) + b.astype(F32)).astype(BF16)


def halve_kernel(info, a1, g1, a2, g2, k1, s1, k2, s2):
    for part, (a, g, keep, away) in enumerate(((a1, g1, k1, s1), (a2, g2, k2, s2))):
        mine = info[BIT + SPLITS[part][1]]
        for t in range(2):
            to = slice(64 * t, 64 * t + 64)
            for out, bit in ((keep, mine), (away, 1 - mine)):
                at = row_of(2 * t + bit, 64)
                out[to, :] = add(a[at, :], g[at, :])


def quarter_kernel(info, a1, g1, a2, g2, *outs):
    mine = info[BIT + 2] * 2 + info[BIT + 3]
    for part, (a, g) in enumerate(((a1, g1), (a2, g2))):
        for t in range(2):
            to = slice(32 * part + 16 * t, 32 * part + 16 * t + 16)
            for flips, out in enumerate(outs):
                at = row_of(4 * t + (mine ^ flips), 16)
                out[to, :] = add(a[at, :], g[at, :])


def piece_kernel(a, g1, g2, g3, out):
    out[...] = total_of(a, g1, g2, g3).astype(BF16)


def share_kernel(cols, info, a_ref, g_ref, o0, o1, o2, o3, kept):
    width = a_ref.shape[1] - cols
    for j, out in enumerate((o0, o1, o2, o3)):
        rows = row_of(info[ME] ^ j, 16)
        out[...] = add(a_ref[rows, :cols], g_ref[rows, :cols])
    for t in range(GROUP):
        rows = slice(16 * t, 16 * t + 16)
        kept[:, width * t : width * t + width] = add(a_ref[rows, cols:], g_ref[rows, cols:])


def scatter_plane(info, first, name, gates, start=()):
    k1, s1, k2, s2 = first
    width = k1.shape[1]
    s1, s2 = after(s1, *start), after(s2, *start)
    for step, (kernel, shapes) in enumerate(
        ((halve_kernel, [shaped(128, width)] * 4), (quarter_kernel, [shaped(64, width)] * 4))
    ):
        got1 = send(s1, CUBE[SPLITS[0][step]])
        got2 = send(s2, CUBE[SPLITS[1][step]])
        outs = call(
            kernel,
            ("halve_", "quarter_")[step] + name,
            [SMEM] + [VMEM] * 4,
            shapes,
            (info, after(k1, *gates[step]()), got1, k2, got2),
            limit=24,
        )
        k1, s1, k2, s2 = outs
        yield k1
    keep, *away = outs
    got = [send(a, p) for a, p in zip(away, FOUR)]
    yield call(
        piece_kernel,
        "piece_" + name,
        [VMEM] * 4,
        shaped(64, width),
        (after(keep, *gates[2]()), *got),
        limit=24,
    )


def share(info, piece, cols, name, gate=()):
    width = piece.shape[1]
    *blocks, kept = call(
        functools.partial(share_kernel, cols),
        "share_" + name,
        [SMEM] + [VMEM] * 2,
        [shaped(16, cols)] * 4 + [shaped(16, GROUP * (width - cols))],
        (info, after(piece, *gate), send(piece, ZREPLICA)),
        us=20,
        limit=16,
    )
    perms = (None, SIBLING, ZNEAR, ZNEAR_SIBLING)
    return [b if p is None else send(b, p) for b, p in zip(blocks, perms)], kept


def join_mlp_kernel(info, r0, r1, r2, r3, kept, out):
    for j, r in enumerate((r0, r1, r2, r3)):
        s = info[ME] ^ j
        out[:, lanes_of(s * FFP, FFP)] = r[:, :FFP]
        out[:, lanes_of((GROUP + s) * FFP, FFP)] = r[:, FFP:]
    out[:, 2 * GROUP * FFP :] = kept[...]


def join_attn_kernel(info, r0, r1, r2, r3, kept, out):
    refs = (r0, r1, r2, r3)
    for j, r in enumerate(refs):
        s = info[ME] ^ j
        for c in range(3):
            out[:, lanes_of(c * D + s * 256, 256)] = r[:, 256 * c : 256 * c + 256]
    out[:, 3 * D : 3 * D + EX] = total_of(*(r.at[:, 768:] for r in refs)).astype(BF16)
    out[:, 3 * D + EX :] = kept[...]


def slots_of(info, piece):
    d = own_order(info, piece) ^ (info[BIT] * 8 + info[BIT + 1] * 4 + info[BIT + 2] * 2 + info[BIT + 3])
    return d, ((d >> 2) & 1) * 8 + ((d >> 3) & 1) * 4 + (d & 3)


def at_slot(own, got, slot):
    rows = row_of(slot & 7, 16)
    return jnp.where(slot >= 8, got[rows, :].astype(F32), own[rows, :].astype(F32))


def finish_mlp_kernel(info, a1, g1, a2, g2, gu_ref, down_ref, turn_ref):
    for piece in range(16):
        to = slice(16 * piece, 16 * piece + 16)
        one, two = slots_of(info, piece)
        v, u = at_slot(a1, g1, one), at_slot(a2, g2, two)
        for s in range(2 * GROUP):
            src, lo = (v, s * FFP) if s < 6 else (u, (s - 6) * FFP)
            gu_ref[to, FFS * s : FFS * s + FFS] = src[:, lo : lo + FFS]
        turn_ref[to, :] = u[:, 2 * FFP :]
    for t in range(GROUP):
        down_ref[:, 256 * t : 256 * t + 256] = turn_ref[:, FFP * t : FFP * t + FFP].T[:FFS, :]


def finish_attn_kernel(
    info, a1, g1, a2, g2, qkv_ref, out_ref, v0, v1, v2, v3, bias_ref, turn_ref, ex_ref, vec_ref
):
    for piece in range(16):
        to = slice(16 * piece, 16 * piece + 16)
        one, two = slots_of(info, piece)
        qkv_ref[to, : 2 * D] = at_slot(a1, g1, one)
        v = at_slot(a2, g2, two)
        qkv_ref[to, 2 * D :] = v[:, :D]
        ex_ref[to, :] = v[:, D : D + EX]
        turn_ref[to, :] = v[:, D + EX :]
    for t in range(GROUP):
        out_ref[:, 256 * t : 256 * t + 256] = turn_ref[:, 256 * t : 256 * t + 256].T
    vec_ref[...] = ex_ref[...].T
    for n, ref in enumerate((v0, v1, v2, v3)):
        ref[...] = vec_ref[n : n + 1, :].reshape(256)
    bias = [vec_ref[pl.ds(8 + 3 * info[ME] + n, 1), :] for n in range(3)]
    bias_ref[...] = jnp.concatenate(bias, axis=1).reshape(768)


def stack_four_kernel(own, g1, g2, g3, one, two):
    cut = one.shape[1]
    for n, ref in enumerate((own, g1, g2, g3)):
        rows = slice(16 * n, 16 * n + 16)
        one[rows, :] = ref[:, :cut]
        two[rows, :] = ref[:, cut:]


def stack_kernel(a1, g1, a2, g2, one, two):
    rows = a1.shape[0]
    for own, got, out in ((a1, g1, one), (a2, g2, two)):
        out[:rows, :] = own[...]
        out[rows:, :] = got[...]


def gather_plane(piece, cut, name, gates):
    width = piece.shape[1]
    got = [send(piece, p) for p in FOUR]
    yield got
    parts = call(
        stack_four_kernel,
        "stack_four_" + name,
        [VMEM] * 4,
        [shaped(64, cut), shaped(64, width - cut)],
        (after(piece, *gates[0]()), *got),
        limit=16,
    )
    for step in (1, 0):
        got = [send(p, CUBE[SPLITS[i][step]]) for i, p in enumerate(parts)]
        four = (parts[0], got[0], parts[1], got[1])
        if step == 0:
            yield four
            return
        yield got, parts[0]
        parts = call(
            stack_kernel,
            "stack_" + name,
            [VMEM] * 4,
            [shaped(2 * p.shape[0], p.shape[1]) for p in parts],
            (after(four[0], *gates[1]()), *four[1:]),
            us=20,
            limit=16,
        )


def after(value, *earlier):
    return lax.optimization_barrier((value, *earlier))[0]


def body(
    tokens,
    attn_norm_gain,
    attn_norm_shift,
    qkv_weight,
    qkv_bias,
    out_weight,
    mlp_norm_gain,
    mlp_norm_shift,
    gate_up_weight,
    down_weight,
    cotangent,
):
    me = lax.axis_index("fsdp")
    rank = lax.axis_index("dp")
    x, y = (rank // 4) % 4, rank % 4
    first = jnp.where(me % 2 == 0, x, y)
    second = jnp.where(me % 2 == 0, y, x)
    info = jnp.stack(
        [me]
        + [2 * ((n ^ me) % 2) + (n ^ me) // 2 for n in range(GROUP)]
        + [((first + 1) // 2) % 2, first // 2, ((second + 1) // 2) % 2, second // 2]
    ).astype(jnp.int32)
    near = send(tokens, ZNEAR)
    own_w, sibling_w, far_w = pick_qkv(info, qkv_weight)
    far_w = send(far_w, ZFAR)
    cos, sin = tables(info)
    gate_up_parts = pick_gate_up(info, after(gate_up_weight, own_w))
    vec = pack(
        attn_norm_gain, attn_norm_shift, mlp_norm_gain, mlp_norm_shift, after(qkv_bias, cos, gate_up_parts[0])
    )
    near_vec = send(vec, ZNEAR)
    near = after(near, near_vec)
    xs = (tokens, near, send(tokens, SIBLING), send(near, SIBLING))
    vs = (vec, near_vec, send(vec, SIBLING), send(near_vec, SIBLING))
    qkv_ws = (own_w, send(sibling_w, SIBLING), far_w, send(far_w[ROWS:], SIBLING))
    gs = gather_group(after(cotangent, near))
    gate_up_ws = [
        gate_up_parts[0],
        send(after(gate_up_parts[1], near), SIBLING),
        send(after(gate_up_parts[2], far_w, near_vec), ZFAR),
    ]

    hidden, qkv, qkv_w, norms = project(info, xs, vs, qkv_ws, cos, sin)
    gate_up_ws.append(send(after(gate_up_parts[3], gs[1]), ZNEAR_SIBLING))
    mixed, lse, blocks = [], [], []
    for half in range(2):
        m, l, *b = attend(half, after(info, *mixed), qkv, out_weight)
        mixed.append(m)
        lse.append(l)
        blocks.append(b)
    blocks[0][3] = after(blocks[0][3], *gate_up_ws[1:], gs[1])
    gate_up_ws.append(send(after(gate_up_parts[4], gate_up_ws[2], mixed[0]), ZFAR_SIBLING))
    own0, near0 = scatter_half(blocks[0])
    own1, near1 = scatter_half(blocks[1])
    mid0, hid0 = middle_of(0, tokens, own0, after(send(near0, ZNEAR), near1), norms)
    mid1, hid1 = middle_of(1, tokens, own1, send(near1, ZNEAR), norms)
    mids = (mid0, mid1)
    hs = [gather_group(after(hid0, gate_up_ws[4])), gather_group(hid1)]

    act0, dgu0, *blocks0, out_low0, out_up0, feed_w, down_w = feed_first(
        after(info, hid1), hs[0], gs, gate_up_ws, down_weight
    )
    own0, near0 = scatter_half(blocks0)
    act1, dgu1, *blocks1, out_low1, out_up1 = feed_second(after(info, near0), hs[1], gs, feed_w, down_w)
    other0 = send(near0, ZNEAR)
    blocks1[1] = after(blocks1[1], other0)
    own1, near1 = scatter_half(blocks1)
    grad_mid0, branch_own0, sums_m0 = middle_back(0, own0, other0, mids[0], cotangent, norms, 0)
    mlp_halves = mlp_weights(
        info, (*hs[0], *hs[1]), gs, (dgu0, after(dgu1, near1, branch_own0)), (act0, act1)
    )
    other1 = after(send(near1, ZNEAR), mlp_halves[0])
    grad_mid1, branch_own1, sums_m1 = middle_back(1, own1, other1, mids[1], cotangent, norms, 20)
    branch = (*gather_group(branch_own0), *gather_group(branch_own1))
    out_lows = (out_low0, out_low1)
    out_gots = [send(after(v, mlp_halves[0]), SIBLING) for v in (out_up0, out_up1)]
    o_near = out_near_of(out_lows, out_gots)

    ready = {}
    mlp_sums = scatter_plane(
        info,
        mlp_halves,
        "mlp",
        (lambda: (ready["dqkv0"],), lambda: (ready["dqkv1"], layer_out), lambda: (ready["halves"][0],)),
        (branch[1],),
    )
    o_other = send(after(o_near, branch[5]), ZNEAR)
    dqkv0 = attend_back(0, after(info, o_near), qkv, branch, out_weight, lse, cos, sin)
    ready["dqkv0"] = dqkv0
    mlp_sum0 = next(mlp_sums)
    layer_out = layer_out_of(mids, out_lows, out_gots, after(o_other, mlp_sum0))
    dqkv1 = attend_back(1, after(info, mlp_sum0), qkv, branch, out_weight, lse, cos, sin)
    ready["dqkv1"] = dqkv1
    mlp_sum1 = next(mlp_sums)
    dqkvs = (dqkv0, dqkv1)
    attn_halves = attn_weights(
        after(info, mlp_sum1), hidden, dqkvs, qkv_w, mixed, branch, norms, (sums_m0, sums_m1)
    )
    ready["halves"] = attn_halves
    ga_blocks = hidden_back((after(dqkv0, attn_halves[0]), dqkv1), qkv_w)
    mlp_piece = next(mlp_sums)
    ga_own, ga_near = scatter_group(ga_blocks)
    mlp_blocks, mlp_kept = share(info, mlp_piece, 2 * FFP, "mlp", (attn_halves[0],))
    mlp_joined = call(
        join_mlp_kernel,
        "join_mlp",
        [SMEM] + [VMEM] * 5,
        shaped(16, 3 * GROUP * FFP),
        (info, *mlp_blocks, mlp_kept),
        limit=16,
    )
    attn_sums = scatter_plane(
        info,
        attn_halves,
        "attn",
        (
            lambda: (mlp_blocks[0], ga_near),
            lambda: ready["got0"],
            lambda: ready["got1"],
        ),
    )
    sum0 = next(attn_sums)
    mlp_all = gather_plane(mlp_joined, 6 * FFP, "mlp", (lambda: (sum1,), lambda: (attn_piece,)))
    ready["got0"] = next(mlp_all)
    sum1 = next(attn_sums)
    ready["got1"], _ = next(mlp_all)
    attn_piece = next(attn_sums)
    attn_blocks, attn_kept = share(info, attn_piece, 768 + EX, "attn")
    mlp_four = next(mlp_all)
    attn_joined = call(
        join_attn_kernel,
        "join_attn",
        [SMEM] + [VMEM] * 5,
        shaped(16, 4 * D + EX),
        (after(info, mlp_four[0]), *attn_blocks, attn_kept),
        limit=16,
    )
    attn_all = gather_plane(
        attn_joined, 2 * D, "attn", (lambda: (), lambda: (grad_down,))
    )
    next(attn_all)
    _, attn_stacked = next(attn_all)
    ga_other = send(after(ga_near, attn_stacked), ZNEAR)

    grad_gate_up, grad_down = call(
        finish_mlp_kernel,
        "finish_mlp",
        [SMEM] + [VMEM] * 4,
        [shaped(ROWS, 2 * FF, dtype=F32), shaped(FFS, D, dtype=F32)],
        (info, *mlp_four),
        limit=30,
        scratch_shapes=[pltpu.VMEM((ROWS, GROUP * FFP), F32)],
    )
    attn_four = next(attn_all)
    grad_qkv, grad_out, *vectors, grad_bias = call(
        finish_attn_kernel,
        "finish_attn",
        [SMEM] + [VMEM] * 4,
        [shaped(ROWS, 3 * D, dtype=F32), shaped(256, D, dtype=F32)]
        + [shaped(256, dtype=F32)] * 4
        + [shaped(768, dtype=F32)],
        (info, *attn_four),
        limit=24,
        scratch_shapes=[pltpu.VMEM((ROWS, D), F32), pltpu.VMEM((ROWS, EX), F32), pltpu.VMEM((EX, ROWS), F32)],
    )
    tokens_grad = tokens_back(ga_own, after(ga_other, grad_qkv), tokens, (grad_mid0, grad_mid1), norms)
    return (
        layer_out,
        tokens_grad,
        vectors[0],
        vectors[1],
        grad_qkv,
        grad_bias,
        grad_out,
        vectors[2],
        vectors[3],
        grad_gate_up,
        grad_down,
    )


def solution(mesh):
    rows = P(("dp", "fsdp"), None)
    vector = P("fsdp")
    matrix = P("fsdp", None)
    in_specs = (rows, vector, vector, matrix, vector, matrix, vector, vector, matrix, matrix, rows)
    out_specs = (rows, rows, vector, vector, matrix, vector, matrix, vector, vector, matrix, matrix)
    return jax.shard_map(body, mesh=mesh, in_specs=in_specs, out_specs=out_specs, check_vma=False)
```

```python
import functools
import math

import jax
import jax.numpy as jnp
from jax import lax
from jax.experimental import pallas as pl
from jax.experimental.pallas import tpu as pltpu
from jax.sharding import PartitionSpec as P

D = 1024
HEADS = 16
HEAD = 64
ROTARY = 16
FF = 2816
GROUP = 4
ROWS = 256
HALF = 128
FFS = FF // GROUP
FFP = 768
EPS = 1e-05
F32 = jnp.float32
BF16 = jnp.bfloat16
AXES = ("dp", "fsdp")
LOG2E = 1.0 / math.log(2.0)
SCALE2 = HEAD ** (-0.5) * LOG2E


def where_is(lin):
    return [(lin // 16) % 4, (lin // 4) % 4, (lin // 64) * 2 + (lin // 2) % 2, lin % 2]


def linear(x, y, z, core):
    return (((z // 2) * 4 + x) * 4 + y) * 4 + (z % 2) * 2 + core


def perm_of(move):
    return tuple((lin, linear(*move(*where_is(lin)))) for lin in range(128))


def flip(v, which):
    return v ^ 1 if which == 0 else 3 - v


SIBLING = perm_of(lambda x, y, z, c: (x, y, z, 1 - c))
ZNEAR = perm_of(lambda x, y, z, c: (x, y, z ^ 1, c))
ZFAR = perm_of(lambda x, y, z, c: (x, y, 3 - z, c))
ZFAR_SIBLING = perm_of(lambda x, y, z, c: (x, y, 3 - z, 1 - c))
ZNEAR_SIBLING = perm_of(lambda x, y, z, c: (x, y, z ^ 1, 1 - c))
ZREPLICA = perm_of(lambda x, y, z, c: (x, y, (z + 2) % 4, c))
def cube_move(bit):
    def move(x, y, z, c):
        on_x = (bit < 2) == (c == 0)
        return (flip(x, bit % 2), y, z, c) if on_x else (x, flip(y, bit % 2), z, c)

    return perm_of(move)


CUBE = tuple(cube_move(bit) for bit in range(4))
FOUR = (CUBE[3], CUBE[2], tuple((a, CUBE[3][b][1]) for a, b in CUBE[2]))


SPLITS = ((0, 1), (1, 0))
ME, SLOT, BIT = 0, 1, 5


def send(value, perm):
    return lax.ppermute(value, AXES, perm)


def dot(a, b):
    return lax.dot_general(a, b, (((1,), (0,)), ((), ())), preferred_element_type=F32)


def dot_nt(a, b):
    return lax.dot_general(a, b, (((1,), (1,)), ((), ())), preferred_element_type=F32)


def dot_tn(a, b):
    return lax.dot_general(a, b, (((0,), (0,)), ((), ())), preferred_element_type=F32)


def shaped(*shape, dtype=BF16):
    return jax.ShapeDtypeStruct(shape, dtype)


SMEM = pl.BlockSpec(memory_space=pltpu.SMEM)
ANY = pl.BlockSpec(memory_space=pl.ANY)
VMEM = pl.BlockSpec(memory_space=pltpu.VMEM)


def call(kernel, name, in_specs, out_shape, operands, *, us=0, limit=48, **kw):
    return pl.pallas_call(
        kernel,
        in_specs=in_specs,
        out_shape=out_shape,
        compiler_params=pltpu.CompilerParams(vmem_limit_bytes=limit << 20),
        cost_estimate=pl.CostEstimate(flops=us * 10**9, bytes_accessed=us << 20, transcendentals=0),
        name=name,
        **kw,
    )(*operands)


def call_far(kernel, name, out_shape, operands, **kw):
    n = len(operands)
    n_out = len(out_shape) if isinstance(out_shape, list) else 1

    def whole_kernel(*refs):
        ins, outs, held, sems = refs[:n], refs[n : n + n_out], refs[n + n_out : -1], refs[-1]
        copies = [pltpu.make_async_copy(r, h, sems.at[i]) for i, (r, h) in enumerate(zip(ins, held))]
        for copy in copies:
            copy.start()
        for copy in copies:
            copy.wait()
        kernel(*held, *outs)

    return call(
        whole_kernel,
        name,
        [ANY] * n,
        out_shape,
        operands,
        scratch_shapes=[pltpu.VMEM(v.shape, v.dtype) for v in operands] + [pltpu.SemaphoreType.DMA((n,))],
        **kw,
    )


def row_of(slot, rows=ROWS):
    return pl.ds(pl.multiple_of(slot * rows, rows), rows)


def lanes_of(start, width=128):
    return pl.ds(pl.multiple_of(start, 128), width)


def stats_of(x):
    cen = x - jnp.mean(x, axis=1, keepdims=True)
    inv = lax.rsqrt(jnp.mean(cen * cen, axis=1, keepdims=True) + EPS)
    return cen * inv, inv


def partner_of(t, lane):
    return jnp.where(lane % HEAD < ROTARY // 2, pltpu.roll(t, 120, 1), pltpu.roll(t, 8, 1))


def pack_kernel(a_ref, b_ref, c_ref, d_ref, bias_ref, out_ref):
    out_ref[...] = jnp.zeros((16, D), BF16)
    for v, ref in enumerate((a_ref, b_ref, c_ref, d_ref)):
        out_ref[0:1, 256 * v : 256 * v + 256] = ref[...].reshape(1, 256)
    out_ref[1:2, :768] = bias_ref[...].reshape(1, 768)


def pack(*vectors):
    return call(pack_kernel, "pack", [VMEM] * 5, shaped(16, D), vectors, limit=16)


def tables_kernel(info, cos_ref, sin_ref):
    at = lax.broadcasted_iota(jnp.int32, (ROWS, 128), 1) % HEAD
    rate = jnp.exp((at % (ROTARY // 2)).astype(F32) * (-math.log(10000.0) / (ROTARY // 2)))
    row = lax.broadcasted_iota(jnp.int32, (ROWS, 128), 0)
    for j in range(GROUP):
        place = row + (info[ME] ^ (0, 2, 1, 3)[j]) * ROWS
        angle = place.astype(F32) * rate
        sin = jnp.where(at < ROTARY // 2, -jnp.sin(angle), jnp.sin(angle))
        rows = slice(ROWS * j, ROWS * j + ROWS)
        cos_ref[rows, :] = jnp.where(at < ROTARY, jnp.cos(angle), 1.0)
        sin_ref[rows, :] = jnp.where(at < ROTARY, sin, 0.0)


def tables(info):
    return call(tables_kernel, "tables", [SMEM], [shaped(D, 128, dtype=F32)] * 2, (info,), limit=16)


def pick_qkv_kernel(info, w_ref, own, sibling, far):
    for j in range(GROUP):
        d = info[ME] ^ j
        for c in range(3):
            cols = w_ref[:, lanes_of(c * D + d * 256, 256)]
            if j < 2:
                (own, sibling)[j][:, 256 * c : 256 * c + 256] = cols
            else:
                far[ROWS * (j - 2) : ROWS * (j - 1), 256 * c : 256 * c + 256] = cols


def pick_qkv(info, w):
    return call(
        pick_qkv_kernel,
        "pick_qkv",
        [SMEM, VMEM],
        [shaped(ROWS, 768), shaped(ROWS, 768), shaped(2 * ROWS, 768)],
        (info, w),
        limit=32,
    )


CUT = 64


def pick_gate_up_kernel(info, w_ref, *refs):
    outs, all_ref = refs[:5], refs[5]
    all_ref[...] = jnp.zeros_like(all_ref)
    for d in range(GROUP):
        all_ref[d, :, :FFS] = w_ref[:, FFS * d : FFS * d + FFS]
        all_ref[d, :, FFP : FFP + FFS] = w_ref[:, FF + FFS * d : FF + FFS * d + FFS]
    for j, out in enumerate(outs[:3]):
        out[...] = all_ref[info[ME] ^ j]
    outs[3][...] = all_ref[info[ME] ^ 3, :CUT, :]
    outs[4][...] = all_ref[info[ME] ^ 3, CUT:, :]


def pick_gate_up(info, w):
    return call(
        pick_gate_up_kernel,
        "pick_gate_up",
        [SMEM, VMEM],
        [shaped(rows, 2 * FFP) for rows in (ROWS, ROWS, ROWS, CUT, ROWS - CUT)],
        (info, w),
        limit=32,
        scratch_shapes=[pltpu.VMEM((GROUP, ROWS, 2 * FFP), BF16)],
    )


def project_kernel(
    info, x0, x1, x2, x3, v0, v1, v2, v3, w0, w1, w2, w3, cos_ref, sin_ref,
    hid_ref, qkv_ref, w_ref, norms_ref, bias_ref, sems,
):
    me = info[ME]
    copies = []
    for j, w in enumerate((w0, w1, w2, w3)):
        copy = pltpu.make_async_copy(w.at[:ROWS], w_ref.at[row_of(me ^ j)], sems.at[j])
        copy.start()
        copies.append(copy)
    for j, v in enumerate((v0, v1, v2, v3)):
        owner = me ^ (0, 2, 1, 3)[j]
        extra = v[0:2, :].astype(F32)
        for n in range(4):
            norms_ref[n : n + 1, lanes_of(owner * 256, 256)] = extra[0:1, 256 * n : 256 * n + 256]
        bias_ref[0:1, lanes_of(owner * 768, 768)] = extra[1:2, :768]
    gain, shift = norms_ref[0:1, :], norms_ref[1:2, :]
    bias = jnp.concatenate(
        [bias_ref[0:1, lanes_of(c * D + me * 256, 256)] for c in range(3)], axis=1
    )
    lane = lax.broadcasted_iota(jnp.int32, (ROWS, 128), 1)
    for j, x in enumerate((x0, x1, x2, x3)):
        rows = slice(ROWS * j, ROWS * j + ROWS)
        xhat, _ = stats_of(x[...].astype(F32))
        hid = (xhat * gain + shift).astype(BF16)
        hid_ref[rows, :] = hid
        if j == 0:
            for copy in copies:
                copy.wait()
        proj = dot(hid, w_ref[...]) + bias
        cos, sin = cos_ref[rows, :], sin_ref[rows, :]
        for c in range(4):
            t = proj[:, 128 * c : 128 * c + 128]
            qkv_ref[rows, 128 * c : 128 * c + 128] = (t * cos + partner_of(t, lane) * sin).astype(BF16)
        qkv_ref[rows, 512:] = proj[:, 512:].astype(BF16)


def project(info, xs, vs, ws, cos, sin):
    return call(
        project_kernel,
        "project",
        [SMEM] + [VMEM] * 8 + [ANY] * 4 + [VMEM] * 2,
        [shaped(D, D), shaped(D, 768), shaped(D, 768), shaped(8, D, dtype=F32)],
        (info, *xs, *vs, *ws, cos, sin),
        limit=20,
        scratch_shapes=[pltpu.VMEM((8, 3 * D), F32), pltpu.SemaphoreType.DMA((4,))],
    )


def two_heads(v):
    side = lax.broadcasted_iota(jnp.int32, v.shape, 1) // HEAD
    zero = jnp.zeros((), v.dtype)
    return jnp.concatenate([jnp.where(side == h, v, zero) for h in range(2)], axis=0)


def one_pair(vt):
    n = vt.shape[1] // 2
    return jnp.concatenate([vt[:HEAD, :n], vt[HEAD:, n:]], axis=0).T


def later_keys(keys, queries, first):
    return lax.broadcasted_iota(jnp.int32, (keys, 2 * queries), 0) > (
        lax.broadcasted_iota(jnp.int32, (keys, 2 * queries), 1) % queries + first
    )


def half_rows(slot, half):
    return pl.ds(pl.multiple_of(slot * ROWS + half * HALF, HALF), HALF)


def put_blocks(outs, value):
    for j, out in enumerate(outs):
        out[...] = value[HALF * j : HALF * j + HALF, :]


def attend_kernel(half, info, qkv_ref, w_ref, mixed_ref, lse_ref, *outs):
    own_keys = HALF * (half + 1)
    later = later_keys(own_keys, HALF, HALF * half)
    for pair in range(2):
        cols = [slice(256 * c + 128 * pair, 256 * c + 128 * pair + 128) for c in range(3)]
        for i in range(GROUP):
            slot = info[SLOT + i]
            q = two_heads(qkv_ref[half_rows(slot, half), cols[0]])
            there = [row_of(info[SLOT + n]) for n in range(i)]
            there.append(pl.ds(pl.multiple_of(slot * ROWS, ROWS), own_keys))
            tiles = [dot_nt(qkv_ref[at, cols[1]], q) for at in there]
            tiles[i] = jnp.where(later, -1e30, tiles[i])
            top = functools.reduce(jnp.maximum, [jnp.max(t, axis=0, keepdims=True) for t in tiles])
            top = top * SCALE2
            total = jnp.zeros((1, 2 * HALF), F32)
            out = jnp.zeros((128, 2 * HALF), F32)
            for at, tile in zip(there, tiles):
                p = jnp.exp2(tile * SCALE2 - top)
                total = total + jnp.sum(p, axis=0, keepdims=True)
                out = out + dot_tn(qkv_ref[at, cols[2]], p.astype(BF16))
            to = pl.ds(pl.multiple_of(slot * HALF, HALF), HALF)
            mixed_ref[to, 128 * pair : 128 * pair + 128] = one_pair(out / total).astype(BF16)
            lse = top + jnp.log2(total)
            for h in range(2):
                lse_ref[2 * pair + h : 2 * pair + h + 1, to] = lse[:, HALF * h : HALF * h + HALF]
    put_blocks(outs, dot(mixed_ref[...], w_ref[...]).astype(BF16))


def attend(half, info, qkv, w):
    return call(
        functools.partial(attend_kernel, half),
        "attend",
        [SMEM] + [VMEM] * 2,
        [shaped(4 * HALF, 256), shaped(4, 4 * HALF, dtype=F32)] + [shaped(HALF, D)] * 4,
        (info, qkv, w),
        limit=24,
    )


def attend_back_kernel(
    pair, info, qkv_ref, a0, a1, a2, a3, b0, b1, b2, b3, w_ref, lse0, lse1, cos_ref, sin_ref,
    out_ref, do_ref, dq_ref, dk_ref, dv_ref,
):
    cols = [slice(256 * c + 128 * pair, 256 * c + 128 * pair + 128) for c in range(3)]
    later = later_keys(ROWS, ROWS, 0)
    w = w_ref[128 * pair : 128 * pair + 128, :]
    for j, (a, b) in enumerate(((a0, b0), (a1, b1), (a2, b2), (a3, b3))):
        rows = jnp.concatenate([a[...], b[...]], axis=0)
        do_ref[ROWS * j : ROWS * j + ROWS, :] = dot_nt(rows, w).astype(BF16)
    dk_ref[...] = jnp.zeros_like(dk_ref)
    dv_ref[...] = jnp.zeros_like(dv_ref)
    for i in range(GROUP):
        rows = row_of(info[SLOT + i])
        q = two_heads(qkv_ref[rows, cols[0]])
        do = two_heads(do_ref[rows, :])
        to = pl.ds(pl.multiple_of(info[SLOT + i] * HALF, HALF), HALF)
        lse = jnp.concatenate(
            [ref[2 * pair + h : 2 * pair + h + 1, to] for h in range(2) for ref in (lse0, lse1)], axis=1
        )
        probs, grads = [], []
        delta = jnp.zeros((1, 2 * ROWS), F32)
        for n in range(i + 1):
            there = row_of(info[SLOT + n])
            p = jnp.exp2(dot_nt(qkv_ref[there, cols[1]], q) * SCALE2 - lse)
            if n == i:
                p = jnp.where(later, 0.0, p)
            dp = dot_nt(qkv_ref[there, cols[2]], do)
            delta = delta + jnp.sum(p * dp, axis=0, keepdims=True)
            dv_ref[there, :] += dot(p.astype(BF16), do)
            probs.append(p)
            grads.append(dp)
        dqt = jnp.zeros((128, 2 * ROWS), F32)
        for n in range(i + 1):
            there = row_of(info[SLOT + n])
            ds = (probs[n] * (grads[n] - delta)).astype(BF16)
            dk_ref[there, :] += dot(ds, q)
            dqt = dqt + dot_tn(qkv_ref[there, cols[1]], ds)
        dq_ref[rows, :] = one_pair(dqt)
    lane = lax.broadcasted_iota(jnp.int32, (D, 128), 1)
    scale = HEAD ** (-0.5)
    cos, sin = cos_ref[...], sin_ref[...]
    dq = dq_ref[...] * scale
    out_ref[:, :128] = (dq * cos - partner_of(dq, lane) * sin).astype(BF16)
    dk = dk_ref[...] * scale
    out_ref[:, 128:256] = (dk * cos - partner_of(dk, lane) * sin).astype(BF16)
    out_ref[:, 256:] = dv_ref[...].astype(BF16)


def attend_back(pair, info, qkv, branch, w, lse, cos, sin):
    return call(
        functools.partial(attend_back_kernel, pair),
        "attend_back",
        [SMEM] + [VMEM] * 14,
        shaped(D, 384),
        (info, qkv, *branch, w, *lse, cos, sin),
        us=20 * pair,
        limit=32,
        scratch_shapes=[pltpu.VMEM((D, 128), BF16)] + [pltpu.VMEM((D, 128), F32)] * 3,
    )


def whole(first, second):
    return jnp.concatenate(
        [v[:, 128 * c : 128 * c + 128] for c in range(3) for v in (first, second)], axis=1
    )


def hidden_back_kernel(d0, d1, w_ref, *outs):
    for half in range(2):
        rows = slice(512 * half, 512 * half + 512)
        part = dot_nt(whole(d0[rows, :], d1[rows, :]), w_ref[...]).astype(BF16)
        outs[2 * half][...] = part[:ROWS, :]
        outs[2 * half + 1][...] = part[ROWS:, :]


def hidden_back(dqkvs, w):
    return call(
        hidden_back_kernel,
        "hidden_back",
        [VMEM] * 3,
        [shaped(ROWS, D)] * 4,
        (*dqkvs, w),
        limit=24,
    )


def add_near_kernel(low_ref, got_ref, near_ref):
    near_ref[...] = add(low_ref[...], got_ref[...])


def scatter_group(blocks):
    own, near, sibling, both = blocks
    got_near = send(both, SIBLING)
    got_own = send(sibling, SIBLING)
    near = call(add_near_kernel, "add_near", [VMEM] * 2, shaped(ROWS, D), (near, got_near), limit=16)
    return (own, got_own), near


def scatter_half(blocks):
    own, near, sibling, both = blocks
    got_near = send(both, SIBLING)
    got_own = send(sibling, SIBLING)
    near = call(add_near_kernel, "add_half", [VMEM] * 2, shaped(HALF, D), (near, got_near), limit=16)
    return (own, got_own), near


def gather_group(own, keep=None):
    near = send(own, ZNEAR)
    return (own, near, send(own, SIBLING), send(near, SIBLING))


def total_of(*refs):
    return sum(ref[...].astype(F32) for ref in refs)


def half_total(low_ref, got_ref, other_ref):
    return total_of(low_ref.at[:HALF], got_ref.at[:HALF], other_ref)


def middle_kernel(half, x_ref, own_ref, got_ref, other_ref, norms_ref, mid_ref, hid_ref):
    mid = x_ref[HALF * half : HALF * half + HALF, :].astype(F32) + total_of(own_ref, got_ref, other_ref)
    mid_ref[...] = mid
    xhat, _ = stats_of(mid)
    hid_ref[...] = (xhat * norms_ref[2:3, :] + norms_ref[3:4, :]).astype(BF16)


def middle_of(half, x, own, other, norms):
    return call(
        functools.partial(middle_kernel, half),
        "middle",
        [VMEM] * 5,
        [shaped(HALF, D, dtype=F32), shaped(HALF, D)],
        (x, *own, other, norms),
        limit=16,
    )


def norm_back_of(e, x, gain):
    xhat, inv = stats_of(x)
    u = e * gain
    back = u - jnp.mean(u, axis=1, keepdims=True) - xhat * jnp.mean(u * xhat, axis=1, keepdims=True)
    return inv * back, xhat


def middle_back_kernel(
    half, own_ref, got_ref, other_ref, mid_ref, res_ref, norms_ref, out_ref, branch_ref, sums_ref
):
    e = total_of(own_ref, got_ref, other_ref)
    back, xhat = norm_back_of(e, mid_ref[...], norms_ref[2:3, :])
    out = res_ref[HALF * half : HALF * half + HALF, :].astype(F32) + back
    out_ref[...] = out
    branch_ref[...] = out.astype(BF16)
    sums_ref[0:1, :] = jnp.sum(e * xhat, axis=0, keepdims=True)
    sums_ref[1:2, :] = jnp.sum(e, axis=0, keepdims=True)


def middle_back(half, own, other, mid, res, norms, us):
    return call(
        functools.partial(middle_back_kernel, half),
        "middle_back",
        [VMEM] * 6,
        [shaped(HALF, D, dtype=F32), shaped(HALF, D), shaped(2, D, dtype=F32)],
        (*own, other, mid, res, norms),
        us=us,
        limit=16,
    )


def tokens_back_kernel(own_ref, got_ref, other_ref, x_ref, res0, res1, norms_ref, out_ref):
    e = total_of(own_ref, got_ref, other_ref)
    back, _ = norm_back_of(e, x_ref[...].astype(F32), norms_ref[0:1, :])
    out_ref[:HALF, :] = res0[...] + back[:HALF, :]
    out_ref[HALF:, :] = res1[...] + back[HALF:, :]


def tokens_back(own, other, x, res, norms):
    return call_far(
        tokens_back_kernel,
        "tokens_back",
        shaped(ROWS, D, dtype=F32),
        (*own, other, x, *res, norms),
        us=20,
        limit=16,
    )


def out_near_kernel(l0, g0, l1, g1, near_ref):
    near_ref[:HALF, :] = add(l0[HALF:, :], g0[HALF:, :])
    near_ref[HALF:, :] = add(l1[HALF:, :], g1[HALF:, :])


def out_near_of(lows, gots):
    return call_far(
        out_near_kernel,
        "out_near",
        shaped(ROWS, D),
        (lows[0], gots[0], lows[1], gots[1]),
        limit=16,
    )


def layer_out_kernel(m0, m1, l0, g0, l1, g1, other_ref, out_ref):
    for n, (m, low, got) in enumerate(((m0, l0, g0), (m1, l1, g1))):
        rows = slice(HALF * n, HALF * n + HALF)
        out_ref[rows, :] = (m[...] + half_total(low, got, other_ref.at[rows])).astype(BF16)


def layer_out_of(mids, lows, gots, other):
    return call_far(
        layer_out_kernel,
        "layer_out",
        shaped(ROWS, D),
        (*mids, lows[0], gots[0], lows[1], gots[1], other),
        limit=16,
    )


def feed_kernel(h_ref, g_ref, w_ref, down_ref, act_ref, dgu_ref, ghs, out_low, out_up):
    h, g = h_ref[...], g_ref[...]
    gate = dot(h, w_ref[:, :FFP])
    up = dot(h, w_ref[:, FFP:])
    sig = jax.nn.sigmoid(gate)
    silu = gate * sig
    act = (silu * up).astype(BF16)
    act_ref[...] = act
    grad_act = dot_nt(g, down_ref[...])
    dgate = (grad_act * up * (sig * (1.0 + gate * (1.0 - sig)))).astype(BF16)
    dup = (grad_act * silu).astype(BF16)
    dgu_ref[:, :FFP] = dgate
    dgu_ref[:, FFP:] = dup
    put_blocks(ghs, (dot_nt(dgate, w_ref[:, :FFP]) + dot_nt(dup, w_ref[:, FFP:])).astype(BF16))
    out = dot(act, down_ref[...]).astype(BF16)
    out_low[...] = out[:ROWS, :]
    out_up[...] = out[ROWS:, :]


def tokens_in(half, hs, gs, h_ref, g_ref, sems):
    copies = []
    for j in range(GROUP):
        rows = slice(HALF * j, HALF * j + HALF)
        copies.append(pltpu.make_async_copy(hs[j], h_ref.at[rows], sems.at[j]))
        half_g = gs[j].at[HALF * half : HALF * half + HALF]
        copies.append(pltpu.make_async_copy(half_g, g_ref.at[rows], sems.at[GROUP + j]))
    return copies


def feed_first_kernel(
    info, h0, h1, h2, h3, g0, g1, g2, g3, w0, w1, w2, w3, w4, d_ref,
    act_ref, dgu_ref, gh0, gh1, gh2, gh3, out_low, out_up, w_ref, down_ref, h_ref, g_ref, sems,
):
    copies = tokens_in(0, (h0, h1, h2, h3), (g0, g1, g2, g3), h_ref, g_ref, sems)
    for j, w in enumerate((w0, w1, w2)):
        copies.append(pltpu.make_async_copy(w, w_ref.at[row_of(info[ME] ^ j)], sems.at[8 + j]))
    for j, w in enumerate((w3, w4)):
        at = pl.ds(pl.multiple_of((info[ME] ^ 3) * ROWS + j * CUT, CUT), w.shape[0])
        copies.append(pltpu.make_async_copy(w, w_ref.at[at], sems.at[11 + j]))
    copies.append(pltpu.make_async_copy(d_ref, down_ref.at[:FFS], sems.at[13]))
    for copy in copies:
        copy.start()
    down_ref[FFS:, :] = jnp.zeros((FFP - FFS, D), BF16)
    for copy in copies:
        copy.wait()
    feed_kernel(h_ref, g_ref, w_ref, down_ref, act_ref, dgu_ref, (gh0, gh1, gh2, gh3), out_low, out_up)


def feed_second_kernel(
    info, h0, h1, h2, h3, g0, g1, g2, g3, w_ref, down_ref,
    act_ref, dgu_ref, gh0, gh1, gh2, gh3, out_low, out_up, h_ref, g_ref, sems,
):
    copies = tokens_in(1, (h0, h1, h2, h3), (g0, g1, g2, g3), h_ref, g_ref, sems)
    for copy in copies:
        copy.start()
    for copy in copies:
        copy.wait()
    feed_kernel(h_ref, g_ref, w_ref, down_ref, act_ref, dgu_ref, (gh0, gh1, gh2, gh3), out_low, out_up)


FEED_OUT = (
    [shaped(4 * HALF, FFP), shaped(4 * HALF, 2 * FFP)] + [shaped(HALF, D)] * 4 + [shaped(ROWS, D)] * 2
)
FEED_SCRATCH = [pltpu.VMEM((4 * HALF, D), BF16)] * 2


def feed_first(info, hs, gs, ws, down):
    return call(
        feed_first_kernel,
        "feed_first",
        [SMEM] + [ANY] * 14,
        FEED_OUT + [shaped(D, 2 * FFP), shaped(FFP, D)],
        (info, *hs, *gs, *ws, down),
        limit=28,
        scratch_shapes=FEED_SCRATCH + [pltpu.SemaphoreType.DMA((14,))],
    )


def feed_second(info, hs, gs, w, down):
    return call(
        feed_second_kernel,
        "feed_second",
        [SMEM] + [ANY] * 8 + [VMEM] * 2,
        FEED_OUT,
        (info, *hs, *gs, w, down),
        limit=28,
        scratch_shapes=FEED_SCRATCH + [pltpu.SemaphoreType.DMA((8,))],
    )


def own_order(info, piece):
    return jnp.where(info[ME] % 2 == 0, piece, ((piece & 3) << 2) | (piece >> 2))


def split_result(info, res_ref, outs):
    for part in range(2):
        mine = info[BIT + part]
        weight = 8 >> part
        for t in range(2):
            for n in range(8):
                low = n if part == 0 else (n & 3) | ((n & 4) << 1)
                to = slice(128 * t + 16 * n, 128 * t + 16 * n + 16)
                for out, bit in ((outs[2 * part], mine), (outs[2 * part + 1], 1 - mine)):
                    out[to, :] = res_ref[part, row_of(16 * t + own_order(info, low + weight * bit), 16), :]


def mlp_weights_kernel(
    info, h0, h1, h2, h3, h4, h5, h6, h7, g0, g1, g2, g3, dgu0, dgu1, act0, act1,
    k1, s1, k2, s2, h_ref, g_ref, res_ref, sems,
):
    step = pl.program_id(0)

    def copies(which):
        out = []
        for n in range(2 * GROUP):
            rows = slice(HALF * n, HALF * n + HALF)
            half, j = n // GROUP, n % GROUP
            if which == 0:
                out.append(pltpu.make_async_copy((h0, h1, h2, h3, h4, h5, h6, h7)[n], h_ref.at[rows], sems.at[n]))
            else:
                half_g = (g0, g1, g2, g3)[j].at[HALF * half : HALF * half + HALF]
                out.append(pltpu.make_async_copy(half_g, g_ref.at[rows], sems.at[8 + n]))
        return out

    @pl.when(step == 0)
    def _():
        hs = copies(0)
        for copy in hs + copies(1):
            copy.start()
        for copy in hs:
            copy.wait()

    @pl.when(step == 2)
    def _():
        for copy in copies(1):
            copy.wait()

    def product(left, right0, right1, cols):
        both = dot_tn(left[: 4 * HALF, cols], right0[...]) + dot_tn(left[4 * HALF :, cols], right1[...])
        return both.astype(BF16)

    for part in range(2):
        cols = slice(512 * part, 512 * part + 512)

        @pl.when(step < 2)
        def _():
            res_ref[part] = product(h_ref, dgu0, dgu1, cols)

        @pl.when(step == 2)
        def _():
            res_ref[part] = product(g_ref, act0, act1, cols)

    split_result(info, res_ref, (k1, s1, k2, s2))


def mlp_weights(info, hs, gs, dgus, acts):
    col = lambda i: (0, i)
    dgu = pl.BlockSpec((4 * HALF, FFP), lambda i: (0, jnp.minimum(i, 1)))
    act = pl.BlockSpec((4 * HALF, FFP), lambda i: (0, 0))
    return call(
        mlp_weights_kernel,
        "mlp_weights",
        [SMEM] + [ANY] * 12 + [dgu, dgu, act, act],
        [shaped(256, 3 * FFP)] * 4,
        (info, *hs, *gs, *dgus, *acts),
        limit=26,
        grid=(3,),
        out_specs=[pl.BlockSpec((256, FFP), col)] * 4,
        scratch_shapes=[
            pltpu.VMEM((D, D), BF16),
            pltpu.VMEM((D, D), BF16),
            pltpu.VMEM((2, 512, FFP), BF16),
            pltpu.SemaphoreType.DMA((16,)),
        ],
    )


EX = 128
ATT = 768 + EX + 256


def attn_weights_kernel(
    info, h_ref, d0, d1, w_ref, m0, m1, b0, b1, b2, b3, b4, b5, b6, b7, norms_ref, sm0, sm1,
    k1, s1, k2, s2, d_ref, b_ref, ex_ref, res_ref, sems,
):
    me = info[ME]
    copies = [
        pltpu.make_async_copy(r, b_ref.at[HALF * j : HALF * j + HALF], sems.at[j])
        for j, r in enumerate((b0, b1, b2, b3, b4, b5, b6, b7))
    ]
    for copy in copies:
        copy.start()
    d_ref[...] = whole(d0[...], d1[...])
    ex_ref[...] = jnp.zeros_like(ex_ref)
    ex_ref[0:2, :] = norms_ref[0:2, :]
    ex_ref[2:4, :] = sm0[...] + sm1[...]
    db = dot(jnp.ones((8, D), BF16), d_ref[...])[0:1, :]
    for c in range(3):
        one = db[:, 256 * c : 256 * c + 256]
        ex_ref[pl.ds(8 + 4 * c + me, 1), :] = jnp.concatenate([one] * GROUP, axis=1)
    ex = ex_ref[...].T
    lane = lax.broadcasted_iota(jnp.int32, (512, EX), 1)
    for half in range(2):
        rows = slice(512 * half, 512 * half + 512)
        dw = dot_tn(h_ref[:, rows], d_ref[...])
        res_ref[half, :, :768] = dw.astype(BF16)
        w = w_ref[rows, :].astype(F32)
        gain, shift = ex[rows, 0:1], ex[rows, 1:2]
        sum_e = jnp.sum(w * db, axis=1, keepdims=True)
        sum_xe = (jnp.sum(w * dw, axis=1, keepdims=True) - shift * sum_e) / gain
        cols = jnp.where(lane == 0, sum_xe, jnp.where(lane == 1, sum_e, ex[rows, :]))
        res_ref[half, :, 768 : 768 + EX] = cols.astype(BF16)
    for copy in copies:
        copy.wait()
    m = jnp.concatenate([m0[...], m1[...]], axis=0)
    for half in range(2):
        res_ref[half, :, 768 + EX :] = dot_tn(b_ref[:, 512 * half : 512 * half + 512], m).astype(BF16)
    split_result(info, res_ref, (k1, s1, k2, s2))


def attn_weights(info, hidden, dqkvs, w, mixed, branch, norms, sums_m):
    return call(
        attn_weights_kernel,
        "attn_weights",
        [SMEM] + [VMEM] * 6 + [ANY] * 8 + [VMEM] * 3,
        [shaped(256, ATT)] * 4,
        (info, hidden, *dqkvs, w, *mixed, *branch, norms, *sums_m),
        limit=30,
        scratch_shapes=[
            pltpu.VMEM((D, 768), BF16),
            pltpu.VMEM((D, D), BF16),
            pltpu.VMEM((EX, D), F32),
            pltpu.VMEM((2, 512, ATT), BF16),
            pltpu.SemaphoreType.DMA((8,)),
        ],
    )


def add(a, b):
    return (a.astype(F32) + b.astype(F32)).astype(BF16)


def halve_kernel(info, a1, g1, a2, g2, k1, s1, k2, s2):
    for part, (a, g, keep, away) in enumerate(((a1, g1, k1, s1), (a2, g2, k2, s2))):
        mine = info[BIT + SPLITS[part][1]]
        for t in range(2):
            to = slice(64 * t, 64 * t + 64)
            for out, bit in ((keep, mine), (away, 1 - mine)):
                at = row_of(2 * t + bit, 64)
                out[to, :] = add(a[at, :], g[at, :])


def quarter_kernel(info, a1, g1, a2, g2, *outs):
    mine = info[BIT + 2] * 2 + info[BIT + 3]
    for part, (a, g) in enumerate(((a1, g1), (a2, g2))):
        for t in range(2):
            to = slice(32 * part + 16 * t, 32 * part + 16 * t + 16)
            for flips, out in enumerate(outs):
                at = row_of(4 * t + (mine ^ flips), 16)
                out[to, :] = add(a[at, :], g[at, :])


def piece_kernel(a, g1, g2, g3, out):
    out[...] = total_of(a, g1, g2, g3).astype(BF16)


def share_kernel(cols, info, a_ref, g_ref, o0, o1, o2, o3, kept):
    width = a_ref.shape[1] - cols
    for j, out in enumerate((o0, o1, o2, o3)):
        rows = row_of(info[ME] ^ j, 16)
        out[...] = add(a_ref[rows, :cols], g_ref[rows, :cols])
    for t in range(GROUP):
        rows = slice(16 * t, 16 * t + 16)
        kept[:, width * t : width * t + width] = add(a_ref[rows, cols:], g_ref[rows, cols:])


def scatter_plane(info, first, name, gates, start=()):
    k1, s1, k2, s2 = first
    width = k1.shape[1]
    s1, s2 = after(s1, *start), after(s2, *start)
    for step, (kernel, shapes) in enumerate(
        ((halve_kernel, [shaped(128, width)] * 4), (quarter_kernel, [shaped(64, width)] * 4))
    ):
        got1 = send(s1, CUBE[SPLITS[0][step]])
        got2 = send(s2, CUBE[SPLITS[1][step]])
        outs = call(
            kernel,
            ("halve_", "quarter_")[step] + name,
            [SMEM] + [VMEM] * 4,
            shapes,
            (info, after(k1, *gates[step]()), got1, k2, got2),
            limit=24,
        )
        k1, s1, k2, s2 = outs
        yield k1
    keep, *away = outs
    got = [send(a, p) for a, p in zip(away, FOUR)]
    yield call(
        piece_kernel,
        "piece_" + name,
        [VMEM] * 4,
        shaped(64, width),
        (after(keep, *gates[2]()), *got),
        limit=24,
    )


def share(info, piece, cols, name, gate=()):
    width = piece.shape[1]
    *blocks, kept = call(
        functools.partial(share_kernel, cols),
        "share_" + name,
        [SMEM] + [VMEM] * 2,
        [shaped(16, cols)] * 4 + [shaped(16, GROUP * (width - cols))],
        (info, after(piece, *gate), send(piece, ZREPLICA)),
        us=20,
        limit=16,
    )
    perms = (None, SIBLING, ZNEAR, ZNEAR_SIBLING)
    return [b if p is None else send(b, p) for b, p in zip(blocks, perms)], kept


def join_mlp_kernel(info, r0, r1, r2, r3, kept, out):
    for j, r in enumerate((r0, r1, r2, r3)):
        s = info[ME] ^ j
        out[:, lanes_of(s * FFP, FFP)] = r[:, :FFP]
        out[:, lanes_of((GROUP + s) * FFP, FFP)] = r[:, FFP:]
    out[:, 2 * GROUP * FFP :] = kept[...]


def join_attn_kernel(info, r0, r1, r2, r3, kept, out):
    refs = (r0, r1, r2, r3)
    for j, r in enumerate(refs):
        s = info[ME] ^ j
        for c in range(3):
            out[:, lanes_of(c * D + s * 256, 256)] = r[:, 256 * c : 256 * c + 256]
    out[:, 3 * D : 3 * D + EX] = total_of(*(r.at[:, 768:] for r in refs)).astype(BF16)
    out[:, 3 * D + EX :] = kept[...]


def slots_of(info, piece):
    d = own_order(info, piece) ^ (info[BIT] * 8 + info[BIT + 1] * 4 + info[BIT + 2] * 2 + info[BIT + 3])
    return d, ((d >> 2) & 1) * 8 + ((d >> 3) & 1) * 4 + (d & 3)


def at_slot(own, got, slot):
    rows = row_of(slot & 7, 16)
    return jnp.where(slot >= 8, got[rows, :].astype(F32), own[rows, :].astype(F32))


def finish_mlp_kernel(info, a1, g1, a2, g2, gu_ref, down_ref, turn_ref):
    for piece in range(16):
        to = slice(16 * piece, 16 * piece + 16)
        one, two = slots_of(info, piece)
        v, u = at_slot(a1, g1, one), at_slot(a2, g2, two)
        for s in range(2 * GROUP):
            src, lo = (v, s * FFP) if s < 6 else (u, (s - 6) * FFP)
            gu_ref[to, FFS * s : FFS * s + FFS] = src[:, lo : lo + FFS]
        turn_ref[to, :] = u[:, 2 * FFP :]
    for t in range(GROUP):
        down_ref[:, 256 * t : 256 * t + 256] = turn_ref[:, FFP * t : FFP * t + FFP].T[:FFS, :]


def finish_attn_kernel(
    info, a1, g1, a2, g2, qkv_ref, out_ref, v0, v1, v2, v3, bias_ref, turn_ref, ex_ref, vec_ref
):
    for piece in range(16):
        to = slice(16 * piece, 16 * piece + 16)
        one, two = slots_of(info, piece)
        qkv_ref[to, : 2 * D] = at_slot(a1, g1, one)
        v = at_slot(a2, g2, two)
        qkv_ref[to, 2 * D :] = v[:, :D]
        ex_ref[to, :] = v[:, D : D + EX]
        turn_ref[to, :] = v[:, D + EX :]
    for t in range(GROUP):
        out_ref[:, 256 * t : 256 * t + 256] = turn_ref[:, 256 * t : 256 * t + 256].T
    vec_ref[...] = ex_ref[...].T
    for n, ref in enumerate((v0, v1, v2, v3)):
        ref[...] = vec_ref[n : n + 1, :].reshape(256)
    bias = [vec_ref[pl.ds(8 + 3 * info[ME] + n, 1), :] for n in range(3)]
    bias_ref[...] = jnp.concatenate(bias, axis=1).reshape(768)


def stack_four_kernel(own, g1, g2, g3, one, two):
    cut = one.shape[1]
    for n, ref in enumerate((own, g1, g2, g3)):
        rows = slice(16 * n, 16 * n + 16)
        one[rows, :] = ref[:, :cut]
        two[rows, :] = ref[:, cut:]


def stack_kernel(a1, g1, a2, g2, one, two):
    rows = a1.shape[0]
    for own, got, out in ((a1, g1, one), (a2, g2, two)):
        out[:rows, :] = own[...]
        out[rows:, :] = got[...]


def gather_plane(piece, cut, name, gates):
    width = piece.shape[1]
    got = [send(piece, p) for p in FOUR]
    yield got
    parts = call(
        stack_four_kernel,
        "stack_four_" + name,
        [VMEM] * 4,
        [shaped(64, cut), shaped(64, width - cut)],
        (after(piece, *gates[0]()), *got),
        limit=16,
    )
    for step in (1, 0):
        got = [send(p, CUBE[SPLITS[i][step]]) for i, p in enumerate(parts)]
        four = (parts[0], got[0], parts[1], got[1])
        if step == 0:
            yield four
            return
        yield got, parts[0]
        parts = call(
            stack_kernel,
            "stack_" + name,
            [VMEM] * 4,
            [shaped(2 * p.shape[0], p.shape[1]) for p in parts],
            (after(four[0], *gates[1]()), *four[1:]),
            us=20,
            limit=16,
        )


def after(value, *earlier):
    return lax.optimization_barrier((value, *earlier))[0]


def body(
    tokens,
    attn_norm_gain,
    attn_norm_shift,
    qkv_weight,
    qkv_bias,
    out_weight,
    mlp_norm_gain,
    mlp_norm_shift,
    gate_up_weight,
    down_weight,
    cotangent,
):
    me = lax.axis_index("fsdp")
    rank = lax.axis_index("dp")
    x, y = (rank // 4) % 4, rank % 4
    first = jnp.where(me % 2 == 0, x, y)
    second = jnp.where(me % 2 == 0, y, x)
    info = jnp.stack(
        [me]
        + [2 * ((n ^ me) % 2) + (n ^ me) // 2 for n in range(GROUP)]
        + [((first + 1) // 2) % 2, first // 2, ((second + 1) // 2) % 2, second // 2]
    ).astype(jnp.int32)
    near = send(tokens, ZNEAR)
    own_w, sibling_w, far_w = pick_qkv(info, qkv_weight)
    far_w = send(far_w, ZFAR)
    cos, sin = tables(info)
    gate_up_parts = pick_gate_up(info, after(gate_up_weight, own_w))
    vec = pack(
        attn_norm_gain, attn_norm_shift, mlp_norm_gain, mlp_norm_shift, after(qkv_bias, cos, gate_up_parts[0])
    )
    near_vec = send(vec, ZNEAR)
    near = after(near, near_vec)
    xs = (tokens, near, send(tokens, SIBLING), send(near, SIBLING))
    vs = (vec, near_vec, send(vec, SIBLING), send(near_vec, SIBLING))
    qkv_ws = (own_w, send(sibling_w, SIBLING), far_w, send(far_w[ROWS:], SIBLING))
    gs = gather_group(after(cotangent, near))
    gate_up_ws = [
        gate_up_parts[0],
        send(after(gate_up_parts[1], near), SIBLING),
        send(after(gate_up_parts[2], far_w, near_vec), ZFAR),
    ]

    hidden, qkv, qkv_w, norms = project(info, xs, vs, qkv_ws, cos, sin)
    gate_up_ws.append(send(after(gate_up_parts[3], gs[1]), ZNEAR_SIBLING))
    mixed0, lse0, *blocks0 = attend(0, info, qkv, out_weight)
    blocks0[3] = after(blocks0[3], *gate_up_ws[1:], gs[1])
    gate_up_ws.append(send(after(gate_up_parts[4], gate_up_ws[2], mixed0), ZFAR_SIBLING))
    own0, near0 = scatter_half(blocks0)
    mixed1, lse1, *blocks1 = attend(1, after(info, near0), qkv, out_weight)
    other0 = send(near0, ZNEAR)
    blocks1[1] = after(blocks1[1], other0)
    own1, near1 = scatter_half(blocks1)
    mixed, lse = (mixed0, mixed1), (lse0, lse1)
    mid0, hid0 = middle_of(0, tokens, own0, other0, norms)
    mid1, hid1 = middle_of(1, tokens, own1, send(near1, ZNEAR), norms)
    mids = (mid0, mid1)
    hs = [gather_group(hid0), gather_group(after(hid1, gate_up_ws[4]))]

    act0, dgu0, *blocks0, out_low0, out_up0, feed_w, down_w = feed_first(
        after(info, hid1), hs[0], gs, gate_up_ws, down_weight
    )
    own0, near0 = scatter_half(blocks0)
    act1, dgu1, *blocks1, out_low1, out_up1 = feed_second(after(info, near0), hs[1], gs, feed_w, down_w)
    other0 = send(near0, ZNEAR)
    blocks1[1] = after(blocks1[1], other0)
    own1, near1 = scatter_half(blocks1)
    grad_mid0, branch_own0, sums_m0 = middle_back(0, own0, other0, mids[0], cotangent, norms, 0)
    mlp_halves = mlp_weights(
        info, (*hs[0], *hs[1]), gs, (dgu0, after(dgu1, near1, branch_own0)), (act0, act1)
    )
    other1 = after(send(near1, ZNEAR), mlp_halves[0])
    grad_mid1, branch_own1, sums_m1 = middle_back(1, own1, other1, mids[1], cotangent, norms, 20)
    branch = (*gather_group(branch_own0), *gather_group(branch_own1))
    out_lows = (out_low0, out_low1)
    out_gots = [send(after(v, mlp_halves[0]), SIBLING) for v in (out_up0, out_up1)]
    o_near = out_near_of(out_lows, out_gots)

    ready = {}
    mlp_sums = scatter_plane(
        info,
        mlp_halves,
        "mlp",
        (lambda: (ready["dqkv0"],), lambda: (ready["dqkv1"], layer_out), lambda: (ready["halves"][0],)),
        (branch[2],),
    )
    o_other = send(after(o_near, branch[5]), ZNEAR)
    dqkv0 = attend_back(0, after(info, o_near), qkv, branch, out_weight, lse, cos, sin)
    ready["dqkv0"] = dqkv0
    mlp_sum0 = next(mlp_sums)
    layer_out = layer_out_of(mids, out_lows, out_gots, after(o_other, mlp_sum0))
    dqkv1 = attend_back(1, after(info, mlp_sum0), qkv, branch, out_weight, lse, cos, sin)
    ready["dqkv1"] = dqkv1
    mlp_sum1 = next(mlp_sums)
    dqkvs = (dqkv0, dqkv1)
    attn_halves = attn_weights(
        after(info, mlp_sum1), hidden, dqkvs, qkv_w, mixed, branch, norms, (sums_m0, sums_m1)
    )
    ready["halves"] = attn_halves
    mlp_piece = next(mlp_sums)
    ga_blocks = hidden_back((after(dqkv0, mlp_piece), dqkv1), qkv_w)
    ga_own, ga_near = scatter_group(ga_blocks)
    mlp_blocks, mlp_kept = share(info, mlp_piece, 2 * FFP, "mlp", (attn_halves[0],))
    mlp_joined = call(
        join_mlp_kernel,
        "join_mlp",
        [SMEM] + [VMEM] * 5,
        shaped(16, 3 * GROUP * FFP),
        (info, *mlp_blocks, mlp_kept),
        limit=16,
    )
    attn_sums = scatter_plane(
        info,
        attn_halves,
        "attn",
        (
            lambda: (mlp_blocks[0], ga_near),
            lambda: ready["got0"],
            lambda: (),
        ),
    )
    sum0 = next(attn_sums)
    mlp_all = gather_plane(mlp_joined, 6 * FFP, "mlp", (lambda: (sum1,), lambda: (attn_piece,)))
    ready["got0"] = next(mlp_all)
    sum1 = next(attn_sums)
    ready["got1"], _ = next(mlp_all)
    attn_piece = next(attn_sums)
    attn_blocks, attn_kept = share(info, attn_piece, 768 + EX, "attn")
    mlp_four = next(mlp_all)
    attn_joined = call(
        join_attn_kernel,
        "join_attn",
        [SMEM] + [VMEM] * 5,
        shaped(16, 4 * D + EX),
        (after(info, mlp_four[0]), *attn_blocks, attn_kept),
        limit=16,
    )
    attn_all = gather_plane(
        attn_joined, 2 * D, "attn", (lambda: (), lambda: (grad_down,))
    )
    next(attn_all)
    _, attn_stacked = next(attn_all)
    ga_other = send(after(ga_near, attn_stacked), ZNEAR)
    tokens_grad = tokens_back(ga_own, ga_other, tokens, (grad_mid0, grad_mid1), norms)

    grad_gate_up, grad_down = call(
        finish_mlp_kernel,
        "finish_mlp",
        [SMEM] + [VMEM] * 4,
        [shaped(ROWS, 2 * FF, dtype=F32), shaped(FFS, D, dtype=F32)],
        (info, *mlp_four),
        limit=30,
        scratch_shapes=[pltpu.VMEM((ROWS, GROUP * FFP), F32)],
    )
    attn_four = next(attn_all)
    grad_qkv, grad_out, *vectors, grad_bias = call(
        finish_attn_kernel,
        "finish_attn",
        [SMEM] + [VMEM] * 4,
        [shaped(ROWS, 3 * D, dtype=F32), shaped(256, D, dtype=F32)]
        + [shaped(256, dtype=F32)] * 4
        + [shaped(768, dtype=F32)],
        (after(info, tokens_grad), *attn_four),
        limit=24,
        scratch_shapes=[pltpu.VMEM((ROWS, D), F32), pltpu.VMEM((ROWS, EX), F32), pltpu.VMEM((EX, ROWS), F32)],
    )
    return (
        layer_out,
        tokens_grad,
        vectors[0],
        vectors[1],
        grad_qkv,
        grad_bias,
        grad_out,
        vectors[2],
        vectors[3],
        grad_gate_up,
        grad_down,
    )


def solution(mesh):
    rows = P(("dp", "fsdp"), None)
    vector = P("fsdp")
    matrix = P("fsdp", None)
    in_specs = (rows, vector, vector, matrix, vector, matrix, vector, vector, matrix, matrix, rows)
    out_specs = (rows, rows, vector, vector, matrix, vector, matrix, vector, vector, matrix, matrix)
    return jax.shard_map(body, mesh=mesh, in_specs=in_specs, out_specs=out_specs, check_vma=False)
```

```python
import functools
import math

import jax
import jax.numpy as jnp
from jax import lax
from jax.experimental import pallas as pl
from jax.experimental.pallas import tpu as pltpu
from jax.sharding import PartitionSpec as P

D = 1024
HEADS = 16
HEAD = 64
ROTARY = 16
FF = 2816
GROUP = 4
ROWS = 256
HALF = 128
FFS = FF // GROUP
FFP = 768
EPS = 1e-05
F32 = jnp.float32
BF16 = jnp.bfloat16
AXES = ("dp", "fsdp")
LOG2E = 1.0 / math.log(2.0)
SCALE2 = HEAD ** (-0.5) * LOG2E


def where_is(lin):
    return [(lin // 16) % 4, (lin // 4) % 4, (lin // 64) * 2 + (lin // 2) % 2, lin % 2]


def linear(x, y, z, core):
    return (((z // 2) * 4 + x) * 4 + y) * 4 + (z % 2) * 2 + core


def perm_of(move):
    return tuple((lin, linear(*move(*where_is(lin)))) for lin in range(128))


def flip(v, which):
    return v ^ 1 if which == 0 else 3 - v


SIBLING = perm_of(lambda x, y, z, c: (x, y, z, 1 - c))
ZNEAR = perm_of(lambda x, y, z, c: (x, y, z ^ 1, c))
ZFAR = perm_of(lambda x, y, z, c: (x, y, 3 - z, c))
ZFAR_SIBLING = perm_of(lambda x, y, z, c: (x, y, 3 - z, 1 - c))
ZNEAR_SIBLING = perm_of(lambda x, y, z, c: (x, y, z ^ 1, 1 - c))
ZREPLICA = perm_of(lambda x, y, z, c: (x, y, (z + 2) % 4, c))
def cube_move(bit):
    def move(x, y, z, c):
        on_x = (bit < 2) == (c == 0)
        return (flip(x, bit % 2), y, z, c) if on_x else (x, flip(y, bit % 2), z, c)

    return perm_of(move)


CUBE = tuple(cube_move(bit) for bit in range(4))
FOUR = (CUBE[3], CUBE[2], tuple((a, CUBE[3][b][1]) for a, b in CUBE[2]))


SPLITS = ((0, 1), (1, 0))
ME, SLOT, BIT = 0, 1, 5


def send(value, perm):
    return lax.ppermute(value, AXES, perm)


def dot(a, b):
    return lax.dot_general(a, b, (((1,), (0,)), ((), ())), preferred_element_type=F32)


def dot_nt(a, b):
    return lax.dot_general(a, b, (((1,), (1,)), ((), ())), preferred_element_type=F32)


def dot_tn(a, b):
    return lax.dot_general(a, b, (((0,), (0,)), ((), ())), preferred_element_type=F32)


def shaped(*shape, dtype=BF16):
    return jax.ShapeDtypeStruct(shape, dtype)


SMEM = pl.BlockSpec(memory_space=pltpu.SMEM)
ANY = pl.BlockSpec(memory_space=pl.ANY)
VMEM = pl.BlockSpec(memory_space=pltpu.VMEM)


def call(kernel, name, in_specs, out_shape, operands, *, us=0, limit=48, **kw):
    return pl.pallas_call(
        kernel,
        in_specs=in_specs,
        out_shape=out_shape,
        compiler_params=pltpu.CompilerParams(vmem_limit_bytes=limit << 20),
        cost_estimate=pl.CostEstimate(flops=us * 10**9, bytes_accessed=us << 20, transcendentals=0),
        name=name,
        **kw,
    )(*operands)


def call_far(kernel, name, out_shape, operands, **kw):
    n = len(operands)
    n_out = len(out_shape) if isinstance(out_shape, list) else 1

    def whole_kernel(*refs):
        ins, outs, held, sems = refs[:n], refs[n : n + n_out], refs[n + n_out : -1], refs[-1]
        copies = [pltpu.make_async_copy(r, h, sems.at[i]) for i, (r, h) in enumerate(zip(ins, held))]
        for copy in copies:
            copy.start()
        for copy in copies:
            copy.wait()
        kernel(*held, *outs)

    return call(
        whole_kernel,
        name,
        [ANY] * n,
        out_shape,
        operands,
        scratch_shapes=[pltpu.VMEM(v.shape, v.dtype) for v in operands] + [pltpu.SemaphoreType.DMA((n,))],
        **kw,
    )


def row_of(slot, rows=ROWS):
    return pl.ds(pl.multiple_of(slot * rows, rows), rows)


def lanes_of(start, width=128):
    return pl.ds(pl.multiple_of(start, 128), width)


def stats_of(x):
    cen = x - jnp.mean(x, axis=1, keepdims=True)
    inv = lax.rsqrt(jnp.mean(cen * cen, axis=1, keepdims=True) + EPS)
    return cen * inv, inv


def partner_of(t, lane):
    return jnp.where(lane % HEAD < ROTARY // 2, pltpu.roll(t, 120, 1), pltpu.roll(t, 8, 1))


def pack_kernel(a_ref, b_ref, c_ref, d_ref, bias_ref, out_ref):
    norms = [ref[...].reshape(1, 256).astype(F32) for ref in (a_ref, b_ref, c_ref, d_ref)]
    bias = [bias_ref[...].reshape(1, 768).astype(F32), jnp.zeros((1, 256), F32)]
    first = jnp.broadcast_to(jnp.concatenate(norms, axis=1), (16, D))
    second = jnp.broadcast_to(jnp.concatenate(bias, axis=1), (16, D))
    row = lax.broadcasted_iota(jnp.int32, (16, D), 0)
    out_ref[...] = jnp.where(row == 0, first, jnp.where(row == 1, second, 0.0)).astype(BF16)


def pack(*vectors):
    return call(pack_kernel, "pack", [VMEM] * 5, shaped(16, D), vectors, limit=16)


def tables_kernel(info, cos_ref, sin_ref):
    at = lax.broadcasted_iota(jnp.int32, (ROWS, 128), 1) % HEAD
    rate = jnp.exp((at % (ROTARY // 2)).astype(F32) * (-math.log(10000.0) / (ROTARY // 2)))
    row = lax.broadcasted_iota(jnp.int32, (ROWS, 128), 0)
    for j in range(GROUP):
        place = row + (info[ME] ^ (0, 2, 1, 3)[j]) * ROWS
        angle = place.astype(F32) * rate
        sin = jnp.where(at < ROTARY // 2, -jnp.sin(angle), jnp.sin(angle))
        rows = slice(ROWS * j, ROWS * j + ROWS)
        cos_ref[rows, :] = jnp.where(at < ROTARY, jnp.cos(angle), 1.0)
        sin_ref[rows, :] = jnp.where(at < ROTARY, sin, 0.0)


def tables(info):
    return call(tables_kernel, "tables", [SMEM], [shaped(D, 128, dtype=F32)] * 2, (info,), limit=16)


def pick_qkv_kernel(info, w_ref, own, sibling, far):
    for j in range(GROUP):
        d = info[ME] ^ j
        for c in range(3):
            cols = w_ref[:, lanes_of(c * D + d * 256, 256)]
            if j < 2:
                (own, sibling)[j][:, 256 * c : 256 * c + 256] = cols
            else:
                far[ROWS * (j - 2) : ROWS * (j - 1), 256 * c : 256 * c + 256] = cols


def pick_qkv(info, w):
    return call(
        pick_qkv_kernel,
        "pick_qkv",
        [SMEM, VMEM],
        [shaped(ROWS, 768), shaped(ROWS, 768), shaped(2 * ROWS, 768)],
        (info, w),
        limit=32,
    )


CUT = 64


def pick_gate_up_kernel(info, w_ref, *refs):
    outs, all_ref = refs[:5], refs[5]
    all_ref[...] = jnp.zeros_like(all_ref)
    for d in range(GROUP):
        all_ref[d, :, :FFS] = w_ref[:, FFS * d : FFS * d + FFS]
        all_ref[d, :, FFP : FFP + FFS] = w_ref[:, FF + FFS * d : FF + FFS * d + FFS]
    for j, out in enumerate(outs[:3]):
        out[...] = all_ref[info[ME] ^ j]
    outs[3][...] = all_ref[info[ME] ^ 3, :CUT, :]
    outs[4][...] = all_ref[info[ME] ^ 3, CUT:, :]


def pick_gate_up(info, w):
    return call(
        pick_gate_up_kernel,
        "pick_gate_up",
        [SMEM, VMEM],
        [shaped(rows, 2 * FFP) for rows in (ROWS, ROWS, ROWS, CUT, ROWS - CUT)],
        (info, w),
        limit=32,
        scratch_shapes=[pltpu.VMEM((GROUP, ROWS, 2 * FFP), BF16)],
    )


def project_kernel(
    info, x0, x1, x2, x3, v0, v1, v2, v3, w0, w1, w2, w3, cos_ref, sin_ref,
    hid_ref, qkv_ref, w_ref, norms_ref, bias_ref, sems,
):
    me = info[ME]
    copies = []
    for j, w in enumerate((w0, w1, w2, w3)):
        copy = pltpu.make_async_copy(w.at[:ROWS], w_ref.at[row_of(me ^ j)], sems.at[j])
        copy.start()
        copies.append(copy)
    for j, v in enumerate((v0, v1, v2, v3)):
        owner = me ^ (0, 2, 1, 3)[j]
        extra = v[...].astype(F32)
        for n in range(4):
            norms_ref[n : n + 1, lanes_of(owner * 256, 256)] = extra[0:1, 256 * n : 256 * n + 256]
        bias_ref[0:1, lanes_of(owner * 768, 768)] = extra[1:2, :768]
    gain, shift = norms_ref[0:1, :], norms_ref[1:2, :]
    bias = jnp.concatenate(
        [bias_ref[0:1, lanes_of(c * D + me * 256, 256)] for c in range(3)], axis=1
    )
    lane = lax.broadcasted_iota(jnp.int32, (ROWS, 128), 1)
    for j, x in enumerate((x0, x1, x2, x3)):
        rows = slice(ROWS * j, ROWS * j + ROWS)
        xhat, _ = stats_of(x[...].astype(F32))
        hid = (xhat * gain + shift).astype(BF16)
        hid_ref[rows, :] = hid
        if j == 0:
            for copy in copies:
                copy.wait()
        proj = dot(hid, w_ref[...]) + bias
        cos, sin = cos_ref[rows, :], sin_ref[rows, :]
        for c in range(4):
            t = proj[:, 128 * c : 128 * c + 128]
            qkv_ref[rows, 128 * c : 128 * c + 128] = (t * cos + partner_of(t, lane) * sin).astype(BF16)
        qkv_ref[rows, 512:] = proj[:, 512:].astype(BF16)


def project(info, xs, vs, ws, cos, sin):
    return call(
        project_kernel,
        "project",
        [SMEM] + [VMEM] * 8 + [ANY] * 4 + [VMEM] * 2,
        [shaped(D, D), shaped(D, 768), shaped(D, 768), shaped(8, D, dtype=F32)],
        (info, *xs, *vs, *ws, cos, sin),
        limit=20,
        scratch_shapes=[pltpu.VMEM((8, 3 * D), F32), pltpu.SemaphoreType.DMA((4,))],
    )


def two_heads(v):
    side = lax.broadcasted_iota(jnp.int32, v.shape, 1) // HEAD
    zero = jnp.zeros((), v.dtype)
    return jnp.concatenate([jnp.where(side == h, v, zero) for h in range(2)], axis=0)


def one_pair(vt):
    n = vt.shape[1] // 2
    return jnp.concatenate([vt[:HEAD, :n], vt[HEAD:, n:]], axis=0).T


def later_keys(keys, queries, first):
    return lax.broadcasted_iota(jnp.int32, (keys, 2 * queries), 0) > (
        lax.broadcasted_iota(jnp.int32, (keys, 2 * queries), 1) % queries + first
    )


def half_rows(slot, half):
    return pl.ds(pl.multiple_of(slot * ROWS + half * HALF, HALF), HALF)


def put_blocks(outs, value):
    for j, out in enumerate(outs):
        out[...] = value[HALF * j : HALF * j + HALF, :]


def attend_kernel(half, info, qkv_ref, w_ref, mixed_ref, lse_ref, *outs):
    own_keys = HALF * (half + 1)
    later = later_keys(own_keys, HALF, HALF * half)
    for pair in range(2):
        cols = [slice(256 * c + 128 * pair, 256 * c + 128 * pair + 128) for c in range(3)]
        for i in range(GROUP):
            slot = info[SLOT + i]
            q = two_heads(qkv_ref[half_rows(slot, half), cols[0]])
            there = [row_of(info[SLOT + n]) for n in range(i)]
            there.append(pl.ds(pl.multiple_of(slot * ROWS, ROWS), own_keys))
            tiles = [dot_nt(qkv_ref[at, cols[1]], q) for at in there]
            tiles[i] = jnp.where(later, -1e30, tiles[i])
            top = functools.reduce(jnp.maximum, [jnp.max(t, axis=0, keepdims=True) for t in tiles])
            top = top * SCALE2
            total = jnp.zeros((1, 2 * HALF), F32)
            out = jnp.zeros((128, 2 * HALF), F32)
            for at, tile in zip(there, tiles):
                p = jnp.exp2(tile * SCALE2 - top)
                total = total + jnp.sum(p, axis=0, keepdims=True)
                out = out + dot_tn(qkv_ref[at, cols[2]], p.astype(BF16))
            to = pl.ds(pl.multiple_of(slot * HALF, HALF), HALF)
            mixed_ref[to, 128 * pair : 128 * pair + 128] = one_pair(out / total).astype(BF16)
            lse = top + jnp.log2(total)
            for h in range(2):
                lse_ref[2 * pair + h : 2 * pair + h + 1, to] = lse[:, HALF * h : HALF * h + HALF]
    put_blocks(outs, dot(mixed_ref[...], w_ref[...]).astype(BF16))


def attend(half, info, qkv, w):
    return call(
        functools.partial(attend_kernel, half),
        "attend",
        [SMEM] + [VMEM] * 2,
        [shaped(4 * HALF, 256), shaped(4, 4 * HALF, dtype=F32)] + [shaped(HALF, D)] * 4,
        (info, qkv, w),
        limit=24,
    )


def attend_back_kernel(
    pair, info, qkv_ref, a0, a1, a2, a3, b0, b1, b2, b3, w_ref, lse0, lse1, cos_ref, sin_ref,
    out_ref, do_ref, dq_ref, dk_ref, dv_ref,
):
    cols = [slice(256 * c + 128 * pair, 256 * c + 128 * pair + 128) for c in range(3)]
    later = later_keys(ROWS, ROWS, 0)
    w = w_ref[128 * pair : 128 * pair + 128, :]
    for j, (a, b) in enumerate(((a0, b0), (a1, b1), (a2, b2), (a3, b3))):
        rows = jnp.concatenate([a[...], b[...]], axis=0)
        do_ref[ROWS * j : ROWS * j + ROWS, :] = dot_nt(rows, w).astype(BF16)
    dk_ref[...] = jnp.zeros_like(dk_ref)
    dv_ref[...] = jnp.zeros_like(dv_ref)
    for i in range(GROUP):
        rows = row_of(info[SLOT + i])
        q = two_heads(qkv_ref[rows, cols[0]])
        do = two_heads(do_ref[rows, :])
        to = pl.ds(pl.multiple_of(info[SLOT + i] * HALF, HALF), HALF)
        lse = jnp.concatenate(
            [ref[2 * pair + h : 2 * pair + h + 1, to] for h in range(2) for ref in (lse0, lse1)], axis=1
        )
        probs, grads = [], []
        delta = jnp.zeros((1, 2 * ROWS), F32)
        for n in range(i + 1):
            there = row_of(info[SLOT + n])
            p = jnp.exp2(dot_nt(qkv_ref[there, cols[1]], q) * SCALE2 - lse)
            if n == i:
                p = jnp.where(later, 0.0, p)
            dp = dot_nt(qkv_ref[there, cols[2]], do)
            delta = delta + jnp.sum(p * dp, axis=0, keepdims=True)
            dv_ref[there, :] += dot(p.astype(BF16), do)
            probs.append(p)
            grads.append(dp)
        dqt = jnp.zeros((128, 2 * ROWS), F32)
        for n in range(i + 1):
            there = row_of(info[SLOT + n])
            ds = (probs[n] * (grads[n] - delta)).astype(BF16)
            dk_ref[there, :] += dot(ds, q)
            dqt = dqt + dot_tn(qkv_ref[there, cols[1]], ds)
        dq_ref[rows, :] = one_pair(dqt)
    lane = lax.broadcasted_iota(jnp.int32, (D, 128), 1)
    scale = HEAD ** (-0.5)
    cos, sin = cos_ref[...], sin_ref[...]
    dq = dq_ref[...] * scale
    out_ref[:, :128] = (dq * cos - partner_of(dq, lane) * sin).astype(BF16)
    dk = dk_ref[...] * scale
    out_ref[:, 128:256] = (dk * cos - partner_of(dk, lane) * sin).astype(BF16)
    out_ref[:, 256:] = dv_ref[...].astype(BF16)


def attend_back(pair, info, qkv, branch, w, lse, cos, sin):
    return call(
        functools.partial(attend_back_kernel, pair),
        "attend_back",
        [SMEM] + [VMEM] * 14,
        shaped(D, 384),
        (info, qkv, *branch, w, *lse, cos, sin),
        us=20 * pair,
        limit=32,
        scratch_shapes=[pltpu.VMEM((D, 128), BF16)] + [pltpu.VMEM((D, 128), F32)] * 3,
    )


def whole(first, second):
    return jnp.concatenate(
        [v[:, 128 * c : 128 * c + 128] for c in range(3) for v in (first, second)], axis=1
    )


def hidden_back_kernel(d0, d1, w_ref, *outs):
    for half in range(2):
        rows = slice(512 * half, 512 * half + 512)
        part = dot_nt(whole(d0[rows, :], d1[rows, :]), w_ref[...]).astype(BF16)
        outs[2 * half][...] = part[:ROWS, :]
        outs[2 * half + 1][...] = part[ROWS:, :]


def hidden_back(dqkvs, w):
    return call(
        hidden_back_kernel,
        "hidden_back",
        [VMEM] * 3,
        [shaped(ROWS, D)] * 4,
        (*dqkvs, w),
        limit=24,
    )


def add_near_kernel(low_ref, got_ref, near_ref):
    near_ref[...] = add(low_ref[...], got_ref[...])


def scatter_group(blocks):
    own, near, sibling, both = blocks
    got_near = send(both, SIBLING)
    got_own = send(sibling, SIBLING)
    near = call(add_near_kernel, "add_near", [VMEM] * 2, shaped(ROWS, D), (near, got_near), limit=16)
    return (own, got_own), near


def scatter_half(blocks):
    own, near, sibling, both = blocks
    got_near = send(both, SIBLING)
    got_own = send(sibling, SIBLING)
    near = call(add_near_kernel, "add_half", [VMEM] * 2, shaped(HALF, D), (near, got_near), limit=16)
    return (own, got_own), near


def gather_group(own, keep=None):
    near = send(own, ZNEAR)
    return (own, near, send(own, SIBLING), send(near, SIBLING))


def total_of(*refs):
    return sum(ref[...].astype(F32) for ref in refs)


def half_total(low_ref, got_ref, other_ref):
    return total_of(low_ref.at[:HALF], got_ref.at[:HALF], other_ref)


def middle_kernel(half, x_ref, own_ref, got_ref, other_ref, norms_ref, mid_ref, hid_ref):
    mid = x_ref[HALF * half : HALF * half + HALF, :].astype(F32) + total_of(own_ref, got_ref, other_ref)
    mid_ref[...] = mid
    xhat, _ = stats_of(mid)
    hid_ref[...] = (xhat * norms_ref[2:3, :] + norms_ref[3:4, :]).astype(BF16)


def middle_of(half, x, own, other, norms):
    return call(
        functools.partial(middle_kernel, half),
        "middle",
        [VMEM] * 5,
        [shaped(HALF, D, dtype=F32), shaped(HALF, D)],
        (x, *own, other, norms),
        limit=16,
    )


def norm_back_of(e, x, gain):
    xhat, inv = stats_of(x)
    u = e * gain
    back = u - jnp.mean(u, axis=1, keepdims=True) - xhat * jnp.mean(u * xhat, axis=1, keepdims=True)
    return inv * back, xhat


def middle_back_kernel(
    half, own_ref, got_ref, other_ref, mid_ref, res_ref, norms_ref, out_ref, branch_ref, sums_ref
):
    e = total_of(own_ref, got_ref, other_ref)
    back, xhat = norm_back_of(e, mid_ref[...], norms_ref[2:3, :])
    out = res_ref[HALF * half : HALF * half + HALF, :].astype(F32) + back
    out_ref[...] = out
    branch_ref[...] = out.astype(BF16)
    sums_ref[0:1, :] = jnp.sum(e * xhat, axis=0, keepdims=True)
    sums_ref[1:2, :] = jnp.sum(e, axis=0, keepdims=True)


def middle_back(half, own, other, mid, res, norms, us):
    return call(
        functools.partial(middle_back_kernel, half),
        "middle_back",
        [VMEM] * 6,
        [shaped(HALF, D, dtype=F32), shaped(HALF, D), shaped(2, D, dtype=F32)],
        (*own, other, mid, res, norms),
        us=us,
        limit=16,
    )


def tokens_back_kernel(own_ref, got_ref, other_ref, x_ref, res0, res1, norms_ref, out_ref):
    e = total_of(own_ref, got_ref, other_ref)
    back, _ = norm_back_of(e, x_ref[...].astype(F32), norms_ref[0:1, :])
    out_ref[:HALF, :] = res0[...] + back[:HALF, :]
    out_ref[HALF:, :] = res1[...] + back[HALF:, :]


def tokens_back(own, other, x, res, norms):
    return call_far(
        tokens_back_kernel,
        "tokens_back",
        shaped(ROWS, D, dtype=F32),
        (*own, other, x, *res, norms),
        us=20,
        limit=16,
    )


def out_near_kernel(l0, g0, l1, g1, near_ref):
    near_ref[:HALF, :] = add(l0[HALF:, :], g0[HALF:, :])
    near_ref[HALF:, :] = add(l1[HALF:, :], g1[HALF:, :])


def out_near_of(lows, gots):
    return call_far(
        out_near_kernel,
        "out_near",
        shaped(ROWS, D),
        (lows[0], gots[0], lows[1], gots[1]),
        limit=16,
    )


def layer_out_kernel(m0, m1, l0, g0, l1, g1, other_ref, out_ref):
    for n, (m, low, got) in enumerate(((m0, l0, g0), (m1, l1, g1))):
        rows = slice(HALF * n, HALF * n + HALF)
        out_ref[rows, :] = (m[...] + half_total(low, got, other_ref.at[rows])).astype(BF16)


def layer_out_of(mids, lows, gots, other):
    return call_far(
        layer_out_kernel,
        "layer_out",
        shaped(ROWS, D),
        (*mids, lows[0], gots[0], lows[1], gots[1], other),
        limit=16,
    )


def feed_kernel(h_ref, g_ref, w_ref, down_ref, act_ref, dgu_ref, ghs, out_low, out_up):
    h, g = h_ref[...], g_ref[...]
    gate = dot(h, w_ref[:, :FFP])
    up = dot(h, w_ref[:, FFP:])
    sig = jax.nn.sigmoid(gate)
    silu = gate * sig
    act = (silu * up).astype(BF16)
    act_ref[...] = act
    grad_act = dot_nt(g, down_ref[...])
    dgate = (grad_act * up * (sig * (1.0 + gate * (1.0 - sig)))).astype(BF16)
    dup = (grad_act * silu).astype(BF16)
    dgu_ref[:, :FFP] = dgate
    dgu_ref[:, FFP:] = dup
    put_blocks(ghs, (dot_nt(dgate, w_ref[:, :FFP]) + dot_nt(dup, w_ref[:, FFP:])).astype(BF16))
    out = dot(act, down_ref[...]).astype(BF16)
    out_low[...] = out[:ROWS, :]
    out_up[...] = out[ROWS:, :]


def tokens_in(half, hs, gs, h_ref, g_ref, sems):
    copies = []
    for j in range(GROUP):
        rows = slice(HALF * j, HALF * j + HALF)
        copies.append(pltpu.make_async_copy(hs[j], h_ref.at[rows], sems.at[j]))
        half_g = gs[j].at[HALF * half : HALF * half + HALF]
        copies.append(pltpu.make_async_copy(half_g, g_ref.at[rows], sems.at[GROUP + j]))
    return copies


def feed_first_kernel(
    info, h0, h1, h2, h3, g0, g1, g2, g3, w0, w1, w2, w3, w4, d_ref,
    act_ref, dgu_ref, gh0, gh1, gh2, gh3, out_low, out_up, w_ref, down_ref, h_ref, g_ref, sems,
):
    copies = tokens_in(0, (h0, h1, h2, h3), (g0, g1, g2, g3), h_ref, g_ref, sems)
    for j, w in enumerate((w0, w1, w2)):
        copies.append(pltpu.make_async_copy(w, w_ref.at[row_of(info[ME] ^ j)], sems.at[8 + j]))
    for j, w in enumerate((w3, w4)):
        at = pl.ds(pl.multiple_of((info[ME] ^ 3) * ROWS + j * CUT, CUT), w.shape[0])
        copies.append(pltpu.make_async_copy(w, w_ref.at[at], sems.at[11 + j]))
    copies.append(pltpu.make_async_copy(d_ref, down_ref.at[:FFS], sems.at[13]))
    for copy in copies:
        copy.start()
    down_ref[FFS:, :] = jnp.zeros((FFP - FFS, D), BF16)
    for copy in copies:
        copy.wait()
    feed_kernel(h_ref, g_ref, w_ref, down_ref, act_ref, dgu_ref, (gh0, gh1, gh2, gh3), out_low, out_up)


def feed_second_kernel(
    info, h0, h1, h2, h3, g0, g1, g2, g3, w_ref, down_ref,
    act_ref, dgu_ref, gh0, gh1, gh2, gh3, out_low, out_up, h_ref, g_ref, sems,
):
    copies = tokens_in(1, (h0, h1, h2, h3), (g0, g1, g2, g3), h_ref, g_ref, sems)
    for copy in copies:
        copy.start()
    for copy in copies:
        copy.wait()
    feed_kernel(h_ref, g_ref, w_ref, down_ref, act_ref, dgu_ref, (gh0, gh1, gh2, gh3), out_low, out_up)


FEED_OUT = (
    [shaped(4 * HALF, FFP), shaped(4 * HALF, 2 * FFP)] + [shaped(HALF, D)] * 4 + [shaped(ROWS, D)] * 2
)
FEED_SCRATCH = [pltpu.VMEM((4 * HALF, D), BF16)] * 2


def feed_first(info, hs, gs, ws, down):
    return call(
        feed_first_kernel,
        "feed_first",
        [SMEM] + [ANY] * 14,
        FEED_OUT + [shaped(D, 2 * FFP), shaped(FFP, D)],
        (info, *hs, *gs, *ws, down),
        limit=28,
        scratch_shapes=FEED_SCRATCH + [pltpu.SemaphoreType.DMA((14,))],
    )


def feed_second(info, hs, gs, w, down):
    return call(
        feed_second_kernel,
        "feed_second",
        [SMEM] + [ANY] * 8 + [VMEM] * 2,
        FEED_OUT,
        (info, *hs, *gs, w, down),
        limit=28,
        scratch_shapes=FEED_SCRATCH + [pltpu.SemaphoreType.DMA((8,))],
    )


def own_order(info, piece):
    return jnp.where(info[ME] % 2 == 0, piece, ((piece & 3) << 2) | (piece >> 2))


def split_result(info, res_ref, outs):
    for part in range(2):
        mine = info[BIT + part]
        weight = 8 >> part
        for t in range(2):
            for n in range(8):
                low = n if part == 0 else (n & 3) | ((n & 4) << 1)
                to = slice(128 * t + 16 * n, 128 * t + 16 * n + 16)
                for out, bit in ((outs[2 * part], mine), (outs[2 * part + 1], 1 - mine)):
                    out[to, :] = res_ref[part, row_of(16 * t + own_order(info, low + weight * bit), 16), :]


def mlp_weights_kernel(
    info, h0, h1, h2, h3, h4, h5, h6, h7, g0, g1, g2, g3, dgu0, dgu1, act0, act1,
    k1, s1, k2, s2, h_ref, g_ref, res_ref, sems,
):
    step = pl.program_id(0)

    def copies(which):
        out = []
        for n in range(2 * GROUP):
            rows = slice(HALF * n, HALF * n + HALF)
            half, j = n // GROUP, n % GROUP
            if which == 0:
                out.append(pltpu.make_async_copy((h0, h1, h2, h3, h4, h5, h6, h7)[n], h_ref.at[rows], sems.at[n]))
            else:
                half_g = (g0, g1, g2, g3)[j].at[HALF * half : HALF * half + HALF]
                out.append(pltpu.make_async_copy(half_g, g_ref.at[rows], sems.at[8 + n]))
        return out

    @pl.when(step == 0)
    def _():
        hs = copies(0)
        for copy in hs + copies(1):
            copy.start()
        for copy in hs:
            copy.wait()

    @pl.when(step == 2)
    def _():
        for copy in copies(1):
            copy.wait()

    def product(left, right0, right1, cols):
        both = dot_tn(left[: 4 * HALF, cols], right0[...]) + dot_tn(left[4 * HALF :, cols], right1[...])
        return both.astype(BF16)

    for part in range(2):
        cols = slice(512 * part, 512 * part + 512)

        @pl.when(step < 2)
        def _():
            res_ref[part] = product(h_ref, dgu0, dgu1, cols)

        @pl.when(step == 2)
        def _():
            res_ref[part] = product(g_ref, act0, act1, cols)

    split_result(info, res_ref, (k1, s1, k2, s2))


def mlp_weights(info, hs, gs, dgus, acts):
    col = lambda i: (0, i)
    dgu = pl.BlockSpec((4 * HALF, FFP), lambda i: (0, jnp.minimum(i, 1)))
    act = pl.BlockSpec((4 * HALF, FFP), lambda i: (0, 0))
    return call(
        mlp_weights_kernel,
        "mlp_weights",
        [SMEM] + [ANY] * 12 + [dgu, dgu, act, act],
        [shaped(256, 3 * FFP)] * 4,
        (info, *hs, *gs, *dgus, *acts),
        limit=26,
        grid=(3,),
        out_specs=[pl.BlockSpec((256, FFP), col)] * 4,
        scratch_shapes=[
            pltpu.VMEM((D, D), BF16),
            pltpu.VMEM((D, D), BF16),
            pltpu.VMEM((2, 512, FFP), BF16),
            pltpu.SemaphoreType.DMA((16,)),
        ],
    )


EX = 128
ATT = 768 + EX + 256


def attn_weights_kernel(
    info, h_ref, d0, d1, w_ref, m0, m1, b0, b1, b2, b3, b4, b5, b6, b7, norms_ref, sm0, sm1,
    k1, s1, k2, s2, d_ref, b_ref, ex_ref, res_ref, sems,
):
    me = info[ME]
    copies = [
        pltpu.make_async_copy(r, b_ref.at[HALF * j : HALF * j + HALF], sems.at[j])
        for j, r in enumerate((b0, b1, b2, b3, b4, b5, b6, b7))
    ]
    for copy in copies:
        copy.start()
    d_ref[...] = whole(d0[...], d1[...])
    ex_ref[...] = jnp.zeros_like(ex_ref)
    ex_ref[0:2, :] = norms_ref[0:2, :]
    ex_ref[2:4, :] = sm0[...] + sm1[...]
    db = dot(jnp.ones((8, D), BF16), d_ref[...])[0:1, :]
    for c in range(3):
        one = db[:, 256 * c : 256 * c + 256]
        ex_ref[pl.ds(8 + 4 * c + me, 1), :] = jnp.concatenate([one] * GROUP, axis=1)
    ex = ex_ref[...].T
    lane = lax.broadcasted_iota(jnp.int32, (512, EX), 1)
    for half in range(2):
        rows = slice(512 * half, 512 * half + 512)
        dw = dot_tn(h_ref[:, rows], d_ref[...])
        res_ref[half, :, :768] = dw.astype(BF16)
        w = w_ref[rows, :].astype(F32)
        gain, shift = ex[rows, 0:1], ex[rows, 1:2]
        sum_e = jnp.sum(w * db, axis=1, keepdims=True)
        sum_xe = (jnp.sum(w * dw, axis=1, keepdims=True) - shift * sum_e) / gain
        cols = jnp.where(lane == 0, sum_xe, jnp.where(lane == 1, sum_e, ex[rows, :]))
        res_ref[half, :, 768 : 768 + EX] = cols.astype(BF16)
    for copy in copies:
        copy.wait()
    m = jnp.concatenate([m0[...], m1[...]], axis=0)
    for half in range(2):
        res_ref[half, :, 768 + EX :] = dot_tn(b_ref[:, 512 * half : 512 * half + 512], m).astype(BF16)
    split_result(info, res_ref, (k1, s1, k2, s2))


def attn_weights(info, hidden, dqkvs, w, mixed, branch, norms, sums_m):
    return call(
        attn_weights_kernel,
        "attn_weights",
        [SMEM] + [VMEM] * 6 + [ANY] * 8 + [VMEM] * 3,
        [shaped(256, ATT)] * 4,
        (info, hidden, *dqkvs, w, *mixed, *branch, norms, *sums_m),
        limit=30,
        scratch_shapes=[
            pltpu.VMEM((D, 768), BF16),
            pltpu.VMEM((D, D), BF16),
            pltpu.VMEM((EX, D), F32),
            pltpu.VMEM((2, 512, ATT), BF16),
            pltpu.SemaphoreType.DMA((8,)),
        ],
    )


def add(a, b):
    return (a.astype(F32) + b.astype(F32)).astype(BF16)


def halve_kernel(info, a1, g1, a2, g2, k1, s1, k2, s2):
    for part, (a, g, keep, away) in enumerate(((a1, g1, k1, s1), (a2, g2, k2, s2))):
        mine = info[BIT + SPLITS[part][1]]
        for t in range(2):
            to = slice(64 * t, 64 * t + 64)
            for out, bit in ((keep, mine), (away, 1 - mine)):
                at = row_of(2 * t + bit, 64)
                out[to, :] = add(a[at, :], g[at, :])


def quarter_kernel(info, a1, g1, a2, g2, *outs):
    mine = info[BIT + 2] * 2 + info[BIT + 3]
    for part, (a, g) in enumerate(((a1, g1), (a2, g2))):
        for t in range(2):
            to = slice(32 * part + 16 * t, 32 * part + 16 * t + 16)
            for flips, out in enumerate(outs):
                at = row_of(4 * t + (mine ^ flips), 16)
                out[to, :] = add(a[at, :], g[at, :])


def piece_kernel(a, g1, g2, g3, out):
    out[...] = total_of(a, g1, g2, g3).astype(BF16)


def share_kernel(cols, info, a_ref, g_ref, o0, o1, o2, o3, kept):
    width = a_ref.shape[1] - cols
    for j, out in enumerate((o0, o1, o2, o3)):
        rows = row_of(info[ME] ^ j, 16)
        out[...] = add(a_ref[rows, :cols], g_ref[rows, :cols])
    for t in range(GROUP):
        rows = slice(16 * t, 16 * t + 16)
        kept[:, width * t : width * t + width] = add(a_ref[rows, cols:], g_ref[rows, cols:])


def scatter_plane(info, first, name, gates, start=()):
    k1, s1, k2, s2 = first
    width = k1.shape[1]
    s1, s2 = after(s1, *start), after(s2, *start)
    for step, (kernel, shapes) in enumerate(
        ((halve_kernel, [shaped(128, width)] * 4), (quarter_kernel, [shaped(64, width)] * 4))
    ):
        got1 = send(s1, CUBE[SPLITS[0][step]])
        got2 = send(s2, CUBE[SPLITS[1][step]])
        outs = call(
            kernel,
            ("halve_", "quarter_")[step] + name,
            [SMEM] + [VMEM] * 4,
            shapes,
            (info, after(k1, *gates[step]()), got1, k2, got2),
            limit=24,
        )
        k1, s1, k2, s2 = outs
        yield k1
    keep, *away = outs
    got = [send(a, p) for a, p in zip(away, FOUR)]
    yield call(
        piece_kernel,
        "piece_" + name,
        [VMEM] * 4,
        shaped(64, width),
        (after(keep, *gates[2]()), *got),
        limit=24,
    )


def share(info, piece, cols, name, gate=()):
    width = piece.shape[1]
    *blocks, kept = call(
        functools.partial(share_kernel, cols),
        "share_" + name,
        [SMEM] + [VMEM] * 2,
        [shaped(16, cols)] * 4 + [shaped(16, GROUP * (width - cols))],
        (info, after(piece, *gate), send(piece, ZREPLICA)),
        us=20,
        limit=16,
    )
    perms = (None, SIBLING, ZNEAR, ZNEAR_SIBLING)
    return [b if p is None else send(b, p) for b, p in zip(blocks, perms)], kept


def join_mlp_kernel(info, r0, r1, r2, r3, kept, out):
    for j, r in enumerate((r0, r1, r2, r3)):
        s = info[ME] ^ j
        out[:, lanes_of(s * FFP, FFP)] = r[:, :FFP]
        out[:, lanes_of((GROUP + s) * FFP, FFP)] = r[:, FFP:]
    out[:, 2 * GROUP * FFP :] = kept[...]


def join_attn_kernel(info, r0, r1, r2, r3, kept, out):
    refs = (r0, r1, r2, r3)
    for j, r in enumerate(refs):
        s = info[ME] ^ j
        for c in range(3):
            out[:, lanes_of(c * D + s * 256, 256)] = r[:, 256 * c : 256 * c + 256]
    out[:, 3 * D : 3 * D + EX] = total_of(*(r.at[:, 768:] for r in refs)).astype(BF16)
    out[:, 3 * D + EX :] = kept[...]


def slots_of(info, piece):
    d = own_order(info, piece) ^ (info[BIT] * 8 + info[BIT + 1] * 4 + info[BIT + 2] * 2 + info[BIT + 3])
    return d, ((d >> 2) & 1) * 8 + ((d >> 3) & 1) * 4 + (d & 3)


def at_slot(own, got, slot):
    rows = row_of(slot & 7, 16)
    return jnp.where(slot >= 8, got[rows, :].astype(F32), own[rows, :].astype(F32))


def finish_mlp_kernel(info, a1, g1, a2, g2, gu_ref, down_ref, turn_ref):
    for piece in range(16):
        to = slice(16 * piece, 16 * piece + 16)
        one, two = slots_of(info, piece)
        v, u = at_slot(a1, g1, one), at_slot(a2, g2, two)
        for s in range(2 * GROUP):
            src, lo = (v, s * FFP) if s < 6 else (u, (s - 6) * FFP)
            gu_ref[to, FFS * s : FFS * s + FFS] = src[:, lo : lo + FFS]
        turn_ref[to, :] = u[:, 2 * FFP :]
    for t in range(GROUP):
        down_ref[:, 256 * t : 256 * t + 256] = turn_ref[:, FFP * t : FFP * t + FFP].T[:FFS, :]


def finish_attn_kernel(
    info, a1, g1, a2, g2, qkv_ref, out_ref, v0, v1, v2, v3, bias_ref, turn_ref, ex_ref, vec_ref
):
    for piece in range(16):
        to = slice(16 * piece, 16 * piece + 16)
        one, two = slots_of(info, piece)
        qkv_ref[to, : 2 * D] = at_slot(a1, g1, one)
        v = at_slot(a2, g2, two)
        qkv_ref[to, 2 * D :] = v[:, :D]
        ex_ref[to, :] = v[:, D : D + EX]
        turn_ref[to, :] = v[:, D + EX :]
    for t in range(GROUP):
        out_ref[:, 256 * t : 256 * t + 256] = turn_ref[:, 256 * t : 256 * t + 256].T
    vec_ref[...] = ex_ref[...].T
    for n, ref in enumerate((v0, v1, v2, v3)):
        ref[...] = vec_ref[n : n + 1, :].reshape(256)
    bias = [vec_ref[pl.ds(8 + 3 * info[ME] + n, 1), :] for n in range(3)]
    bias_ref[...] = jnp.concatenate(bias, axis=1).reshape(768)


def stack_four_kernel(own, g1, g2, g3, one, two):
    cut = one.shape[1]
    for n, ref in enumerate((own, g1, g2, g3)):
        rows = slice(16 * n, 16 * n + 16)
        one[rows, :] = ref[:, :cut]
        two[rows, :] = ref[:, cut:]


def stack_kernel(a1, g1, a2, g2, one, two):
    rows = a1.shape[0]
    for own, got, out in ((a1, g1, one), (a2, g2, two)):
        out[:rows, :] = own[...]
        out[rows:, :] = got[...]


def gather_plane(piece, cut, name, gates):
    width = piece.shape[1]
    got = [send(piece, p) for p in FOUR]
    yield got
    parts = call(
        stack_four_kernel,
        "stack_four_" + name,
        [VMEM] * 4,
        [shaped(64, cut), shaped(64, width - cut)],
        (after(piece, *gates[0]()), *got),
        limit=16,
    )
    for step in (1, 0):
        got = [send(p, CUBE[SPLITS[i][step]]) for i, p in enumerate(parts)]
        four = (parts[0], got[0], parts[1], got[1])
        if step == 0:
            yield four
            return
        yield got, parts[0]
        parts = call(
            stack_kernel,
            "stack_" + name,
            [VMEM] * 4,
            [shaped(2 * p.shape[0], p.shape[1]) for p in parts],
            (after(four[0], *gates[1]()), *four[1:]),
            us=20,
            limit=16,
        )


def after(value, *earlier):
    return lax.optimization_barrier((value, *earlier))[0]


def body(
    tokens,
    attn_norm_gain,
    attn_norm_shift,
    qkv_weight,
    qkv_bias,
    out_weight,
    mlp_norm_gain,
    mlp_norm_shift,
    gate_up_weight,
    down_weight,
    cotangent,
):
    me = lax.axis_index("fsdp")
    rank = lax.axis_index("dp")
    x, y = (rank // 4) % 4, rank % 4
    first = jnp.where(me % 2 == 0, x, y)
    second = jnp.where(me % 2 == 0, y, x)
    info = jnp.stack(
        [me]
        + [2 * ((n ^ me) % 2) + (n ^ me) // 2 for n in range(GROUP)]
        + [((first + 1) // 2) % 2, first // 2, ((second + 1) // 2) % 2, second // 2]
    ).astype(jnp.int32)
    near = send(tokens, ZNEAR)
    own_w, sibling_w, far_w = pick_qkv(info, qkv_weight)
    far_w = send(far_w, ZFAR)
    cos, sin = tables(info)
    gate_up_parts = pick_gate_up(info, after(gate_up_weight, own_w))
    vec = pack(
        attn_norm_gain, attn_norm_shift, mlp_norm_gain, mlp_norm_shift, after(qkv_bias, cos, gate_up_parts[0])
    )
    near_vec = send(vec, ZNEAR)
    near = after(near, near_vec)
    xs = (tokens, near, send(tokens, SIBLING), send(near, SIBLING))
    vs = (vec, near_vec, send(vec, SIBLING), send(near_vec, SIBLING))
    qkv_ws = (own_w, send(sibling_w, SIBLING), far_w, send(far_w[ROWS:], SIBLING))
    gs = gather_group(after(cotangent, near))
    gate_up_ws = [
        gate_up_parts[0],
        send(after(gate_up_parts[1], near), SIBLING),
        send(after(gate_up_parts[2], far_w, near_vec), ZFAR),
    ]

    hidden, qkv, qkv_w, norms = project(info, xs, vs, qkv_ws, cos, sin)
    gate_up_ws.append(send(after(gate_up_parts[3], gs[1]), ZNEAR_SIBLING))
    mixed0, lse0, *blocks0 = attend(0, info, qkv, out_weight)
    blocks0[3] = after(blocks0[3], *gate_up_ws[1:], gs[1])
    gate_up_ws.append(send(after(gate_up_parts[4], gate_up_ws[2], mixed0), ZFAR_SIBLING))
    own0, near0 = scatter_half(blocks0)
    mixed1, lse1, *blocks1 = attend(1, after(info, near0), qkv, out_weight)
    other0 = send(near0, ZNEAR)
    blocks1[1] = after(blocks1[1], other0)
    own1, near1 = scatter_half(blocks1)
    mixed, lse = (mixed0, mixed1), (lse0, lse1)
    mid0, hid0 = middle_of(0, tokens, own0, other0, norms)
    mid1, hid1 = middle_of(1, tokens, own1, send(near1, ZNEAR), norms)
    mids = (mid0, mid1)
    hs = [gather_group(hid0), gather_group(after(hid1, gate_up_ws[4]))]

    act0, dgu0, *blocks0, out_low0, out_up0, feed_w, down_w = feed_first(
        after(info, hid1), hs[0], gs, gate_up_ws, down_weight
    )
    own0, near0 = scatter_half(blocks0)
    act1, dgu1, *blocks1, out_low1, out_up1 = feed_second(after(info, near0), hs[1], gs, feed_w, down_w)
    other0 = send(near0, ZNEAR)
    blocks1[1] = after(blocks1[1], other0)
    own1, near1 = scatter_half(blocks1)
    grad_mid0, branch_own0, sums_m0 = middle_back(0, own0, other0, mids[0], cotangent, norms, 0)
    mlp_halves = mlp_weights(
        info, (*hs[0], *hs[1]), gs, (dgu0, after(dgu1, near1, branch_own0)), (act0, act1)
    )
    other1 = after(send(near1, ZNEAR), mlp_halves[0])
    grad_mid1, branch_own1, sums_m1 = middle_back(1, own1, other1, mids[1], cotangent, norms, 20)
    branch = (*gather_group(branch_own0), *gather_group(branch_own1))
    out_lows = (out_low0, out_low1)
    out_gots = [send(after(v, mlp_halves[0]), SIBLING) for v in (out_up0, out_up1)]
    o_near = out_near_of(out_lows, out_gots)

    ready = {}
    mlp_sums = scatter_plane(
        info,
        mlp_halves,
        "mlp",
        (lambda: (ready["dqkv0"],), lambda: (ready["dqkv1"], layer_out), lambda: (ready["halves"][0],)),
        (branch[2],),
    )
    o_other = send(after(o_near, branch[5]), ZNEAR)
    dqkv0 = attend_back(0, after(info, o_near), qkv, branch, out_weight, lse, cos, sin)
    ready["dqkv0"] = dqkv0
    mlp_sum0 = next(mlp_sums)
    layer_out = layer_out_of(mids, out_lows, out_gots, after(o_other, mlp_sum0))
    dqkv1 = attend_back(1, after(info, mlp_sum0), qkv, branch, out_weight, lse, cos, sin)
    ready["dqkv1"] = dqkv1
    mlp_sum1 = next(mlp_sums)
    dqkvs = (dqkv0, dqkv1)
    attn_halves = attn_weights(
        after(info, mlp_sum1), hidden, dqkvs, qkv_w, mixed, branch, norms, (sums_m0, sums_m1)
    )
    ready["halves"] = attn_halves
    mlp_piece = next(mlp_sums)
    ga_blocks = hidden_back((after(dqkv0, mlp_piece), dqkv1), qkv_w)
    ga_own, ga_near = scatter_group(ga_blocks)
    mlp_blocks, mlp_kept = share(info, mlp_piece, 2 * FFP, "mlp", (attn_halves[0],))
    mlp_joined = call(
        join_mlp_kernel,
        "join_mlp",
        [SMEM] + [VMEM] * 5,
        shaped(16, 3 * GROUP * FFP),
        (info, *mlp_blocks, mlp_kept),
        limit=16,
    )
    attn_sums = scatter_plane(
        info,
        attn_halves,
        "attn",
        (
            lambda: (mlp_blocks[0], ga_near),
            lambda: ready["got0"],
            lambda: (),
        ),
    )
    sum0 = next(attn_sums)
    mlp_all = gather_plane(mlp_joined, 6 * FFP, "mlp", (lambda: (sum1,), lambda: (attn_piece,)))
    ready["got0"] = next(mlp_all)
    sum1 = next(attn_sums)
    ready["got1"], _ = next(mlp_all)
    attn_piece = next(attn_sums)
    attn_blocks, attn_kept = share(info, attn_piece, 768 + EX, "attn")
    mlp_four = next(mlp_all)
    attn_joined = call(
        join_attn_kernel,
        "join_attn",
        [SMEM] + [VMEM] * 5,
        shaped(16, 4 * D + EX),
        (after(info, mlp_four[0]), *attn_blocks, attn_kept),
        limit=16,
    )
    attn_all = gather_plane(
        attn_joined, 2 * D, "attn", (lambda: (), lambda: (grad_down,))
    )
    next(attn_all)
    _, attn_stacked = next(attn_all)
    ga_other = send(after(ga_near, attn_stacked), ZNEAR)
    tokens_grad = tokens_back(ga_own, ga_other, tokens, (grad_mid0, grad_mid1), norms)

    grad_gate_up, grad_down = call(
        finish_mlp_kernel,
        "finish_mlp",
        [SMEM] + [VMEM] * 4,
        [shaped(ROWS, 2 * FF, dtype=F32), shaped(FFS, D, dtype=F32)],
        (info, *mlp_four),
        limit=30,
        scratch_shapes=[pltpu.VMEM((ROWS, GROUP * FFP), F32)],
    )
    attn_four = next(attn_all)
    grad_qkv, grad_out, *vectors, grad_bias = call(
        finish_attn_kernel,
        "finish_attn",
        [SMEM] + [VMEM] * 4,
        [shaped(ROWS, 3 * D, dtype=F32), shaped(256, D, dtype=F32)]
        + [shaped(256, dtype=F32)] * 4
        + [shaped(768, dtype=F32)],
        (after(info, tokens_grad), *attn_four),
        limit=24,
        scratch_shapes=[pltpu.VMEM((ROWS, D), F32), pltpu.VMEM((ROWS, EX), F32), pltpu.VMEM((EX, ROWS), F32)],
    )
    return (
        layer_out,
        tokens_grad,
        vectors[0],
        vectors[1],
        grad_qkv,
        grad_bias,
        grad_out,
        vectors[2],
        vectors[3],
        grad_gate_up,
        grad_down,
    )


def solution(mesh):
    rows = P(("dp", "fsdp"), None)
    vector = P("fsdp")
    matrix = P("fsdp", None)
    in_specs = (rows, vector, vector, matrix, vector, matrix, vector, vector, matrix, matrix, rows)
    out_specs = (rows, rows, vector, vector, matrix, vector, matrix, vector, vector, matrix, matrix)
    return jax.shard_map(body, mesh=mesh, in_specs=in_specs, out_specs=out_specs, check_vma=False)
```

```python
import functools
import math

import jax
import jax.numpy as jnp
from jax import lax
from jax.experimental import pallas as pl
from jax.experimental.pallas import tpu as pltpu
from jax.sharding import PartitionSpec as P

D = 1024
HEADS = 16
HEAD = 64
ROTARY = 16
FF = 2816
GROUP = 4
ROWS = 256
HALF = 128
FFS = FF // GROUP
FFP = 768
EPS = 1e-05
F32 = jnp.float32
BF16 = jnp.bfloat16
AXES = ("dp", "fsdp")
LOG2E = 1.0 / math.log(2.0)
SCALE2 = HEAD ** (-0.5) * LOG2E


def where_is(lin):
    return [(lin // 16) % 4, (lin // 4) % 4, (lin // 64) * 2 + (lin // 2) % 2, lin % 2]


def linear(x, y, z, core):
    return (((z // 2) * 4 + x) * 4 + y) * 4 + (z % 2) * 2 + core


def perm_of(move):
    return tuple((lin, linear(*move(*where_is(lin)))) for lin in range(128))


def flip(v, which):
    return v ^ 1 if which == 0 else 3 - v


SIBLING = perm_of(lambda x, y, z, c: (x, y, z, 1 - c))
ZNEAR = perm_of(lambda x, y, z, c: (x, y, z ^ 1, c))
ZFAR = perm_of(lambda x, y, z, c: (x, y, 3 - z, c))
ZFAR_SIBLING = perm_of(lambda x, y, z, c: (x, y, 3 - z, 1 - c))
ZNEAR_SIBLING = perm_of(lambda x, y, z, c: (x, y, z ^ 1, 1 - c))
ZREPLICA = perm_of(lambda x, y, z, c: (x, y, (z + 2) % 4, c))
def cube_move(bit):
    def move(x, y, z, c):
        on_x = (bit < 2) == (c == 0)
        return (flip(x, bit % 2), y, z, c) if on_x else (x, flip(y, bit % 2), z, c)

    return perm_of(move)


CUBE = tuple(cube_move(bit) for bit in range(4))
FOUR = (CUBE[3], CUBE[2], tuple((a, CUBE[3][b][1]) for a, b in CUBE[2]))


SPLITS = ((0, 1), (1, 0))
ME, SLOT, BIT = 0, 1, 5


def send(value, perm):
    return lax.ppermute(value, AXES, perm)


def dot(a, b):
    return lax.dot_general(a, b, (((1,), (0,)), ((), ())), preferred_element_type=F32)


def dot_nt(a, b):
    return lax.dot_general(a, b, (((1,), (1,)), ((), ())), preferred_element_type=F32)


def dot_tn(a, b):
    return lax.dot_general(a, b, (((0,), (0,)), ((), ())), preferred_element_type=F32)


def shaped(*shape, dtype=BF16):
    return jax.ShapeDtypeStruct(shape, dtype)


SMEM = pl.BlockSpec(memory_space=pltpu.SMEM)
ANY = pl.BlockSpec(memory_space=pl.ANY)
VMEM = pl.BlockSpec(memory_space=pltpu.VMEM)


def call(kernel, name, in_specs, out_shape, operands, *, us=0, limit=48, **kw):
    return pl.pallas_call(
        kernel,
        in_specs=in_specs,
        out_shape=out_shape,
        compiler_params=pltpu.CompilerParams(vmem_limit_bytes=limit << 20),
        cost_estimate=pl.CostEstimate(flops=us * 10**9, bytes_accessed=us << 20, transcendentals=0),
        name=name,
        **kw,
    )(*operands)


def call_far(kernel, name, out_shape, operands, **kw):
    n = len(operands)
    n_out = len(out_shape) if isinstance(out_shape, list) else 1

    def whole_kernel(*refs):
        ins, outs, held, sems = refs[:n], refs[n : n + n_out], refs[n + n_out : -1], refs[-1]
        copies = [pltpu.make_async_copy(r, h, sems.at[i]) for i, (r, h) in enumerate(zip(ins, held))]
        for copy in copies:
            copy.start()
        for copy in copies:
            copy.wait()
        kernel(*held, *outs)

    return call(
        whole_kernel,
        name,
        [ANY] * n,
        out_shape,
        operands,
        scratch_shapes=[pltpu.VMEM(v.shape, v.dtype) for v in operands] + [pltpu.SemaphoreType.DMA((n,))],
        **kw,
    )


def row_of(slot, rows=ROWS):
    return pl.ds(pl.multiple_of(slot * rows, rows), rows)


def lanes_of(start, width=128):
    return pl.ds(pl.multiple_of(start, 128), width)


def stats_of(x):
    cen = x - jnp.mean(x, axis=1, keepdims=True)
    inv = lax.rsqrt(jnp.mean(cen * cen, axis=1, keepdims=True) + EPS)
    return cen * inv, inv


def partner_of(t, lane):
    return jnp.where(lane % HEAD < ROTARY // 2, pltpu.roll(t, 120, 1), pltpu.roll(t, 8, 1))


def pack_kernel(a_ref, b_ref, c_ref, d_ref, bias_ref, out_ref):
    norms = [ref[...].reshape(1, 256).astype(F32) for ref in (a_ref, b_ref, c_ref, d_ref)]
    bias = [bias_ref[...].reshape(1, 768).astype(F32), jnp.zeros((1, 256), F32)]
    first = jnp.broadcast_to(jnp.concatenate(norms, axis=1), (16, D))
    second = jnp.broadcast_to(jnp.concatenate(bias, axis=1), (16, D))
    row = lax.broadcasted_iota(jnp.int32, (16, D), 0)
    out_ref[...] = jnp.where(row == 0, first, jnp.where(row == 1, second, 0.0)).astype(BF16)


def pack(*vectors):
    return call(pack_kernel, "pack", [VMEM] * 5, shaped(16, D), vectors, limit=16)


def tables_kernel(info, cos_ref, sin_ref):
    at = lax.broadcasted_iota(jnp.int32, (ROWS, 128), 1) % HEAD
    rate = jnp.exp((at % (ROTARY // 2)).astype(F32) * (-math.log(10000.0) / (ROTARY // 2)))
    row = lax.broadcasted_iota(jnp.int32, (ROWS, 128), 0)
    for j in range(GROUP):
        place = row + (info[ME] ^ (0, 2, 1, 3)[j]) * ROWS
        angle = place.astype(F32) * rate
        sin = jnp.where(at < ROTARY // 2, -jnp.sin(angle), jnp.sin(angle))
        rows = slice(ROWS * j, ROWS * j + ROWS)
        cos_ref[rows, :] = jnp.where(at < ROTARY, jnp.cos(angle), 1.0)
        sin_ref[rows, :] = jnp.where(at < ROTARY, sin, 0.0)


def tables(info):
    return call(tables_kernel, "tables", [SMEM], [shaped(D, 128, dtype=F32)] * 2, (info,), limit=16)


def pick_qkv_kernel(info, w_ref, own, sibling, far):
    for j in range(GROUP):
        d = info[ME] ^ j
        for c in range(3):
            cols = w_ref[:, lanes_of(c * D + d * 256, 256)]
            if j < 2:
                (own, sibling)[j][:, 256 * c : 256 * c + 256] = cols
            else:
                far[ROWS * (j - 2) : ROWS * (j - 1), 256 * c : 256 * c + 256] = cols


def pick_qkv(info, w):
    return call(
        pick_qkv_kernel,
        "pick_qkv",
        [SMEM, VMEM],
        [shaped(ROWS, 768), shaped(ROWS, 768), shaped(2 * ROWS, 768)],
        (info, w),
        limit=32,
    )


CUT = 16


def pick_gate_up_kernel(info, w_ref, *refs):
    outs, all_ref = refs[:5], refs[5]
    all_ref[...] = jnp.zeros_like(all_ref)
    for d in range(GROUP):
        all_ref[d, :, :FFS] = w_ref[:, FFS * d : FFS * d + FFS]
        all_ref[d, :, FFP : FFP + FFS] = w_ref[:, FF + FFS * d : FF + FFS * d + FFS]
    for j, out in enumerate(outs[:3]):
        out[...] = all_ref[info[ME] ^ j]
    outs[3][...] = all_ref[info[ME] ^ 3, :CUT, :]
    outs[4][...] = all_ref[info[ME] ^ 3, CUT:, :]


def pick_gate_up(info, w):
    return call(
        pick_gate_up_kernel,
        "pick_gate_up",
        [SMEM, VMEM],
        [shaped(rows, 2 * FFP) for rows in (ROWS, ROWS, ROWS, CUT, ROWS - CUT)],
        (info, w),
        limit=32,
        scratch_shapes=[pltpu.VMEM((GROUP, ROWS, 2 * FFP), BF16)],
    )


def project_kernel(
    info, x0, x1, x2, x3, v0, v1, v2, v3, w0, w1, w2, w3, cos_ref, sin_ref,
    hid_ref, qkv_ref, w_ref, norms_ref, bias_ref, sems,
):
    me = info[ME]
    copies = []
    for j, w in enumerate((w0, w1, w2, w3)):
        copy = pltpu.make_async_copy(w.at[:ROWS], w_ref.at[row_of(me ^ j)], sems.at[j])
        copy.start()
        copies.append(copy)
    for j, v in enumerate((v0, v1, v2, v3)):
        owner = me ^ (0, 2, 1, 3)[j]
        extra = v[...].astype(F32)
        for n in range(4):
            norms_ref[n : n + 1, lanes_of(owner * 256, 256)] = extra[0:1, 256 * n : 256 * n + 256]
        bias_ref[0:1, lanes_of(owner * 768, 768)] = extra[1:2, :768]
    gain, shift = norms_ref[0:1, :], norms_ref[1:2, :]
    bias = jnp.concatenate(
        [bias_ref[0:1, lanes_of(c * D + me * 256, 256)] for c in range(3)], axis=1
    )
    lane = lax.broadcasted_iota(jnp.int32, (ROWS, 128), 1)
    for j, x in enumerate((x0, x1, x2, x3)):
        rows = slice(ROWS * j, ROWS * j + ROWS)
        xhat, _ = stats_of(x[...].astype(F32))
        hid = (xhat * gain + shift).astype(BF16)
        hid_ref[rows, :] = hid
        if j == 0:
            for copy in copies:
                copy.wait()
        proj = dot(hid, w_ref[...]) + bias
        cos, sin = cos_ref[rows, :], sin_ref[rows, :]
        for c in range(4):
            t = proj[:, 128 * c : 128 * c + 128]
            qkv_ref[rows, 128 * c : 128 * c + 128] = (t * cos + partner_of(t, lane) * sin).astype(BF16)
        qkv_ref[rows, 512:] = proj[:, 512:].astype(BF16)


def project(info, xs, vs, ws, cos, sin):
    return call(
        project_kernel,
        "project",
        [SMEM] + [VMEM] * 8 + [ANY] * 4 + [VMEM] * 2,
        [shaped(D, D), shaped(D, 768), shaped(D, 768), shaped(8, D, dtype=F32)],
        (info, *xs, *vs, *ws, cos, sin),
        limit=20,
        scratch_shapes=[pltpu.VMEM((8, 3 * D), F32), pltpu.SemaphoreType.DMA((4,))],
    )


def two_heads(v):
    side = lax.broadcasted_iota(jnp.int32, v.shape, 1) // HEAD
    zero = jnp.zeros((), v.dtype)
    return jnp.concatenate([jnp.where(side == h, v, zero) for h in range(2)], axis=0)


def one_pair(vt):
    n = vt.shape[1] // 2
    return jnp.concatenate([vt[:HEAD, :n], vt[HEAD:, n:]], axis=0).T


def later_keys(keys, queries, first):
    return lax.broadcasted_iota(jnp.int32, (keys, 2 * queries), 0) > (
        lax.broadcasted_iota(jnp.int32, (keys, 2 * queries), 1) % queries + first
    )


def half_rows(slot, half):
    return pl.ds(pl.multiple_of(slot * ROWS + half * HALF, HALF), HALF)


def put_blocks(outs, value):
    for j, out in enumerate(outs):
        out[...] = value[HALF * j : HALF * j + HALF, :]


def attend_kernel(half, info, qkv_ref, w_ref, mixed_ref, lse_ref, *outs):
    own_keys = HALF * (half + 1)
    later = later_keys(own_keys, HALF, HALF * half)
    for pair in range(2):
        cols = [slice(256 * c + 128 * pair, 256 * c + 128 * pair + 128) for c in range(3)]
        for i in range(GROUP):
            slot = info[SLOT + i]
            q = two_heads(qkv_ref[half_rows(slot, half), cols[0]])
            there = [row_of(info[SLOT + n]) for n in range(i)]
            there.append(pl.ds(pl.multiple_of(slot * ROWS, ROWS), own_keys))
            tiles = [dot_nt(qkv_ref[at, cols[1]], q) for at in there]
            tiles[i] = jnp.where(later, -1e30, tiles[i])
            top = functools.reduce(jnp.maximum, [jnp.max(t, axis=0, keepdims=True) for t in tiles])
            top = top * SCALE2
            total = jnp.zeros((1, 2 * HALF), F32)
            out = jnp.zeros((128, 2 * HALF), F32)
            for at, tile in zip(there, tiles):
                p = jnp.exp2(tile * SCALE2 - top)
                total = total + jnp.sum(p, axis=0, keepdims=True)
                out = out + dot_tn(qkv_ref[at, cols[2]], p.astype(BF16))
            to = pl.ds(pl.multiple_of(slot * HALF, HALF), HALF)
            mixed_ref[to, 128 * pair : 128 * pair + 128] = one_pair(out / total).astype(BF16)
            lse = top + jnp.log2(total)
            for h in range(2):
                lse_ref[2 * pair + h : 2 * pair + h + 1, to] = lse[:, HALF * h : HALF * h + HALF]
    put_blocks(outs, dot(mixed_ref[...], w_ref[...]).astype(BF16))


def attend(half, info, qkv, w):
    return call(
        functools.partial(attend_kernel, half),
        "attend",
        [SMEM] + [VMEM] * 2,
        [shaped(4 * HALF, 256), shaped(4, 4 * HALF, dtype=F32)] + [shaped(HALF, D)] * 4,
        (info, qkv, w),
        limit=24,
    )


def attend_back_kernel(
    pair, info, qkv_ref, a0, a1, a2, a3, b0, b1, b2, b3, w_ref, lse0, lse1, cos_ref, sin_ref,
    out_ref, do_ref, dq_ref, dk_ref, dv_ref,
):
    cols = [slice(256 * c + 128 * pair, 256 * c + 128 * pair + 128) for c in range(3)]
    later = later_keys(ROWS, ROWS, 0)
    w = w_ref[128 * pair : 128 * pair + 128, :]
    for j, (a, b) in enumerate(((a0, b0), (a1, b1), (a2, b2), (a3, b3))):
        rows = jnp.concatenate([a[...], b[...]], axis=0)
        do_ref[ROWS * j : ROWS * j + ROWS, :] = dot_nt(rows, w).astype(BF16)
    dk_ref[...] = jnp.zeros_like(dk_ref)
    dv_ref[...] = jnp.zeros_like(dv_ref)
    for i in range(GROUP):
        rows = row_of(info[SLOT + i])
        q = two_heads(qkv_ref[rows, cols[0]])
        do = two_heads(do_ref[rows, :])
        to = pl.ds(pl.multiple_of(info[SLOT + i] * HALF, HALF), HALF)
        lse = jnp.concatenate(
            [ref[2 * pair + h : 2 * pair + h + 1, to] for h in range(2) for ref in (lse0, lse1)], axis=1
        )
        probs, grads = [], []
        delta = jnp.zeros((1, 2 * ROWS), F32)
        for n in range(i + 1):
            there = row_of(info[SLOT + n])
            p = jnp.exp2(dot_nt(qkv_ref[there, cols[1]], q) * SCALE2 - lse)
            if n == i:
                p = jnp.where(later, 0.0, p)
            dp = dot_nt(qkv_ref[there, cols[2]], do)
            delta = delta + jnp.sum(p * dp, axis=0, keepdims=True)
            dv_ref[there, :] += dot(p.astype(BF16), do)
            probs.append(p)
            grads.append(dp)
        dqt = jnp.zeros((128, 2 * ROWS), F32)
        for n in range(i + 1):
            there = row_of(info[SLOT + n])
            ds = (probs[n] * (grads[n] - delta)).astype(BF16)
            dk_ref[there, :] += dot(ds, q)
            dqt = dqt + dot_tn(qkv_ref[there, cols[1]], ds)
        dq_ref[rows, :] = one_pair(dqt)
    lane = lax.broadcasted_iota(jnp.int32, (D, 128), 1)
    scale = HEAD ** (-0.5)
    cos, sin = cos_ref[...], sin_ref[...]
    dq = dq_ref[...] * scale
    out_ref[:, :128] = (dq * cos - partner_of(dq, lane) * sin).astype(BF16)
    dk = dk_ref[...] * scale
    out_ref[:, 128:256] = (dk * cos - partner_of(dk, lane) * sin).astype(BF16)
    out_ref[:, 256:] = dv_ref[...].astype(BF16)


def attend_back(pair, info, qkv, branch, w, lse, cos, sin):
    return call(
        functools.partial(attend_back_kernel, pair),
        "attend_back",
        [SMEM] + [VMEM] * 14,
        shaped(D, 384),
        (info, qkv, *branch, w, *lse, cos, sin),
        us=20 * pair,
        limit=32,
        scratch_shapes=[pltpu.VMEM((D, 128), BF16)] + [pltpu.VMEM((D, 128), F32)] * 3,
    )


def whole(first, second):
    return jnp.concatenate(
        [v[:, 128 * c : 128 * c + 128] for c in range(3) for v in (first, second)], axis=1
    )


def hidden_back_kernel(d0, d1, w_ref, *outs):
    for half in range(2):
        rows = slice(512 * half, 512 * half + 512)
        part = dot_nt(whole(d0[rows, :], d1[rows, :]), w_ref[...]).astype(BF16)
        outs[2 * half][...] = part[:ROWS, :]
        outs[2 * half + 1][...] = part[ROWS:, :]


def hidden_back(dqkvs, w):
    return call(
        hidden_back_kernel,
        "hidden_back",
        [VMEM] * 3,
        [shaped(ROWS, D)] * 4,
        (*dqkvs, w),
        limit=24,
    )


def add_near_kernel(low_ref, got_ref, near_ref):
    near_ref[...] = add(low_ref[...], got_ref[...])


def scatter_group(blocks):
    own, near, sibling, both = blocks
    got_near = send(both, SIBLING)
    got_own = send(sibling, SIBLING)
    near = call(add_near_kernel, "add_near", [VMEM] * 2, shaped(ROWS, D), (near, got_near), limit=16)
    return (own, got_own), near


def scatter_half(blocks):
    own, near, sibling, both = blocks
    got_near = send(both, SIBLING)
    got_own = send(sibling, SIBLING)
    near = call(add_near_kernel, "add_half", [VMEM] * 2, shaped(HALF, D), (near, got_near), limit=16)
    return (own, got_own), near


def gather_group(own, keep=None):
    near = send(own, ZNEAR)
    return (own, near, send(own, SIBLING), send(near, SIBLING))


def total_of(*refs):
    return sum(ref[...].astype(F32) for ref in refs)


def half_total(low_ref, got_ref, other_ref):
    return total_of(low_ref.at[:HALF], got_ref.at[:HALF], other_ref)


def middle_kernel(half, x_ref, own_ref, got_ref, other_ref, norms_ref, mid_ref, hid_ref):
    mid = x_ref[HALF * half : HALF * half + HALF, :].astype(F32) + total_of(own_ref, got_ref, other_ref)
    mid_ref[...] = mid
    xhat, _ = stats_of(mid)
    hid_ref[...] = (xhat * norms_ref[2:3, :] + norms_ref[3:4, :]).astype(BF16)


def middle_of(half, x, own, other, norms):
    return call(
        functools.partial(middle_kernel, half),
        "middle",
        [VMEM] * 5,
        [shaped(HALF, D, dtype=F32), shaped(HALF, D)],
        (x, *own, other, norms),
        limit=16,
    )


def norm_back_of(e, x, gain):
    xhat, inv = stats_of(x)
    u = e * gain
    back = u - jnp.mean(u, axis=1, keepdims=True) - xhat * jnp.mean(u * xhat, axis=1, keepdims=True)
    return inv * back, xhat


def middle_back_kernel(
    half, own_ref, got_ref, other_ref, mid_ref, res_ref, norms_ref, out_ref, branch_ref, sums_ref
):
    e = total_of(own_ref, got_ref, other_ref)
    back, xhat = norm_back_of(e, mid_ref[...], norms_ref[2:3, :])
    out = res_ref[HALF * half : HALF * half + HALF, :].astype(F32) + back
    out_ref[...] = out
    branch_ref[...] = out.astype(BF16)
    sums_ref[0:1, :] = jnp.sum(e * xhat, axis=0, keepdims=True)
    sums_ref[1:2, :] = jnp.sum(e, axis=0, keepdims=True)


def middle_back(half, own, other, mid, res, norms, us):
    return call(
        functools.partial(middle_back_kernel, half),
        "middle_back",
        [VMEM] * 6,
        [shaped(HALF, D, dtype=F32), shaped(HALF, D), shaped(2, D, dtype=F32)],
        (*own, other, mid, res, norms),
        us=us,
        limit=16,
    )


def tokens_back_kernel(own_ref, got_ref, other_ref, x_ref, res0, res1, norms_ref, out_ref):
    e = total_of(own_ref, got_ref, other_ref)
    back, _ = norm_back_of(e, x_ref[...].astype(F32), norms_ref[0:1, :])
    out_ref[:HALF, :] = res0[...] + back[:HALF, :]
    out_ref[HALF:, :] = res1[...] + back[HALF:, :]


def tokens_back(own, other, x, res, norms):
    return call_far(
        tokens_back_kernel,
        "tokens_back",
        shaped(ROWS, D, dtype=F32),
        (*own, other, x, *res, norms),
        us=20,
        limit=16,
    )


def out_near_kernel(l0, g0, l1, g1, near_ref):
    near_ref[:HALF, :] = add(l0[HALF:, :], g0[HALF:, :])
    near_ref[HALF:, :] = add(l1[HALF:, :], g1[HALF:, :])


def out_near_of(lows, gots):
    return call_far(
        out_near_kernel,
        "out_near",
        shaped(ROWS, D),
        (lows[0], gots[0], lows[1], gots[1]),
        limit=16,
    )


def layer_out_kernel(m0, m1, l0, g0, l1, g1, other_ref, out_ref):
    for n, (m, low, got) in enumerate(((m0, l0, g0), (m1, l1, g1))):
        rows = slice(HALF * n, HALF * n + HALF)
        out_ref[rows, :] = (m[...] + half_total(low, got, other_ref.at[rows])).astype(BF16)


def layer_out_of(mids, lows, gots, other):
    return call_far(
        layer_out_kernel,
        "layer_out",
        shaped(ROWS, D),
        (*mids, lows[0], gots[0], lows[1], gots[1], other),
        limit=16,
    )


def feed_kernel(h_ref, g_ref, w_ref, down_ref, act_ref, dgu_ref, ghs, out_low, out_up):
    h, g = h_ref[...], g_ref[...]
    gate = dot(h, w_ref[:, :FFP])
    up = dot(h, w_ref[:, FFP:])
    sig = jax.nn.sigmoid(gate)
    silu = gate * sig
    act = (silu * up).astype(BF16)
    act_ref[...] = act
    grad_act = dot_nt(g, down_ref[...])
    dgate = (grad_act * up * (sig * (1.0 + gate * (1.0 - sig)))).astype(BF16)
    dup = (grad_act * silu).astype(BF16)
    dgu_ref[:, :FFP] = dgate
    dgu_ref[:, FFP:] = dup
    put_blocks(ghs, (dot_nt(dgate, w_ref[:, :FFP]) + dot_nt(dup, w_ref[:, FFP:])).astype(BF16))
    out = dot(act, down_ref[...]).astype(BF16)
    out_low[...] = out[:ROWS, :]
    out_up[...] = out[ROWS:, :]


def tokens_in(half, hs, gs, h_ref, g_ref, sems):
    copies = []
    for j in range(GROUP):
        rows = slice(HALF * j, HALF * j + HALF)
        copies.append(pltpu.make_async_copy(hs[j], h_ref.at[rows], sems.at[j]))
        half_g = gs[j].at[HALF * half : HALF * half + HALF]
        copies.append(pltpu.make_async_copy(half_g, g_ref.at[rows], sems.at[GROUP + j]))
    return copies


def feed_first_kernel(
    info, h0, h1, h2, h3, g0, g1, g2, g3, w0, w1, w2, w3, w4, d_ref,
    act_ref, dgu_ref, gh0, gh1, gh2, gh3, out_low, out_up, w_ref, down_ref, h_ref, g_ref, sems,
):
    copies = tokens_in(0, (h0, h1, h2, h3), (g0, g1, g2, g3), h_ref, g_ref, sems)
    for j, w in enumerate((w0, w1, w2)):
        copies.append(pltpu.make_async_copy(w, w_ref.at[row_of(info[ME] ^ j)], sems.at[8 + j]))
    for j, w in enumerate((w3, w4)):
        at = pl.ds(pl.multiple_of((info[ME] ^ 3) * ROWS + j * CUT, CUT), w.shape[0])
        copies.append(pltpu.make_async_copy(w, w_ref.at[at], sems.at[11 + j]))
    copies.append(pltpu.make_async_copy(d_ref, down_ref.at[:FFS], sems.at[13]))
    for copy in copies:
        copy.start()
    down_ref[FFS:, :] = jnp.zeros((FFP - FFS, D), BF16)
    for copy in copies:
        copy.wait()
    feed_kernel(h_ref, g_ref, w_ref, down_ref, act_ref, dgu_ref, (gh0, gh1, gh2, gh3), out_low, out_up)


def feed_second_kernel(
    info, h0, h1, h2, h3, g0, g1, g2, g3, w_ref, down_ref,
    act_ref, dgu_ref, gh0, gh1, gh2, gh3, out_low, out_up, h_ref, g_ref, sems,
):
    copies = tokens_in(1, (h0, h1, h2, h3), (g0, g1, g2, g3), h_ref, g_ref, sems)
    for copy in copies:
        copy.start()
    for copy in copies:
        copy.wait()
    feed_kernel(h_ref, g_ref, w_ref, down_ref, act_ref, dgu_ref, (gh0, gh1, gh2, gh3), out_low, out_up)


FEED_OUT = (
    [shaped(4 * HALF, FFP), shaped(4 * HALF, 2 * FFP)] + [shaped(HALF, D)] * 4 + [shaped(ROWS, D)] * 2
)
FEED_SCRATCH = [pltpu.VMEM((4 * HALF, D), BF16)] * 2


def feed_first(info, hs, gs, ws, down):
    return call(
        feed_first_kernel,
        "feed_first",
        [SMEM] + [ANY] * 14,
        FEED_OUT + [shaped(D, 2 * FFP), shaped(FFP, D)],
        (info, *hs, *gs, *ws, down),
        limit=28,
        scratch_shapes=FEED_SCRATCH + [pltpu.SemaphoreType.DMA((14,))],
    )


def feed_second(info, hs, gs, w, down):
    return call(
        feed_second_kernel,
        "feed_second",
        [SMEM] + [ANY] * 8 + [VMEM] * 2,
        FEED_OUT,
        (info, *hs, *gs, w, down),
        limit=28,
        scratch_shapes=FEED_SCRATCH + [pltpu.SemaphoreType.DMA((8,))],
    )


def own_order(info, piece):
    return jnp.where(info[ME] % 2 == 0, piece, ((piece & 3) << 2) | (piece >> 2))


def split_result(info, res_ref, outs):
    for part in range(2):
        mine = info[BIT + part]
        weight = 8 >> part
        for t in range(2):
            for n in range(8):
                low = n if part == 0 else (n & 3) | ((n & 4) << 1)
                to = slice(128 * t + 16 * n, 128 * t + 16 * n + 16)
                for out, bit in ((outs[2 * part], mine), (outs[2 * part + 1], 1 - mine)):
                    out[to, :] = res_ref[part, row_of(16 * t + own_order(info, low + weight * bit), 16), :]


def mlp_weights_kernel(
    info, h0, h1, h2, h3, h4, h5, h6, h7, g0, g1, g2, g3, dgu0, dgu1, act0, act1,
    k1, s1, k2, s2, h_ref, g_ref, res_ref, sems,
):
    step = pl.program_id(0)

    def copies(which):
        out = []
        for n in range(2 * GROUP):
            rows = slice(HALF * n, HALF * n + HALF)
            half, j = n // GROUP, n % GROUP
            if which == 0:
                out.append(pltpu.make_async_copy((h0, h1, h2, h3, h4, h5, h6, h7)[n], h_ref.at[rows], sems.at[n]))
            else:
                half_g = (g0, g1, g2, g3)[j].at[HALF * half : HALF * half + HALF]
                out.append(pltpu.make_async_copy(half_g, g_ref.at[rows], sems.at[8 + n]))
        return out

    @pl.when(step == 0)
    def _():
        hs = copies(0)
        for copy in hs + copies(1):
            copy.start()
        for copy in hs:
            copy.wait()

    @pl.when(step == 2)
    def _():
        for copy in copies(1):
            copy.wait()

    def product(left, right0, right1, cols):
        both = dot_tn(left[: 4 * HALF, cols], right0[...]) + dot_tn(left[4 * HALF :, cols], right1[...])
        return both.astype(BF16)

    for part in range(2):
        cols = slice(512 * part, 512 * part + 512)

        @pl.when(step < 2)
        def _():
            res_ref[part] = product(h_ref, dgu0, dgu1, cols)

        @pl.when(step == 2)
        def _():
            res_ref[part] = product(g_ref, act0, act1, cols)

    split_result(info, res_ref, (k1, s1, k2, s2))


def mlp_weights(info, hs, gs, dgus, acts):
    col = lambda i: (0, i)
    dgu = pl.BlockSpec((4 * HALF, FFP), lambda i: (0, jnp.minimum(i, 1)))
    act = pl.BlockSpec((4 * HALF, FFP), lambda i: (0, 0))
    return call(
        mlp_weights_kernel,
        "mlp_weights",
        [SMEM] + [ANY] * 12 + [dgu, dgu, act, act],
        [shaped(256, 3 * FFP)] * 4,
        (info, *hs, *gs, *dgus, *acts),
        limit=26,
        grid=(3,),
        out_specs=[pl.BlockSpec((256, FFP), col)] * 4,
        scratch_shapes=[
            pltpu.VMEM((D, D), BF16),
            pltpu.VMEM((D, D), BF16),
            pltpu.VMEM((2, 512, FFP), BF16),
            pltpu.SemaphoreType.DMA((16,)),
        ],
    )


EX = 128
ATT = 768 + EX + 256


def attn_weights_kernel(
    info, h_ref, d0, d1, w_ref, m0, m1, b0, b1, b2, b3, b4, b5, b6, b7, norms_ref, sm0, sm1,
    k1, s1, k2, s2, d_ref, b_ref, ex_ref, res_ref, sems,
):
    me = info[ME]
    copies = [
        pltpu.make_async_copy(r, b_ref.at[HALF * j : HALF * j + HALF], sems.at[j])
        for j, r in enumerate((b0, b1, b2, b3, b4, b5, b6, b7))
    ]
    for copy in copies:
        copy.start()
    d_ref[...] = whole(d0[...], d1[...])
    ex_ref[...] = jnp.zeros_like(ex_ref)
    ex_ref[0:2, :] = norms_ref[0:2, :]
    ex_ref[2:4, :] = sm0[...] + sm1[...]
    db = dot(jnp.ones((8, D), BF16), d_ref[...])[0:1, :]
    for c in range(3):
        one = db[:, 256 * c : 256 * c + 256]
        ex_ref[pl.ds(8 + 4 * c + me, 1), :] = jnp.concatenate([one] * GROUP, axis=1)
    ex = ex_ref[...].T
    lane = lax.broadcasted_iota(jnp.int32, (512, EX), 1)
    for half in range(2):
        rows = slice(512 * half, 512 * half + 512)
        dw = dot_tn(h_ref[:, rows], d_ref[...])
        res_ref[half, :, :768] = dw.astype(BF16)
        w = w_ref[rows, :].astype(F32)
        gain, shift = ex[rows, 0:1], ex[rows, 1:2]
        sum_e = jnp.sum(w * db, axis=1, keepdims=True)
        sum_xe = (jnp.sum(w * dw, axis=1, keepdims=True) - shift * sum_e) / gain
        cols = jnp.where(lane == 0, sum_xe, jnp.where(lane == 1, sum_e, ex[rows, :]))
        res_ref[half, :, 768 : 768 + EX] = cols.astype(BF16)
    for copy in copies:
        copy.wait()
    m = jnp.concatenate([m0[...], m1[...]], axis=0)
    for half in range(2):
        res_ref[half, :, 768 + EX :] = dot_tn(b_ref[:, 512 * half : 512 * half + 512], m).astype(BF16)
    split_result(info, res_ref, (k1, s1, k2, s2))


def attn_weights(info, hidden, dqkvs, w, mixed, branch, norms, sums_m):
    return call(
        attn_weights_kernel,
        "attn_weights",
        [SMEM] + [VMEM] * 6 + [ANY] * 8 + [VMEM] * 3,
        [shaped(256, ATT)] * 4,
        (info, hidden, *dqkvs, w, *mixed, *branch, norms, *sums_m),
        limit=30,
        scratch_shapes=[
            pltpu.VMEM((D, 768), BF16),
            pltpu.VMEM((D, D), BF16),
            pltpu.VMEM((EX, D), F32),
            pltpu.VMEM((2, 512, ATT), BF16),
            pltpu.SemaphoreType.DMA((8,)),
        ],
    )


def add(a, b):
    return (a.astype(F32) + b.astype(F32)).astype(BF16)


def halve_kernel(info, a1, g1, a2, g2, k1, s1, k2, s2):
    for part, (a, g, keep, away) in enumerate(((a1, g1, k1, s1), (a2, g2, k2, s2))):
        mine = info[BIT + SPLITS[part][1]]
        for t in range(2):
            to = slice(64 * t, 64 * t + 64)
            for out, bit in ((keep, mine), (away, 1 - mine)):
                at = row_of(2 * t + bit, 64)
                out[to, :] = add(a[at, :], g[at, :])


def quarter_kernel(info, a1, g1, a2, g2, *outs):
    mine = info[BIT + 2] * 2 + info[BIT + 3]
    for part, (a, g) in enumerate(((a1, g1), (a2, g2))):
        for t in range(2):
            to = slice(32 * part + 16 * t, 32 * part + 16 * t + 16)
            for flips, out in enumerate(outs):
                at = row_of(4 * t + (mine ^ flips), 16)
                out[to, :] = add(a[at, :], g[at, :])


def piece_kernel(a, g1, g2, g3, out):
    out[...] = total_of(a, g1, g2, g3).astype(BF16)


def share_kernel(cols, info, a_ref, g_ref, o0, o1, o2, o3, kept):
    width = a_ref.shape[1] - cols
    for j, out in enumerate((o0, o1, o2, o3)):
        rows = row_of(info[ME] ^ j, 16)
        out[...] = add(a_ref[rows, :cols], g_ref[rows, :cols])
    for t in range(GROUP):
        rows = slice(16 * t, 16 * t + 16)
        kept[:, width * t : width * t + width] = add(a_ref[rows, cols:], g_ref[rows, cols:])


def scatter_plane(info, first, name, gates, start=()):
    k1, s1, k2, s2 = first
    width = k1.shape[1]
    s1, s2 = after(s1, *start), after(s2, *start)
    for step, (kernel, shapes) in enumerate(
        ((halve_kernel, [shaped(128, width)] * 4), (quarter_kernel, [shaped(64, width)] * 4))
    ):
        got1 = send(s1, CUBE[SPLITS[0][step]])
        got2 = send(s2, CUBE[SPLITS[1][step]])
        outs = call(
            kernel,
            ("halve_", "quarter_")[step] + name,
            [SMEM] + [VMEM] * 4,
            shapes,
            (info, after(k1, *gates[step]()), got1, k2, got2),
            limit=24,
        )
        k1, s1, k2, s2 = outs
        yield k1
    keep, *away = outs
    got = [send(a, p) for a, p in zip(away, FOUR)]
    yield call(
        piece_kernel,
        "piece_" + name,
        [VMEM] * 4,
        shaped(64, width),
        (after(keep, *gates[2]()), *got),
        limit=24,
    )


def share(info, piece, cols, name, gate=()):
    width = piece.shape[1]
    *blocks, kept = call(
        functools.partial(share_kernel, cols),
        "share_" + name,
        [SMEM] + [VMEM] * 2,
        [shaped(16, cols)] * 4 + [shaped(16, GROUP * (width - cols))],
        (info, after(piece, *gate), send(piece, ZREPLICA)),
        us=20,
        limit=16,
    )
    perms = (None, SIBLING, ZNEAR, ZNEAR_SIBLING)
    return [b if p is None else send(b, p) for b, p in zip(blocks, perms)], kept


def join_mlp_kernel(info, r0, r1, r2, r3, kept, out):
    for j, r in enumerate((r0, r1, r2, r3)):
        s = info[ME] ^ j
        out[:, lanes_of(s * FFP, FFP)] = r[:, :FFP]
        out[:, lanes_of((GROUP + s) * FFP, FFP)] = r[:, FFP:]
    out[:, 2 * GROUP * FFP :] = kept[...]


def join_attn_kernel(info, r0, r1, r2, r3, kept, out):
    refs = (r0, r1, r2, r3)
    for j, r in enumerate(refs):
        s = info[ME] ^ j
        for c in range(3):
            out[:, lanes_of(c * D + s * 256, 256)] = r[:, 256 * c : 256 * c + 256]
    out[:, 3 * D : 3 * D + EX] = total_of(*(r.at[:, 768:] for r in refs)).astype(BF16)
    out[:, 3 * D + EX :] = kept[...]


def slots_of(info, piece):
    d = own_order(info, piece) ^ (info[BIT] * 8 + info[BIT + 1] * 4 + info[BIT + 2] * 2 + info[BIT + 3])
    return d, ((d >> 2) & 1) * 8 + ((d >> 3) & 1) * 4 + (d & 3)


def at_slot(own, got, slot):
    rows = row_of(slot & 7, 16)
    return jnp.where(slot >= 8, got[rows, :].astype(F32), own[rows, :].astype(F32))


def finish_mlp_kernel(info, a1, g1, a2, g2, gu_ref, down_ref, turn_ref):
    for piece in range(16):
        to = slice(16 * piece, 16 * piece + 16)
        one, two = slots_of(info, piece)
        v, u = at_slot(a1, g1, one), at_slot(a2, g2, two)
        for s in range(2 * GROUP):
            src, lo = (v, s * FFP) if s < 6 else (u, (s - 6) * FFP)
            gu_ref[to, FFS * s : FFS * s + FFS] = src[:, lo : lo + FFS]
        turn_ref[to, :] = u[:, 2 * FFP :]
    for t in range(GROUP):
        down_ref[:, 256 * t : 256 * t + 256] = turn_ref[:, FFP * t : FFP * t + FFP].T[:FFS, :]


def finish_attn_kernel(
    info, a1, g1, a2, g2, qkv_ref, out_ref, v0, v1, v2, v3, bias_ref, turn_ref, ex_ref, vec_ref
):
    for piece in range(16):
        to = slice(16 * piece, 16 * piece + 16)
        one, two = slots_of(info, piece)
        qkv_ref[to, : 2 * D] = at_slot(a1, g1, one)
        v = at_slot(a2, g2, two)
        qkv_ref[to, 2 * D :] = v[:, :D]
        ex_ref[to, :] = v[:, D : D + EX]
        turn_ref[to, :] = v[:, D + EX :]
    for t in range(GROUP):
        out_ref[:, 256 * t : 256 * t + 256] = turn_ref[:, 256 * t : 256 * t + 256].T
    vec_ref[...] = ex_ref[...].T
    for n, ref in enumerate((v0, v1, v2, v3)):
        ref[...] = vec_ref[n : n + 1, :].reshape(256)
    bias = [vec_ref[pl.ds(8 + 3 * info[ME] + n, 1), :] for n in range(3)]
    bias_ref[...] = jnp.concatenate(bias, axis=1).reshape(768)


def stack_four_kernel(own, g1, g2, g3, one, two):
    cut = one.shape[1]
    for n, ref in enumerate((own, g1, g2, g3)):
        rows = slice(16 * n, 16 * n + 16)
        one[rows, :] = ref[:, :cut]
        two[rows, :] = ref[:, cut:]


def stack_kernel(a1, g1, a2, g2, one, two):
    rows = a1.shape[0]
    for own, got, out in ((a1, g1, one), (a2, g2, two)):
        out[:rows, :] = own[...]
        out[rows:, :] = got[...]


def gather_plane(piece, cut, name, gates):
    width = piece.shape[1]
    got = [send(piece, p) for p in FOUR]
    yield got
    parts = call(
        stack_four_kernel,
        "stack_four_" + name,
        [VMEM] * 4,
        [shaped(64, cut), shaped(64, width - cut)],
        (after(piece, *gates[0]()), *got),
        limit=16,
    )
    for step in (1, 0):
        got = [send(p, CUBE[SPLITS[i][step]]) for i, p in enumerate(parts)]
        four = (parts[0], got[0], parts[1], got[1])
        if step == 0:
            yield four
            return
        yield got, parts[0]
        parts = call(
            stack_kernel,
            "stack_" + name,
            [VMEM] * 4,
            [shaped(2 * p.shape[0], p.shape[1]) for p in parts],
            (after(four[0], *gates[1]()), *four[1:]),
            us=20,
            limit=16,
        )


def after(value, *earlier):
    return lax.optimization_barrier((value, *earlier))[0]


def body(
    tokens,
    attn_norm_gain,
    attn_norm_shift,
    qkv_weight,
    qkv_bias,
    out_weight,
    mlp_norm_gain,
    mlp_norm_shift,
    gate_up_weight,
    down_weight,
    cotangent,
):
    me = lax.axis_index("fsdp")
    rank = lax.axis_index("dp")
    x, y = (rank // 4) % 4, rank % 4
    first = jnp.where(me % 2 == 0, x, y)
    second = jnp.where(me % 2 == 0, y, x)
    info = jnp.stack(
        [me]
        + [2 * ((n ^ me) % 2) + (n ^ me) // 2 for n in range(GROUP)]
        + [((first + 1) // 2) % 2, first // 2, ((second + 1) // 2) % 2, second // 2]
    ).astype(jnp.int32)
    near = send(tokens, ZNEAR)
    own_w, sibling_w, far_w = pick_qkv(info, qkv_weight)
    far_w = send(far_w, ZFAR)
    cos, sin = tables(info)
    gate_up_parts = pick_gate_up(info, after(gate_up_weight, own_w))
    vec = pack(
        attn_norm_gain, attn_norm_shift, mlp_norm_gain, mlp_norm_shift, after(qkv_bias, cos, gate_up_parts[0])
    )
    near_vec = send(vec, ZNEAR)
    sibling_x = send(tokens, SIBLING)
    sibling_w = send(sibling_w, SIBLING)
    near = after(near, near_vec, sibling_x, sibling_w)
    xs = (tokens, near, sibling_x, send(near, SIBLING))
    vs = (vec, near_vec, send(vec, SIBLING), send(near_vec, SIBLING))
    qkv_ws = (own_w, sibling_w, far_w, send(far_w[ROWS:], SIBLING))
    gs = gather_group(after(cotangent, near))
    gate_up_ws = [
        gate_up_parts[0],
        send(after(gate_up_parts[1], near), SIBLING),
        send(after(gate_up_parts[2], far_w, near_vec), ZFAR),
    ]

    hidden, qkv, qkv_w, norms = project(info, xs, vs, qkv_ws, cos, sin)
    gate_up_ws.append(send(after(gate_up_parts[3], near), ZNEAR_SIBLING))
    mixed0, lse0, *blocks0 = attend(0, info, qkv, out_weight)
    blocks0[3] = after(blocks0[3], gate_up_ws[1], gate_up_ws[3])
    own0, near0 = scatter_half(blocks0)
    gate_up_ws.append(send(after(gate_up_parts[4], gate_up_ws[2], near0), ZFAR_SIBLING))
    mixed1, lse1, *blocks1 = attend(1, after(info, near0, gate_up_ws[2], gs[1]), qkv, out_weight)
    other0 = send(near0, ZNEAR)
    blocks1[1] = after(blocks1[1], other0)
    own1, near1 = scatter_half(blocks1)
    mixed, lse = (mixed0, mixed1), (lse0, lse1)
    mid0, hid0 = middle_of(0, tokens, own0, other0, norms)
    mid1, hid1 = middle_of(1, tokens, own1, send(near1, ZNEAR), norms)
    mids = (mid0, mid1)
    hs = [gather_group(hid0), gather_group(after(hid1, gate_up_ws[4]))]

    act0, dgu0, *blocks0, out_low0, out_up0, feed_w, down_w = feed_first(
        after(info, hid1), hs[0], gs, gate_up_ws, down_weight
    )
    own0, near0 = scatter_half(blocks0)
    act1, dgu1, *blocks1, out_low1, out_up1 = feed_second(after(info, near0), hs[1], gs, feed_w, down_w)
    other0 = send(near0, ZNEAR)
    blocks1[1] = after(blocks1[1], other0)
    own1, near1 = scatter_half(blocks1)
    grad_mid0, branch_own0, sums_m0 = middle_back(0, own0, other0, mids[0], cotangent, norms, 0)
    mlp_halves = mlp_weights(
        info, (*hs[0], *hs[1]), gs, (dgu0, after(dgu1, near1, branch_own0)), (act0, act1)
    )
    other1 = after(send(near1, ZNEAR), mlp_halves[0])
    grad_mid1, branch_own1, sums_m1 = middle_back(1, own1, other1, mids[1], cotangent, norms, 20)
    branch = (*gather_group(branch_own0), *gather_group(branch_own1))
    out_lows = (out_low0, out_low1)
    out_gots = [send(after(v, mlp_halves[0]), SIBLING) for v in (out_up0, out_up1)]
    o_near = out_near_of(out_lows, out_gots)

    ready = {}
    mlp_sums = scatter_plane(
        info,
        mlp_halves,
        "mlp",
        (lambda: (ready["dqkv0"],), lambda: (ready["dqkv1"], layer_out), lambda: (ready["halves"][0],)),
        (branch[2],),
    )
    o_other = send(after(o_near, branch[5]), ZNEAR)
    dqkv0 = attend_back(0, after(info, o_near), qkv, branch, out_weight, lse, cos, sin)
    ready["dqkv0"] = dqkv0
    mlp_sum0 = next(mlp_sums)
    layer_out = layer_out_of(mids, out_lows, out_gots, after(o_other, mlp_sum0))
    dqkv1 = attend_back(1, after(info, mlp_sum0), qkv, branch, out_weight, lse, cos, sin)
    ready["dqkv1"] = dqkv1
    mlp_sum1 = next(mlp_sums)
    dqkvs = (dqkv0, dqkv1)
    attn_halves = attn_weights(
        after(info, mlp_sum1), hidden, dqkvs, qkv_w, mixed, branch, norms, (sums_m0, sums_m1)
    )
    ready["halves"] = attn_halves
    mlp_piece = next(mlp_sums)
    ga_blocks = hidden_back((after(dqkv0, mlp_piece), dqkv1), qkv_w)
    ga_own, ga_near = scatter_group(ga_blocks)
    mlp_blocks, mlp_kept = share(info, mlp_piece, 2 * FFP, "mlp", (attn_halves[0],))
    mlp_joined = call(
        join_mlp_kernel,
        "join_mlp",
        [SMEM] + [VMEM] * 5,
        shaped(16, 3 * GROUP * FFP),
        (info, *mlp_blocks, mlp_kept),
        limit=16,
    )
    attn_sums = scatter_plane(
        info,
        attn_halves,
        "attn",
        (
            lambda: (mlp_blocks[0], ga_near),
            lambda: ready["got0"],
            lambda: (),
        ),
    )
    sum0 = next(attn_sums)
    mlp_all = gather_plane(mlp_joined, 6 * FFP, "mlp", (lambda: (sum1,), lambda: (attn_piece,)))
    ready["got0"] = next(mlp_all)
    sum1 = next(attn_sums)
    ready["got1"], _ = next(mlp_all)
    attn_piece = next(attn_sums)
    attn_blocks, attn_kept = share(info, attn_piece, 768 + EX, "attn")
    mlp_four = next(mlp_all)
    attn_joined = call(
        join_attn_kernel,
        "join_attn",
        [SMEM] + [VMEM] * 5,
        shaped(16, 4 * D + EX),
        (after(info, mlp_four[0]), *attn_blocks, attn_kept),
        limit=16,
    )
    attn_all = gather_plane(
        attn_joined, 2 * D, "attn", (lambda: (), lambda: (mlp_four[1], mlp_four[3]))
    )
    next(attn_all)
    _, attn_stacked = next(attn_all)
    ga_other = send(after(ga_near, attn_stacked), ZNEAR)

    grad_gate_up, grad_down = call(
        finish_mlp_kernel,
        "finish_mlp",
        [SMEM] + [VMEM] * 4,
        [shaped(ROWS, 2 * FF, dtype=F32), shaped(FFS, D, dtype=F32)],
        (info, *mlp_four),
        limit=30,
        scratch_shapes=[pltpu.VMEM((ROWS, GROUP * FFP), F32)],
    )
    tokens_grad = tokens_back(ga_own, after(ga_other, grad_down), tokens, (grad_mid0, grad_mid1), norms)
    attn_four = next(attn_all)
    grad_qkv, grad_out, *vectors, grad_bias = call(
        finish_attn_kernel,
        "finish_attn",
        [SMEM] + [VMEM] * 4,
        [shaped(ROWS, 3 * D, dtype=F32), shaped(256, D, dtype=F32)]
        + [shaped(256, dtype=F32)] * 4
        + [shaped(768, dtype=F32)],
        (after(info, tokens_grad), *attn_four),
        limit=24,
        scratch_shapes=[pltpu.VMEM((ROWS, D), F32), pltpu.VMEM((ROWS, EX), F32), pltpu.VMEM((EX, ROWS), F32)],
    )
    return (
        layer_out,
        tokens_grad,
        vectors[0],
        vectors[1],
        grad_qkv,
        grad_bias,
        grad_out,
        vectors[2],
        vectors[3],
        grad_gate_up,
        grad_down,
    )


def solution(mesh):
    rows = P(("dp", "fsdp"), None)
    vector = P("fsdp")
    matrix = P("fsdp", None)
    in_specs = (rows, vector, vector, matrix, vector, matrix, vector, vector, matrix, matrix, rows)
    out_specs = (rows, rows, vector, vector, matrix, vector, matrix, vector, vector, matrix, matrix)
    return jax.shard_map(body, mesh=mesh, in_specs=in_specs, out_specs=out_specs, check_vma=False)
```
